32 devices in a mesh: grp: 4 (over y, core), ctx: 8 (over z, x).
Axes of the slice: x: 2, y: 2, z: 4, core: 2. Of those that a mesh axis runs over, the one named last changes fastest.
Arguments:
- tokens: bfloat16 [18432, 1024], P(('grp', 'ctx')), may hold values from -6 to 6
- block_table: int32 [288], replicated, may hold values from 0 to 287, as said below
- norm1_gain: float32 [1024], replicated, may hold values from 0.25 to 1.75
- w_query: bfloat16 [1024, 2048], P('ctx'), may hold values from -0.1875 to 0.1875
- key_weight: bfloat16 [1024, 1024], P('ctx'), may hold values from -0.1875 to 0.1875
- value_weight: bfloat16 [1024, 1024], P('ctx'), may hold values from -0.1875 to 0.1875
- query_gain: float32 [128], replicated, may hold values from 0.25 to 1.75
- key_norm_gain: float32 [128], replicated, may hold values from 0.25 to 1.75
- w_out: bfloat16 [2048, 1024], P('ctx'), may hold values from -4 to 4
- norm2_gain: float32 [1024], replicated, may hold values from 0.25 to 1.75
- w_gate: bfloat16 [1024, 3072], P('ctx'), may hold values from -0.1875 to 0.1875
- w_up: bfloat16 [1024, 3072], P('ctx'), may hold values from -0.1875 to 0.1875
- w_down: bfloat16 [3072, 1024], P('ctx'), may hold values from -0.109375 to 0.109375
- out_grad: bfloat16 [18432, 1024], P(('grp', 'ctx')), may hold values from -6 to 6
Outputs:
- layer_out: bfloat16 [18432, 1024], P(('grp', 'ctx'))
- token_grad: float32 [18432, 1024], P(('grp', 'ctx'))
- norm1_gain_grad: float32 [1024], replicated
- w_query_grad: float32 [1024, 2048], P('ctx')
- w_key_grad: float32 [1024, 1024], P('ctx')
- w_value_grad: float32 [1024, 1024], P('ctx')
- query_gain_grad: float32 [128], replicated
- key_gain_grad: float32 [128], replicated
- w_out_grad: float32 [2048, 1024], P('ctx')
- norm2_gain_grad: float32 [1024], replicated
- w_gate_grad: float32 [1024, 3072], P('ctx')
- w_up_grad: float32 [1024, 3072], P('ctx')
- w_down_grad: float32 [3072, 1024], P('ctx')
The draws below stay inside these ranges and needn't reach their ends.
Inputs may be any that keep to these rules, and one draw needn't show every extreme that they name: `block_table`: entry s is the natural block of 16 tokens that storage slot s of every group holds; a group's storage rows run slot after slot, and each device of ctx holds 36 consecutive slots. Every block appears once, and the k-th slots of all devices together hold the k-th run of consecutive natural blocks, one block each.
All inputs are finite; a program needn't handle non-finite values.
Results may differ from the reference program's by a relative error of at most 0.023.
Values may be sent and summed in bfloat16 or wider, within the bound.
No kernel may reach another device: no remote copies, remote signals or barrier semaphores. Data moves between devices by JAX's collectives and lax.ppermute only.
A program may use at most 320 MiB of HBM per device.

```python
import math
import jax
import jax.numpy as jnp
from jax import lax

MODEL_WIDTH = 1024
QUERY_HEADS = 16
KEY_VALUE_HEADS = 8
HEAD_SIZE = 128
FF = 3072
PROMPT = 1024
CONT_LEN = 448
BLK = 16
GROUP_TOKENS = 4608
NBLK = 288
NBLK_DEV = 36
TOKENS = 18432
N_GRP = 4


def draw_block_table(key, part):
    key = jax.random.fold_in(key, 7)
    ctx_width = NBLK // NBLK_DEV

    def one_round(number):
        shuffled = jax.random.permutation(jax.random.fold_in(key, number), ctx_width)
        return shuffled.astype(jnp.int32) + number * ctx_width
    dealt = jax.vmap(one_round)(jnp.arange(NBLK_DEV, dtype=jnp.int32))
    return jnp.transpose(dealt).reshape(NBLK)


def levels(own_key, extent, shards, smallest, top_value):
    level = 1.0
    for axis_at, shards_of in shards:
        steps = jax.random.uniform(jax.random.fold_in(jax.random.fold_in(own_key, 6), axis_at), (shards_of,), jnp.float32, smallest / len(shards), top_value / len(shards))
        level = level * jnp.repeat(jnp.exp(steps), extent[axis_at] // shards_of).reshape((-1,) + (1,) * (len(extent) - 1 - axis_at))
    return level


def gaussian(rng, extent, deviation, limit, pieces=(), kind=jnp.bfloat16):
    level = levels(rng, extent, pieces, -0.22, 0.18) if pieces else 1.0
    drawn = jax.random.normal(rng, extent, jnp.float32) * deviation * level
    return jnp.minimum(jnp.maximum(drawn, -limit), limit).astype(kind)


def setup_inputs(seed: int = 0) -> dict:
    streams_of = jax.random.split(jax.random.key(seed), 15)
    tokens = gaussian(streams_of[0], (TOKENS, MODEL_WIDTH), 1.0, 6.0, ((0, 32),))
    block_table = draw_block_table(jax.random.fold_in(streams_of[14], 71), 0)
    norm1_gain = jnp.clip(1.0 + 0.15 * jax.random.normal(streams_of[2], (MODEL_WIDTH,), jnp.float32), 0.25, 1.75)
    w_query = gaussian(streams_of[3], (MODEL_WIDTH, QUERY_HEADS * HEAD_SIZE), MODEL_WIDTH ** -0.5, 0.1875, ((0, 8),))
    key_weight = gaussian(streams_of[4], (MODEL_WIDTH, KEY_VALUE_HEADS * HEAD_SIZE), MODEL_WIDTH ** -0.5, 0.1875, ((0, 8),))
    value_weight = gaussian(streams_of[5], (MODEL_WIDTH, KEY_VALUE_HEADS * HEAD_SIZE), MODEL_WIDTH ** -0.5, 0.1875, ((0, 8),))
    query_gain = jnp.clip(1.0 + 0.15 * jax.random.normal(streams_of[6], (HEAD_SIZE,), jnp.float32), 0.25, 1.75)
    key_norm_gain = jnp.clip(1.0 + 0.15 * jax.random.normal(streams_of[7], (HEAD_SIZE,), jnp.float32), 0.25, 1.75)
    w_out = gaussian(streams_of[8], (QUERY_HEADS * HEAD_SIZE, MODEL_WIDTH), (max(1, QUERY_HEADS * HEAD_SIZE * 2 // (PROMPT + CONT_LEN))) ** -0.5, 4.0, ((0, 8),))
    norm2_gain = jnp.clip(1.0 + 0.15 * jax.random.normal(streams_of[9], (MODEL_WIDTH,), jnp.float32), 0.25, 1.75)
    w_gate = gaussian(streams_of[10], (MODEL_WIDTH, FF), MODEL_WIDTH ** -0.5, 0.1875, ((0, 8),))
    w_up = gaussian(streams_of[11], (MODEL_WIDTH, FF), MODEL_WIDTH ** -0.5, 0.1875, ((0, 8),))
    w_down = gaussian(streams_of[12], (FF, MODEL_WIDTH), FF ** -0.5, 0.109375, ((0, 8),))
    out_grad = gaussian(streams_of[13], (TOKENS, MODEL_WIDTH), 1.0, 6.0, ((0, 32),))
    return dict(tokens=tokens, block_table=block_table, norm1_gain=norm1_gain, w_query=w_query, key_weight=key_weight, value_weight=value_weight, query_gain=query_gain, key_norm_gain=key_norm_gain, w_out=w_out, norm2_gain=norm2_gain, w_gate=w_gate, w_up=w_up, w_down=w_down, out_grad=out_grad)


eps = 1e-06
theta = 1000000.0
key_span = 512
masked_score = -1e+30
highest_precision = lax.Precision.HIGHEST

@jax.custom_vjp
def reduced_precision(v):
    return lax.optimization_barrier(v.astype(jnp.bfloat16)).astype(jnp.float32)

@jax.custom_vjp
def reduced_backward(v):
    return v

def low_keep(v):
    return (reduced_precision(v), None)

def low_pass(kept, grad):
    return (grad,)

def back_keep(v):
    return (v, None)

def back_low(kept, grad):
    return (reduced_precision(grad),)
reduced_precision.defvjp(low_keep, low_pass)
reduced_backward.defvjp(back_keep, back_low)

def normed(value_rows):
    return value_rows * lax.rsqrt(lax.optimization_barrier(jnp.mean(value_rows * value_rows, axis=-1, keepdims=True)) + eps)

def layout(block_table):
    slot_ids = jnp.arange(GROUP_TOKENS, dtype=jnp.int32)
    natural = block_table[slot_ids // BLK] * BLK + slot_ids % BLK
    beyond = natural - PROMPT
    segment = jnp.where(natural < PROMPT, 0, 1 + beyond // CONT_LEN).astype(jnp.int32)
    places = jnp.where(natural < PROMPT, natural, PROMPT + beyond % CONT_LEN)
    return (natural, segment, places)

def rotation(places):
    half_dim = HEAD_SIZE // 2
    frequency = jnp.exp(jnp.arange(half_dim, dtype=jnp.float32) * (-2.0 * math.log(theta) / HEAD_SIZE))
    angles = places.astype(jnp.float32)[:, None] * frequency[None, :]
    return (jnp.cos(angles), jnp.sin(angles))

def apply_rotation(value_rows, cosine_table, sine_table):
    half_dim = value_rows.shape[-1] // 2
    first_half = value_rows[..., :half_dim]
    second_half = value_rows[..., half_dim:]
    return jnp.concatenate([first_half * cosine_table - second_half * sine_table, second_half * cosine_table + first_half * sine_table], axis=-1)

def attention(query_rows, key_rows, value_rows, natural, segment):
    sharing_count = QUERY_HEADS // KEY_VALUE_HEADS
    block_rows = key_span if GROUP_TOKENS % key_span == 0 else GROUP_TOKENS
    block_count = GROUP_TOKENS // block_rows
    grouped_queries = query_rows.reshape(N_GRP, GROUP_TOKENS, KEY_VALUE_HEADS, sharing_count, HEAD_SIZE)
    grouped_keys = key_rows.reshape(N_GRP, GROUP_TOKENS, KEY_VALUE_HEADS, HEAD_SIZE)
    grouped_values = value_rows.reshape(N_GRP, GROUP_TOKENS, KEY_VALUE_HEADS, HEAD_SIZE)
    softmax_scale = 1.0 / math.sqrt(HEAD_SIZE)

    def query_block(number):
        group_id = number // block_count
        row_first = number % block_count * block_rows
        query_part = lax.dynamic_index_in_dim(grouped_queries, group_id, 0, keepdims=False)
        query_part = lax.dynamic_slice_in_dim(query_part, row_first, block_rows, 0)
        keys_part = lax.dynamic_index_in_dim(grouped_keys, group_id, 0, keepdims=False)
        values_part = lax.dynamic_index_in_dim(grouped_values, group_id, 0, keepdims=False)
        nat_query = lax.dynamic_slice_in_dim(natural, row_first, block_rows)
        seg_query = lax.dynamic_slice_in_dim(segment, row_first, block_rows)
        raw_scores = jnp.einsum('tgrd,ngd->grtn', query_part, keys_part, precision=highest_precision) * softmax_scale
        scores = reduced_backward(raw_scores)
        allowed = (natural[None, :] <= nat_query[:, None]) & ((segment[None, :] == 0) | (segment[None, :] == seg_query[:, None]))
        scores = jnp.where(allowed, scores, masked_score)
        row_max = lax.optimization_barrier(jnp.max(scores, axis=-1, keepdims=True))
        weights = jnp.exp(scores - row_max)
        row_sum = lax.optimization_barrier(jnp.sum(weights, axis=-1, keepdims=True))
        mixed = jnp.einsum('grtn,ngd->grtd', reduced_precision(weights), values_part, precision=highest_precision) / row_sum
        return jnp.transpose(mixed, (2, 0, 1, 3))
    outcome = lax.map(jax.checkpoint(query_block), jnp.arange(N_GRP * block_count, dtype=jnp.int32))
    return outcome.reshape(N_GRP * GROUP_TOKENS, QUERY_HEADS, HEAD_SIZE)

def layer_forward(inputs, gain_one, query_w, key_matrix, value_matrix, query_g, key_g, out_w, gain_two, gate_w, up_w, down_w, cosine_table, sine_table, natural, segment):
    token_total = inputs.shape[0]
    first_hidden = reduced_precision(normed(inputs) * gain_one)
    query_raw = reduced_backward(jnp.dot(first_hidden, query_w, precision=highest_precision, preferred_element_type=jnp.float32)).reshape(token_total, QUERY_HEADS, HEAD_SIZE)
    unnormalized_keys = reduced_backward(jnp.dot(first_hidden, key_matrix, precision=highest_precision, preferred_element_type=jnp.float32)).reshape(token_total, KEY_VALUE_HEADS, HEAD_SIZE)
    reduced_value = reduced_precision(reduced_backward(jnp.dot(first_hidden, value_matrix, precision=highest_precision, preferred_element_type=jnp.float32))).reshape(token_total, KEY_VALUE_HEADS, HEAD_SIZE)
    reduced_query = reduced_precision(apply_rotation(normed(query_raw) * query_g, cosine_table, sine_table))
    key_low = reduced_precision(apply_rotation(normed(unnormalized_keys) * key_g, cosine_table, sine_table))
    attended = attention(reduced_query, key_low, reduced_value, natural, segment)
    flat_low = reduced_precision(reduced_backward(attended)).reshape(token_total, QUERY_HEADS * HEAD_SIZE)
    resid_one = inputs + reduced_backward(jnp.dot(flat_low, out_w, precision=highest_precision, preferred_element_type=jnp.float32))
    hidden_two = reduced_precision(normed(resid_one) * gain_two)
    gate_proj = reduced_backward(jnp.dot(hidden_two, gate_w, precision=highest_precision, preferred_element_type=jnp.float32))
    up_proj = reduced_backward(jnp.dot(hidden_two, up_w, precision=highest_precision, preferred_element_type=jnp.float32))
    hidden_low = reduced_precision(jax.nn.silu(gate_proj) * up_proj)
    return resid_one + jnp.dot(hidden_low, down_w, precision=highest_precision, preferred_element_type=jnp.float32)

def reference(tokens, block_table, norm1_gain, w_query, key_weight, value_weight, query_gain, key_norm_gain, w_out, norm2_gain, w_gate, w_up, w_down, out_grad):
    natural, segment, places = layout(block_table)
    cosine_table, sine_table = rotation(places)
    cosine_table = jnp.tile(cosine_table, (N_GRP, 1))[:, None, :]
    sine_table = jnp.tile(sine_table, (N_GRP, 1))[:, None, :]

    def forward(inputs, gain_one, query_w, key_matrix, value_matrix, query_g, key_g, out_w, gain_two, gate_w, up_w, down_w):
        return layer_forward(inputs, gain_one, query_w, key_matrix, value_matrix, query_g, key_g, out_w, gain_two, gate_w, up_w, down_w, cosine_table, sine_table, natural, segment)
    outcome, pullback = jax.vjp(forward, tokens.astype(jnp.float32), norm1_gain.astype(jnp.float32), w_query.astype(jnp.float32), key_weight.astype(jnp.float32), value_weight.astype(jnp.float32), query_gain.astype(jnp.float32), key_norm_gain.astype(jnp.float32), w_out.astype(jnp.float32), norm2_gain.astype(jnp.float32), w_gate.astype(jnp.float32), w_up.astype(jnp.float32), w_down.astype(jnp.float32))
    grad_tokens, grad_norm1, grad_query_w, grad_key_w, grad_value_w, grad_qgain, grad_kgain, grad_out_w, grad_norm2, grad_gate_w, grad_up_w, grad_down_w = pullback(out_grad.astype(jnp.float32))
    return (outcome.astype(jnp.bfloat16), grad_tokens, grad_norm1, grad_query_w, grad_key_w, grad_value_w, grad_qgain, grad_kgain, grad_out_w, grad_norm2, grad_gate_w, grad_up_w, grad_down_w)
```

```python
import functools
import math

import jax
import jax.numpy as jnp
from jax import lax
from jax.experimental import pallas as pl
from jax.experimental.pallas import tpu as pltpu
from jax.sharding import PartitionSpec as P

QUERY_HEADS = 16
KEY_VALUE_HEADS = 8
HEAD_SIZE = 128
PROMPT = 1024
CONT_LEN = 448
BLK = 16


eps = 1e-06
theta = 1000000.0
key_span = 512
masked_score = -1e30


def normed_parts(value_rows):
    inverse = lax.rsqrt(jnp.mean(value_rows * value_rows, axis=-1, keepdims=True) + eps)
    return (value_rows * inverse, inverse)


def norm_back(grad_normed, normed, inverse):
    return inverse * (grad_normed - normed * jnp.mean(grad_normed * normed, axis=-1, keepdims=True))


def layout(block_table, slot_ids):
    natural = block_table[slot_ids // BLK] * BLK + slot_ids % BLK
    beyond = natural - PROMPT
    segment = jnp.where(natural < PROMPT, 0, 1 + beyond // CONT_LEN)
    places = jnp.where(natural < PROMPT, natural, PROMPT + beyond % CONT_LEN)
    return (natural, segment, places)


def rotation(places):
    half_dim = HEAD_SIZE // 2
    frequency = jnp.exp(
        jnp.arange(half_dim, dtype=jnp.float32) * (-2.0 * math.log(theta) / HEAD_SIZE)
    )
    angles = places.astype(jnp.float32)[:, None] * frequency[None, :]
    return (jnp.cos(angles)[:, None, :], jnp.sin(angles)[:, None, :])


def apply_rotation(value_rows, cosine_table, sine_table):
    half_dim = value_rows.shape[-1] // 2
    first_half = value_rows[..., :half_dim]
    second_half = value_rows[..., half_dim:]
    return jnp.concatenate(
        [
            first_half * cosine_table - second_half * sine_table,
            second_half * cosine_table + first_half * sine_table,
        ],
        axis=-1,
    )


def rotate_back(value_rows, cosine_table, sine_table):
    half_dim = value_rows.shape[-1] // 2
    first_half = value_rows[..., :half_dim]
    second_half = value_rows[..., half_dim:]
    return jnp.concatenate(
        [
            first_half * cosine_table + second_half * sine_table,
            second_half * cosine_table - first_half * sine_table,
        ],
        axis=-1,
    )


def allowed_mask(own_nat, own_seg, key_nat, key_seg):
    return (key_nat[None, :] <= own_nat[:, None]) & (
        (key_seg[None, :] == 0) | (key_seg[None, :] == own_seg[:, None])
    )


def span_of():
    return key_span


def over_blocks(advance, running, length):
    block_span_width = span_of()

    def scan_step(inner_state, key_first):
        return (advance(inner_state, key_first, block_span_width), None)

    running, ignored = lax.scan(
        scan_step,
        running,
        jnp.arange(length // block_span_width, dtype=jnp.int32) * block_span_width,
    )
    return running


def attend_block(running, query_head_rows, keys_part, values_part, allowed, softmax_scale):
    row_max, row_sum, accum = running
    raw_scores = (
        jnp.einsum("grtd,ngd->grtn", query_head_rows, keys_part, preferred_element_type=jnp.float32)
        * softmax_scale
    )
    scores = jnp.where(allowed, raw_scores, masked_score)
    new_max = jnp.maximum(row_max, jnp.max(scores, axis=-1))
    rescale = jnp.exp(row_max - new_max)
    weights = jnp.exp(scores - new_max[..., None])
    row_sum = row_sum * rescale + jnp.sum(weights, axis=-1)
    accum = accum * rescale[..., None] + jnp.einsum(
        "grtn,ngd->grtd",
        weights.astype(jnp.bfloat16),
        values_part,
        preferred_element_type=jnp.float32,
    )
    return (new_max, row_sum, accum)


def key_terms(
    grad_scores, weights, query_head_rows, scaled_high, scaled_rest, softmax_scale, block_span_width
):
    grad_keys = (
        jnp.einsum(
            "grtn,grtd->ngd", grad_scores, query_head_rows, preferred_element_type=jnp.float32
        )
        * softmax_scale
    )
    weights_low = weights.astype(jnp.bfloat16)
    grad_values = jnp.einsum(
        "grtn,grtd->ngd", weights_low, scaled_high, preferred_element_type=jnp.float32
    )
    grad_values = grad_values + jnp.einsum(
        "grtn,grtd->ngd", weights_low, scaled_rest, preferred_element_type=jnp.float32
    )
    return jnp.stack(
        [grad_keys.reshape(block_span_width, -1), grad_values.reshape(block_span_width, -1)], axis=1
    )


def shards(
    tokens,
    block_table,
    norm1_gain,
    w_query,
    key_weight,
    value_weight,
    query_gain,
    key_norm_gain,
    w_out,
    norm2_gain,
    w_gate,
    w_up,
    w_down,
    out_grad,
):
    row_total = tokens.shape[0]
    group_length = block_table.shape[0] * BLK
    sharing_count = QUERY_HEADS // KEY_VALUE_HEADS
    softmax_scale = 1.0 / math.sqrt(HEAD_SIZE)
    position = lax.axis_index("ctx")
    all_nat, all_seg, all_places = layout(block_table, jnp.arange(group_length, dtype=jnp.int32))
    own_slots = position * row_total + jnp.arange(row_total, dtype=jnp.int32)
    own_nat, own_seg, own_places = layout(block_table, own_slots)
    cosine_table, sine_table = rotation(own_places)
    query_full, key_full, value_full, out_full = (
        lax.all_gather(w_query, "ctx", axis=0, tiled=True),
        lax.all_gather(key_weight, "ctx", axis=0, tiled=True),
        lax.all_gather(value_weight, "ctx", axis=0, tiled=True),
        lax.all_gather(w_out, "ctx", axis=0, tiled=True),
    )
    inputs = tokens.astype(jnp.float32)
    normed_one, inverse_one = normed_parts(inputs)
    first_hidden = (normed_one * norm1_gain).astype(jnp.bfloat16)
    query_raw = jnp.dot(first_hidden, query_full, preferred_element_type=jnp.float32).reshape(
        row_total, QUERY_HEADS, HEAD_SIZE
    )
    unnormalized_keys = jnp.dot(first_hidden, key_full, preferred_element_type=jnp.float32).reshape(
        row_total, KEY_VALUE_HEADS, HEAD_SIZE
    )
    reduced_value = jnp.dot(first_hidden, value_full, preferred_element_type=jnp.float32).astype(
        jnp.bfloat16
    )
    query_normed, query_inverse = normed_parts(query_raw)
    normalized_keys, key_inverse = normed_parts(unnormalized_keys)
    reduced_query = apply_rotation(query_normed * query_gain, cosine_table, sine_table).astype(
        jnp.bfloat16
    )
    key_low = (
        apply_rotation(normalized_keys * key_norm_gain, cosine_table, sine_table)
        .astype(jnp.bfloat16)
        .reshape(row_total, KEY_VALUE_HEADS * HEAD_SIZE)
    )
    query_head_rows = jnp.transpose(
        reduced_query.reshape(row_total, KEY_VALUE_HEADS, sharing_count, HEAD_SIZE), (1, 2, 0, 3)
    )

    def attend(running, pieces):
        piece_keys, piece_values = pieces

        def advance(inner_state, key_first, block_span_width):
            keys_part = lax.dynamic_slice_in_dim(
                piece_keys, key_first, block_span_width, 0
            ).reshape(block_span_width, KEY_VALUE_HEADS, HEAD_SIZE)
            values_part = lax.dynamic_slice_in_dim(
                piece_values, key_first, block_span_width, 0
            ).reshape(block_span_width, KEY_VALUE_HEADS, HEAD_SIZE)
            key_nat = lax.dynamic_slice_in_dim(all_nat, key_first, block_span_width)
            key_seg = lax.dynamic_slice_in_dim(all_seg, key_first, block_span_width)
            allowed = allowed_mask(own_nat, own_seg, key_nat, key_seg)
            return attend_block(
                inner_state, query_head_rows, keys_part, values_part, allowed, softmax_scale
            )

        return over_blocks(advance, running, piece_keys.shape[0])

    statistic_shape = (KEY_VALUE_HEADS, sharing_count, row_total)
    initial = (
        jnp.full(statistic_shape, masked_score, jnp.float32),
        jnp.zeros(statistic_shape, jnp.float32),
        jnp.zeros(statistic_shape + (HEAD_SIZE,), jnp.float32),
    )
    row_max, row_sum, accum = attend(
        initial,
        (
            lax.all_gather(key_low, "ctx", axis=0, tiled=True),
            lax.all_gather(reduced_value, "ctx", axis=0, tiled=True),
        ),
    )
    mixed_heads = accum / row_sum[..., None]
    flat_low = (
        jnp.transpose(mixed_heads, (2, 0, 1, 3))
        .reshape(row_total, QUERY_HEADS * HEAD_SIZE)
        .astype(jnp.bfloat16)
    )
    resid_one = inputs + jnp.dot(flat_low, out_full, preferred_element_type=jnp.float32)
    gate_full, up_full, down_full = (
        lax.all_gather(w_gate, "ctx", axis=0, tiled=True),
        lax.all_gather(w_up, "ctx", axis=0, tiled=True),
        lax.all_gather(w_down, "ctx", axis=0, tiled=True),
    )
    normed_two, inverse_two = normed_parts(resid_one)
    hidden_two = (normed_two * norm2_gain).astype(jnp.bfloat16)
    gate_proj = jnp.dot(hidden_two, gate_full, preferred_element_type=jnp.float32)
    up_proj = jnp.dot(hidden_two, up_full, preferred_element_type=jnp.float32)
    gate_sigmoid = jax.nn.sigmoid(gate_proj)
    gate_silu = gate_proj * gate_sigmoid
    hidden_low = (gate_silu * up_proj).astype(jnp.bfloat16)
    outcome = resid_one + jnp.dot(hidden_low, down_full, preferred_element_type=jnp.float32)
    gate_full, up_full, down_full = (
        lax.all_gather(w_gate, "ctx", axis=0, tiled=True),
        lax.all_gather(w_up, "ctx", axis=0, tiled=True),
        lax.all_gather(w_down, "ctx", axis=0, tiled=True),
    )
    grad_out = out_grad.astype(jnp.float32)
    grad_down = jnp.einsum("tf,td->fd", hidden_low, out_grad, preferred_element_type=jnp.float32)
    grad_hidden = jnp.einsum("td,fd->tf", out_grad, down_full, preferred_element_type=jnp.float32)
    grad_gate = (
        grad_hidden * up_proj * gate_sigmoid * (1.0 + gate_proj * (1.0 - gate_sigmoid))
    ).astype(jnp.bfloat16)
    grad_up = (grad_hidden * gate_silu).astype(jnp.bfloat16)
    grad_wgate = jnp.einsum("tk,tf->kf", hidden_two, grad_gate, preferred_element_type=jnp.float32)
    grad_wup = jnp.einsum("tk,tf->kf", hidden_two, grad_up, preferred_element_type=jnp.float32)
    grad_two = jnp.einsum(
        "tf,kf->tk", grad_gate, gate_full, preferred_element_type=jnp.float32
    ) + jnp.einsum("tf,kf->tk", grad_up, up_full, preferred_element_type=jnp.float32)
    gain_two_part = jnp.sum(grad_two * normed_two, axis=0)
    grad_resid = grad_out + norm_back(grad_two * norm2_gain, normed_two, inverse_two)
    grad_attn = grad_resid.astype(jnp.bfloat16)
    query_full, key_full, value_full, out_full = (
        lax.all_gather(w_query, "ctx", axis=0, tiled=True),
        lax.all_gather(key_weight, "ctx", axis=0, tiled=True),
        lax.all_gather(value_weight, "ctx", axis=0, tiled=True),
        lax.all_gather(w_out, "ctx", axis=0, tiled=True),
    )
    keys_all, values_all = (
        lax.all_gather(key_low, "ctx", axis=0, tiled=True),
        lax.all_gather(reduced_value, "ctx", axis=0, tiled=True),
    )
    grad_wout = jnp.einsum("tk,td->kd", flat_low, grad_attn, preferred_element_type=jnp.float32)
    flattened_grad = jnp.einsum(
        "td,kd->tk", grad_attn, out_full, preferred_element_type=jnp.float32
    ).astype(jnp.bfloat16)
    head_grads = jnp.transpose(
        flattened_grad.reshape(row_total, KEY_VALUE_HEADS, sharing_count, HEAD_SIZE), (1, 2, 0, 3)
    )
    grad_heads_wide = head_grads.astype(jnp.float32)
    row_delta = jnp.sum(grad_heads_wide * mixed_heads, axis=-1)
    scaled_grad = grad_heads_wide / row_sum[..., None]
    scaled_high = scaled_grad.astype(jnp.bfloat16)
    scaled_rest = (scaled_grad - scaled_high.astype(jnp.float32)).astype(jnp.bfloat16)

    def block_back(key_first, block_span_width):
        keys_part = lax.dynamic_slice_in_dim(keys_all, key_first, block_span_width, 0).reshape(
            block_span_width, KEY_VALUE_HEADS, HEAD_SIZE
        )
        values_part = lax.dynamic_slice_in_dim(values_all, key_first, block_span_width, 0).reshape(
            block_span_width, KEY_VALUE_HEADS, HEAD_SIZE
        )
        key_nat = lax.dynamic_slice_in_dim(all_nat, key_first, block_span_width)
        key_seg = lax.dynamic_slice_in_dim(all_seg, key_first, block_span_width)
        allowed = allowed_mask(own_nat, own_seg, key_nat, key_seg)
        raw_scores = (
            jnp.einsum(
                "grtd,ngd->grtn", query_head_rows, keys_part, preferred_element_type=jnp.float32
            )
            * softmax_scale
        )
        scores = jnp.where(allowed, raw_scores, masked_score)
        weights = jnp.exp(scores - row_max[..., None])
        grad_prob = jnp.einsum(
            "grtd,ngd->grtn", head_grads, values_part, preferred_element_type=jnp.float32
        )
        grad_scores = (weights * (grad_prob - row_delta[..., None]) / row_sum[..., None]).astype(
            jnp.bfloat16
        )
        return (keys_part, grad_scores, weights)

    empty_query = jnp.zeros((KEY_VALUE_HEADS, sharing_count, row_total, HEAD_SIZE), jnp.float32)
    span_back = span_of()

    def pass_step(grad_query, key_first):
        keys_part, grad_scores, weights = block_back(key_first, span_back)
        grad_query = grad_query + jnp.einsum(
            "grtn,ngd->grtd", grad_scores, keys_part, preferred_element_type=jnp.float32
        )
        return (
            grad_query,
            key_terms(
                grad_scores,
                weights,
                query_head_rows,
                scaled_high,
                scaled_rest,
                softmax_scale,
                span_back,
            ),
        )

    grad_query, key_gradient_parts = lax.scan(
        pass_step, empty_query, jnp.arange(group_length // span_back, dtype=jnp.int32) * span_back
    )
    self_terms = lax.psum_scatter(
        key_gradient_parts.reshape(group_length, 2, KEY_VALUE_HEADS * HEAD_SIZE).astype(
            jnp.bfloat16
        ),
        "ctx",
        scatter_dimension=0,
        tiled=True,
    ).astype(jnp.float32)
    grad_query_rows = jnp.transpose(grad_query * softmax_scale, (2, 0, 1, 3)).reshape(
        row_total, QUERY_HEADS, HEAD_SIZE
    )
    grad_query_normed = rotate_back(grad_query_rows, cosine_table, sine_table)
    gain_query_part = jnp.sum(grad_query_normed * query_normed, axis=(0, 1))
    grad_query_raw = (
        norm_back(grad_query_normed * query_gain, query_normed, query_inverse)
        .reshape(row_total, QUERY_HEADS * HEAD_SIZE)
        .astype(jnp.bfloat16)
    )
    key_row_grads = self_terms[:, 0, :].reshape(row_total, KEY_VALUE_HEADS, HEAD_SIZE)
    grad_key_normed = rotate_back(key_row_grads, cosine_table, sine_table)
    gain_key_part = jnp.sum(grad_key_normed * normalized_keys, axis=(0, 1))
    grad_key_raw = (
        norm_back(grad_key_normed * key_norm_gain, normalized_keys, key_inverse)
        .reshape(row_total, KEY_VALUE_HEADS * HEAD_SIZE)
        .astype(jnp.bfloat16)
    )
    grad_value_low = self_terms[:, 1, :].astype(jnp.bfloat16)
    grad_wquery = jnp.einsum(
        "tk,tq->kq", first_hidden, grad_query_raw, preferred_element_type=jnp.float32
    )
    grad_wkey = jnp.einsum(
        "tk,tq->kq", first_hidden, grad_key_raw, preferred_element_type=jnp.float32
    )
    grad_wvalue = jnp.einsum(
        "tk,tq->kq", first_hidden, grad_value_low, preferred_element_type=jnp.float32
    )
    grad_one = jnp.einsum(
        "tq,kq->tk", grad_query_raw, query_full, preferred_element_type=jnp.float32
    )
    grad_one = grad_one + jnp.einsum(
        "tq,kq->tk", grad_key_raw, key_full, preferred_element_type=jnp.float32
    )
    grad_one = grad_one + jnp.einsum(
        "tq,kq->tk", grad_value_low, value_full, preferred_element_type=jnp.float32
    )
    gain_one_part = jnp.sum(grad_one * normed_one, axis=0)
    grad_tokens = grad_resid + norm_back(grad_one * norm1_gain, normed_one, inverse_one)
    shard_grads = (
        lax.psum_scatter(
            grad_wquery.astype(jnp.bfloat16), "ctx", scatter_dimension=0, tiled=True
        ).astype(jnp.float32),
        lax.psum_scatter(
            grad_wkey.astype(jnp.bfloat16), "ctx", scatter_dimension=0, tiled=True
        ).astype(jnp.float32),
        lax.psum_scatter(
            grad_wvalue.astype(jnp.bfloat16), "ctx", scatter_dimension=0, tiled=True
        ).astype(jnp.float32),
        lax.psum_scatter(
            grad_wout.astype(jnp.bfloat16), "ctx", scatter_dimension=0, tiled=True
        ).astype(jnp.float32),
        lax.psum_scatter(
            grad_wgate.astype(jnp.bfloat16), "ctx", scatter_dimension=0, tiled=True
        ).astype(jnp.float32),
        lax.psum_scatter(
            grad_wup.astype(jnp.bfloat16), "ctx", scatter_dimension=0, tiled=True
        ).astype(jnp.float32),
        lax.psum_scatter(
            grad_down.astype(jnp.bfloat16), "ctx", scatter_dimension=0, tiled=True
        ).astype(jnp.float32),
    )
    shard_grads = (
        lax.psum(shard_grads[0].astype(jnp.bfloat16), "grp").astype(jnp.float32),
        lax.psum(shard_grads[1].astype(jnp.bfloat16), "grp").astype(jnp.float32),
        lax.psum(shard_grads[2].astype(jnp.bfloat16), "grp").astype(jnp.float32),
        lax.psum(shard_grads[3].astype(jnp.bfloat16), "grp").astype(jnp.float32),
        lax.psum(shard_grads[4].astype(jnp.bfloat16), "grp").astype(jnp.float32),
        lax.psum(shard_grads[5].astype(jnp.bfloat16), "grp").astype(jnp.float32),
        lax.psum(shard_grads[6].astype(jnp.bfloat16), "grp").astype(jnp.float32),
    )
    gain_grads = lax.psum(
        (gain_one_part, gain_query_part, gain_key_part, gain_two_part), ("grp", "ctx")
    )
    return (
        outcome.astype(jnp.bfloat16),
        grad_tokens,
        gain_grads[0],
        shard_grads[0],
        shard_grads[1],
        shard_grads[2],
        gain_grads[1],
        gain_grads[2],
        shard_grads[3],
        gain_grads[3],
        shard_grads[4],
        shard_grads[5],
        shard_grads[6],
    )


f32 = jnp.float32
bf16 = jnp.bfloat16
AXES = ("grp", "ctx")
N_GRP = 4
N_CTX = 8
SCALE = 1.0 / math.sqrt(HEAD_SIZE)
EXP2_SCALE = math.log2(math.e) / math.sqrt(HEAD_SIZE)
VMEM_LIMIT = 60 * 1024 * 1024


def nt(a, b):
    return lax.dot_general(a, b, (((1,), (1,)), ((), ())), preferred_element_type=f32)


def nn(a, b):
    return jnp.dot(a, b, preferred_element_type=f32)


def tn(a, b):
    return lax.dot_general(a, b, (((0,), (0,)), ((), ())), preferred_element_type=f32)


def rows16(start):
    return pl.ds(pl.multiple_of(start, BLK), BLK)


def rope_kernel_form(u, cos, sin):
    return u * cos + pltpu.roll(u, HEAD_SIZE // 2, 1) * sin


def rope_back_kernel_form(d, cos, sin):
    return d * cos - pltpu.roll(d, HEAD_SIZE // 2, 1) * sin


def qkv_kernel(dst, *refs):
    pieces = refs[:8]
    w_ref, qg_ref, kg_ref, cos_ref, sin_ref, h_ref, q_ref, k_ref, v_ref, raw_ref = refs[8:]
    step = pl.program_id(0)
    for r in range(8):
        for kk in range(4):
            place = dst[r, step * 4 + kk]
            h_ref[rows16(kk * 128 + place * BLK), :] = pieces[r][kk * BLK : (kk + 1) * BLK, :]
    acc = nn(h_ref[...], w_ref[...])
    cos, sin = cos_ref[...], sin_ref[...]
    for i in range(3):
        u = acc[:, i * 128 : (i + 1) * 128]
        raw_ref[:, i * 128 : (i + 1) * 128] = u
        n, _ = normed_parts(u)
        gain = qg_ref[...] if i < 2 else kg_ref[...]
        out = rope_kernel_form(n * gain, cos, sin).astype(bf16)
        if i < 2:
            q_ref[:, i * 128 : (i + 1) * 128] = out
        else:
            k_ref[...] = out
    v_ref[...] = acc[:, 384:].astype(bf16)


def qkv_call(dst, pieces, w, qg, kg, cos, sin, group_length):
    rows = 512
    return pl.pallas_call(
        qkv_kernel,
        grid_spec=pltpu.PrefetchScalarGridSpec(
            num_scalar_prefetch=1,
            grid=(group_length // rows,),
            in_specs=[pl.BlockSpec((rows // 8, w.shape[0]), lambda g, d: (g, 0))] * 8
            + [
                pl.BlockSpec(w.shape, lambda g, d: (0, 0)),
                pl.BlockSpec((1, 128), lambda g, d: (0, 0)),
                pl.BlockSpec((1, 128), lambda g, d: (0, 0)),
                pl.BlockSpec((rows, 128), lambda g, d: (g, 0)),
                pl.BlockSpec((rows, 128), lambda g, d: (g, 0)),
            ],
            out_specs=[
                pl.BlockSpec((rows, w.shape[0]), lambda g, d: (g, 0)),
                pl.BlockSpec((rows, 256), lambda g, d: (g, 0)),
                pl.BlockSpec((rows, 128), lambda g, d: (g, 0)),
                pl.BlockSpec((rows, 128), lambda g, d: (g, 0)),
                pl.BlockSpec((rows, 384), lambda g, d: (g, 0)),
            ],
        ),
        out_shape=[
            jax.ShapeDtypeStruct((group_length, w.shape[0]), bf16),
            jax.ShapeDtypeStruct((group_length, 256), bf16),
            jax.ShapeDtypeStruct((group_length, 128), bf16),
            jax.ShapeDtypeStruct((group_length, 128), bf16),
            jax.ShapeDtypeStruct((group_length, 384), f32),
        ],
        compiler_params=pltpu.CompilerParams(vmem_limit_bytes=VMEM_LIMIT),
        name="qkv_rope",
    )(dst, *pieces, w, qg, kg, cos, sin)


def causal(p, first_key, first_row):
    key = lax.broadcasted_iota(jnp.int32, p.shape, 0) + first_key
    row = lax.broadcasted_iota(jnp.int32, p.shape, 1) + first_row
    return jnp.where(key <= row, p, 0.0)


SPAN = 512
PROMPT_UNITS = tuple(
    (row0, tuple((key0, key0 == row0) for key0 in range(0, row0 + 1, SPAN)))
    for row0 in range(0, PROMPT, SPAN)
)


def attn_fwd_kernel(n_cont, dst, q_ref, k_ref, v_ref, *refs):
    outs = refs[:8]
    o_ref, lse_ref, vt_ref = refs[8:]
    vt_ref[...] = jnp.transpose(v_ref[:PROMPT, :])

    def unit(index, row0, n, tiles):
        for h in range(2):
            cols = slice(h * 128, (h + 1) * 128)
            qh = q_ref[pl.ds(row0, n), cols]
            total = jnp.zeros((1, n), f32)
            mixed = jnp.zeros((HEAD_SIZE, n), f32)
            for keys, values_t, diagonal in tiles:
                p = jnp.exp2(nt(keys, qh) * EXP2_SCALE)
                if diagonal:
                    p = causal(p, 0, 0)
                total = total + jnp.sum(p, axis=0, keepdims=True)
                mixed = mixed + nn(values_t, p.astype(bf16))
            o_ref[pl.ds(row0, n), cols] = jnp.transpose(mixed / total)
            lse_ref[index, h : h + 1, :n] = jnp.log2(total)

    def prompt_tile(key0, diagonal):
        return (k_ref[key0 : key0 + SPAN, :], vt_ref[:, key0 : key0 + SPAN], diagonal)

    for index, (row0, tiles) in enumerate(PROMPT_UNITS):
        unit(index, row0, SPAN, [prompt_tile(*t) for t in tiles])

    def continuation(c, carry):
        row0 = pl.multiple_of(PROMPT + c * CONT_LEN, 64)
        own = pl.ds(row0, CONT_LEN)
        tiles = [prompt_tile(key0, False) for key0 in range(0, PROMPT, SPAN)]
        tiles.append((k_ref[own, :], jnp.transpose(v_ref[own, :]), True))
        unit(c + len(PROMPT_UNITS), row0, CONT_LEN, tiles)
        return carry

    lax.fori_loop(0, n_cont, continuation, 0)

    def send_slot(slot, carry):
        for r in range(8):
            natural = slot * 128 + dst[r, slot] * BLK
            rows = o_ref[rows16(natural), :].astype(bf16)
            head, other = r // 4, 1 - r // 4
            outs[r][rows16(slot * BLK), :] = rows[:, head * 128 : (head + 1) * 128]
            outs[r ^ 4][rows16(slot * BLK + outs[0].shape[0] // 2), :] = rows[
                :, other * 128 : (other + 1) * 128
            ]
        return carry

    lax.fori_loop(0, outs[0].shape[0] // 2 // BLK, send_slot, 0)


def whole_call(kernel, name, args, outs, scratch, cost):
    smem = pl.BlockSpec(memory_space=pltpu.SMEM)
    vmem = pl.BlockSpec(memory_space=pltpu.VMEM)
    return pl.pallas_call(
        kernel,
        in_specs=[smem if a.dtype == jnp.int32 else vmem for a in args],
        out_specs=[vmem] * len(outs),
        out_shape=[jax.ShapeDtypeStruct(s, t) for s, t in outs],
        scratch_shapes=scratch,
        compiler_params=pltpu.CompilerParams(vmem_limit_bytes=VMEM_LIMIT),
        cost_estimate=pl.CostEstimate(flops=cost, bytes_accessed=20000000, transcendentals=0),
        name=name,
    )(*args)


def attn_fwd_call(dst, q, k, v):
    length = q.shape[0]
    n_cont = (length - PROMPT) // CONT_LEN
    row_total = length // 8
    outs = [((2 * row_total, 128), bf16)] * 8 + [
        ((length, 256), f32),
        ((n_cont + len(PROMPT_UNITS), 8, SPAN), f32),
    ]
    return whole_call(
        functools.partial(attn_fwd_kernel, n_cont),
        "attn_fwd",
        (dst, q, k, v),
        outs,
        [pltpu.VMEM((128, PROMPT), bf16)],
        7000000000,
    )


def attn_bwd_kernel(n_cont, dst, flag, q_ref, k_ref, v_ref, o_ref, lse_ref, raw_ref, *refs):
    pieces = refs[:8]
    qg_ref, kg_ref, cos_ref, sin_ref = refs[8:12]
    outs = refs[12:20]
    grads_ref, gains_ref, do_ref, kt_ref, dk_ref, dv_ref = refs[20:]
    row_total = pieces[0].shape[0] // 2

    def take_slot(slot, carry):
        for r in range(8):
            natural = slot * 128 + dst[r, slot] * BLK
            head, other = r // 4, 1 - r // 4
            do_ref[rows16(natural), head * 128 : (head + 1) * 128] = pieces[r][
                rows16(slot * BLK), :
            ]
            do_ref[rows16(natural), other * 128 : (other + 1) * 128] = pieces[r ^ 4][
                rows16(slot * BLK + row_total), :
            ]
        return carry

    lax.fori_loop(0, row_total // BLK, take_slot, 0)
    kt_ref[...] = jnp.transpose(k_ref[:PROMPT, :])
    dk_ref[...] = jnp.zeros_like(dk_ref)
    dv_ref[...] = jnp.zeros_like(dv_ref)
    gains_ref[...] = jnp.zeros_like(gains_ref)

    def head_back(grad, row0, n, head, table0, gain, gain_row):
        cols = slice(head * 128, (head + 1) * 128)
        table = slice(table0, table0 + n)
        normed, inverse = normed_parts(raw_ref[pl.ds(row0, n), cols])
        back = rope_back_kernel_form(grad * SCALE, cos_ref[table, :], sin_ref[table, :])
        gains_ref[gain_row : gain_row + 1, :] += jnp.sum(back * normed, axis=0, keepdims=True)
        grads_ref[pl.ds(row0, n), cols] = norm_back(back * gain, normed, inverse).astype(bf16)

    def unit(index, row0, n, table0, tiles):
        for h in range(2):
            cols = slice(h * 128, (h + 1) * 128)
            qh = q_ref[pl.ds(row0, n), cols]
            doh = do_ref[pl.ds(row0, n), cols]
            lse = lse_ref[index, h : h + 1, :n]
            delta = jnp.sum(
                jnp.transpose(doh.astype(f32) * o_ref[pl.ds(row0, n), cols]), axis=0, keepdims=True
            )
            dq = jnp.zeros((HEAD_SIZE, n), f32)
            for keys, keys_t, values, diagonal, accumulate in tiles:
                p = jnp.exp2(nt(keys, qh) * EXP2_SCALE - lse)
                if diagonal:
                    p = causal(p, 0, 0)
                ds = (p * (nt(values, doh) - delta)).astype(bf16)
                accumulate(h, nn(ds, qh), nn(p.astype(bf16), doh))
                dq = dq + nn(keys_t, ds)
            head_back(jnp.transpose(dq), row0, n, h, table0, qg_ref[...], 0)

    def prompt_tile(key0, diagonal):
        keys = slice(key0, key0 + SPAN)

        def accumulate(h, dk, dv):
            dk_ref[keys, :] += dk
            dv_ref[keys, :] += dv

        return (k_ref[keys, :], kt_ref[:, keys], v_ref[keys, :], diagonal, accumulate)

    for index, (row0, tiles) in enumerate(PROMPT_UNITS):
        unit(index, row0, SPAN, row0, [prompt_tile(*t) for t in tiles])

    def continuation(c, carry):
        row0 = pl.multiple_of(PROMPT + c * CONT_LEN, 64)
        own = pl.ds(row0, CONT_LEN)
        kept = []

        def accumulate(h, dk, dv):
            kept.append((dk, dv))

        tiles = [prompt_tile(key0, False) for key0 in range(0, PROMPT, SPAN)]
        keys = k_ref[own, :]
        tiles.append((keys, jnp.transpose(keys), v_ref[own, :], True, accumulate))
        unit(c + len(PROMPT_UNITS), row0, CONT_LEN, PROMPT, tiles)
        head_back(kept[0][0] + kept[1][0], row0, CONT_LEN, 2, PROMPT, kg_ref[...], 1)
        grads_ref[own, 384:] = (kept[0][1] + kept[1][1]).astype(bf16)
        return carry

    lax.fori_loop(0, n_cont, continuation, 0)
    head_back(dk_ref[...], 0, PROMPT, 2, 0, kg_ref[...], 1)
    grads_ref[:PROMPT, 384:] = dv_ref[...].astype(bf16)

    def send_slot(slot, carry):
        for r in range(8):
            natural = slot * 128 + dst[r, slot] * BLK
            rows = grads_ref[rows16(natural), :]
            first = flag[0] == 0
            parts = (
                jnp.where(first, rows[:, 256:384], rows[:, 384:]),
                jnp.where(first, rows[:, 384:], rows[:, 256:384]),
            )
            head, other = r // 4, 1 - r // 4
            own = rows16(slot * BLK)
            outs[r][own, :128] = rows[:, head * 128 : (head + 1) * 128]
            outs[r][own, 128:] = parts[head]
            sibling = rows16(slot * BLK + row_total)
            outs[r ^ 4][sibling, :128] = rows[:, other * 128 : (other + 1) * 128]
            outs[r ^ 4][sibling, 128:] = parts[other]
        return carry

    lax.fori_loop(0, row_total // BLK, send_slot, 0)


def attn_bwd_call(dst, flag, q, k, v, o, lse, raw, pieces, qg, kg, cos, sin):
    length = q.shape[0]
    n_cont = (length - PROMPT) // CONT_LEN
    row_total = length // 8
    outs = [((2 * row_total, 256), bf16)] * 8 + [((length, 512), bf16), ((8, 128), f32)]
    scratch = [
        pltpu.VMEM((length, 256), bf16),
        pltpu.VMEM((128, PROMPT), bf16),
        pltpu.VMEM((PROMPT, 128), f32),
        pltpu.VMEM((PROMPT, 128), f32),
    ]
    return whole_call(
        functools.partial(attn_bwd_kernel, n_cont),
        "attn_bwd",
        (dst, flag, q, k, v, o, lse, raw, *pieces, qg, kg, cos, sin),
        outs,
        scratch,
        17000000000,
    )


def device_of(y, core, z_hi, z_lo, x):
    return (y * 2 + core) * N_CTX + z_hi * 4 + z_lo * 2 + x


def permutation(target):
    pairs = []
    for i in range(N_GRP * N_CTX):
        bits = ((i >> 4) & 1, (i >> 3) & 1, (i >> 2) & 1, (i >> 1) & 1, i & 1)
        pairs.append((i, device_of(*target(*bits))))
    return pairs


HALVES = permutation(lambda y, core, z_hi, z_lo, x: (y, z_hi, core, z_lo, x))
OVER_Y = permutation(lambda y, core, z_hi, z_lo, x: (1 - y, core, z_hi, z_lo, x))
SIBLING = permutation(lambda y, core, z_hi, z_lo, x: (y, 1 - core, z_hi, z_lo, x))
CUBE = [
    permutation(
        lambda y, core, z_hi, z_lo, x, r=r: (
            y,
            core ^ (r >> 2),
            z_hi,
            z_lo ^ ((r >> 1) & 1),
            x ^ (r & 1),
        )
    )
    for r in range(8)
]
CUBES = [
    [device_of(y, m >> 2, z_hi, (m >> 1) & 1, m & 1) for m in range(8)]
    for y in range(2)
    for z_hi in range(2)
]


def permute(a, pairs):
    return lax.ppermute(a, AXES, pairs)


def exchange(chunks):
    return [chunks[0]] + [permute(chunks[r], CUBE[r]) for r in range(1, 8)]


def gather_cube(a):
    near = [a] + [permute(a, CUBE[r]) for r in range(1, 4)]
    return near + [permute(t, SIBLING) for t in near]


def relative(a, member):
    return jnp.concatenate(
        [lax.dynamic_slice_in_dim(a, member ^ r, 1, 0) for r in range(a.shape[0])], axis=0
    )


def reduce_owned(grad, core):
    part = lax.psum_scatter(grad, "ctx", scatter_dimension=0, tiled=True)
    part = (part.astype(f32) + permute(part, OVER_Y).astype(f32)).astype(bf16)
    other = permute(part, SIBLING)
    first = core == 0
    return jnp.where(first, part, other), jnp.where(first, other, part)


def shards_split(
    tokens,
    block_table,
    norm1_gain,
    w_query,
    key_weight,
    value_weight,
    query_gain,
    key_norm_gain,
    w_out,
    norm2_gain,
    w_gate,
    w_up,
    w_down,
    out_grad,
):
    row_total, width = tokens.shape
    group_length = block_table.shape[0] * BLK
    n_slots = row_total // BLK
    ff = w_gate.shape[1]
    position = lax.axis_index("ctx")
    core = lax.axis_index("grp") % 2
    member = core * 4 + position % 4
    qg, kg = query_gain.reshape(1, 128), key_norm_gain.reshape(1, 128)

    inputs_low = permute(tokens, HALVES)
    inputs = inputs_low.astype(f32)
    normed_one, inverse_one = normed_parts(inputs)
    first_hidden = (normed_one * norm1_gain).astype(bf16)
    hidden_pieces = gather_cube(first_hidden)

    def half(w, parts):
        return lax.dynamic_index_in_dim(w, core, parts, keepdims=False)

    query_parts = w_query.reshape(-1, 8, 2, 128)
    key_parts = key_weight.reshape(-1, 8, 128)
    value_parts = value_weight.reshape(-1, 8, 128)
    swapped = jnp.concatenate([query_parts[:, :4], query_parts[:, 4:, ::-1]], axis=1)
    own_columns = jnp.concatenate(
        [swapped.reshape(-1, 8, 256), key_parts, value_parts], axis=2
    ).transpose(1, 0, 2)
    w_attn = lax.all_to_all(
        permute(own_columns, HALVES), AXES, 0, 0, tiled=True, axis_index_groups=CUBES
    ).reshape(width, 512)

    gate_half = half(w_gate.reshape(-1, N_CTX, 2, ff // 16), 2).reshape(-1, ff // 2)
    up_half = half(w_up.reshape(-1, N_CTX, 2, ff // 16), 2).reshape(-1, ff // 2)
    down_half = half(w_down.reshape(2, -1, width), 0)
    out_half = half(w_out.reshape(2, -1, width), 0)
    back_half = jnp.concatenate(
        [half(query_parts, 2), jnp.where(core == 0, key_parts, value_parts)], axis=2
    ).reshape(-1, 2048)

    def gather(w):
        return lax.all_gather(w, "ctx", axis=0, tiled=True)

    out_rel = relative(gather(out_half).reshape(8, 128, width), member).reshape(8 * 128, width)
    gate_full, up_full, down_full = gather(gate_half), gather(up_half), gather(down_half)
    back_full = gather(back_half).reshape(width, 8, 256).transpose(1, 0, 2)
    back_rel = relative(back_full, member).transpose(1, 0, 2).reshape(width, 2048)
    grad_low = permute(out_grad, HALVES)
    grad_both = jnp.concatenate([grad_low, permute(grad_low, SIBLING)], axis=0)

    cosine, sine = rotation(jnp.arange(PROMPT + CONT_LEN, dtype=jnp.int32))
    cos = jnp.concatenate([cosine[:, 0], cosine[:, 0]], axis=1)
    sin = jnp.concatenate([-sine[:, 0], sine[:, 0]], axis=1)
    n_cont = (group_length - PROMPT) // CONT_LEN
    cos_all = jnp.concatenate([cos[:PROMPT]] + [cos[PROMPT:]] * n_cont, axis=0)
    sin_all = jnp.concatenate([sin[:PROMPT]] + [sin[PROMPT:]] * n_cont, axis=0)

    dst = relative(block_table.reshape(8, n_slots), member) - 8 * jnp.arange(n_slots)[None, :]

    h_nat, q, k, v, raw = qkv_call(
        dst, hidden_pieces, w_attn, qg, kg, cos_all, sin_all, group_length
    )
    *mixed_out, mixed, lse = attn_fwd_call(dst, q, k, v)
    mixed_both = jnp.concatenate(exchange(mixed_out), axis=1)

    def with_sibling(part):
        return part[:row_total] + permute(part[row_total:].astype(bf16), SIBLING).astype(f32)

    def both(a):
        return jnp.concatenate([a, permute(a, SIBLING)], axis=0)

    resid_one = inputs + with_sibling(nn(mixed_both, out_rel))
    normed_two, inverse_two = normed_parts(resid_one)
    hidden_two = both((normed_two * norm2_gain).astype(bf16))
    gate_proj = nn(hidden_two, gate_full)
    up_proj = nn(hidden_two, up_full)
    gate_sigmoid = jax.nn.sigmoid(gate_proj)
    gate_silu = gate_proj * gate_sigmoid
    hidden_low = (gate_silu * up_proj).astype(bf16)
    outcome = (resid_one + with_sibling(nn(hidden_low, down_full))).astype(bf16)
    outcome = permute(outcome, HALVES)

    grad_hidden = nt(grad_both, down_full)
    grad_gate = (
        grad_hidden * up_proj * gate_sigmoid * (1.0 + gate_proj * (1.0 - gate_sigmoid))
    ).astype(bf16)
    grad_up = (grad_hidden * gate_silu).astype(bf16)
    grad_two = with_sibling(nt(grad_gate, gate_full) + nt(grad_up, up_full))
    gain_two_part = jnp.sum(grad_two * normed_two, axis=0)
    grad_resid = grad_low.astype(f32) + norm_back(grad_two * norm2_gain, normed_two, inverse_two)
    grad_attn = both(grad_resid.astype(bf16))
    mixed_grads = nt(grad_attn, out_rel).astype(bf16)
    grad_pieces = exchange([mixed_grads[:, r * 128 : (r + 1) * 128] for r in range(8)])

    grad_wdown = tn(hidden_low, grad_both).astype(bf16)
    grad_wgate = tn(hidden_two, grad_gate).astype(bf16)
    grad_wup = tn(hidden_two, grad_up).astype(bf16)
    grad_wout = tn(mixed_both, grad_attn).astype(bf16)
    grad_wout = relative(grad_wout.reshape(8, 128, width), member).reshape(8 * 128, width)

    flag = core.astype(jnp.int32).reshape(1)
    *qkv_out, qkv_grads, gains = attn_bwd_call(
        dst, flag, q, k, v, mixed, lse, raw, grad_pieces, qg, kg, cos, sin
    )
    qkv_both = jnp.concatenate(exchange(qkv_out), axis=1)
    grad_one = with_sibling(nt(qkv_both, back_rel))
    gain_one_part = jnp.sum(grad_one * normed_one, axis=0)
    grad_tokens = grad_resid + norm_back(grad_one * norm1_gain, normed_one, inverse_one)
    grad_tokens = permute(grad_tokens.astype(bf16), HALVES).astype(f32)

    def interleave(grad):
        pair = reduce_owned(grad, core)
        return (
            jnp.stack([p.reshape(-1, N_CTX, ff // 16) for p in pair], axis=2)
            .reshape(-1, ff)
            .astype(f32)
        )

    grad_wgate, grad_wup = interleave(grad_wgate), interleave(grad_wup)
    grad_wdown = jnp.concatenate(reduce_owned(grad_wdown, core), axis=0).astype(f32)
    grad_wout = jnp.concatenate(reduce_owned(grad_wout, core), axis=0).astype(f32)

    grad_attn_w = tn(h_nat, qkv_grads).astype(bf16)
    owned = lax.all_to_all(
        grad_attn_w.reshape(8, -1, 512), AXES, 0, 0, tiled=True, axis_index_groups=CUBES
    )
    owned = permute(owned, HALVES)
    owned = (owned.astype(f32) + permute(owned, OVER_Y).astype(f32)).astype(bf16)
    owned = owned.astype(f32) + permute(owned, SIBLING).astype(f32)
    owned = owned.transpose(1, 0, 2)
    query_grads = owned[:, :, :256].reshape(-1, 8, 2, 128)
    query_grads = jnp.concatenate([query_grads[:, :4], query_grads[:, 4:, ::-1]], axis=1)

    gain_grads = lax.psum((gain_one_part, gains[0], gains[1], gain_two_part), AXES)
    return (
        outcome,
        grad_tokens,
        gain_grads[0],
        query_grads.reshape(-1, 2048),
        owned[:, :, 256:384].reshape(-1, 1024),
        owned[:, :, 384:].reshape(-1, 1024),
        gain_grads[1],
        gain_grads[2],
        grad_wout,
        gain_grads[3],
        grad_wgate,
        grad_wup,
        grad_wdown,
    )


def solution(mesh):
    split = mesh.shape["grp"] == N_GRP and mesh.shape["ctx"] == N_CTX
    return jax.shard_map(
        shards_split if split else shards,
        mesh=mesh,
        in_specs=(
            P(("grp", "ctx"), None),
            P(),
            P(),
            P("ctx", None),
            P("ctx", None),
            P("ctx", None),
            P(),
            P(),
            P("ctx", None),
            P(),
            P("ctx", None),
            P("ctx", None),
            P("ctx", None),
            P(("grp", "ctx"), None),
        ),
        out_specs=(
            P(("grp", "ctx"), None),
            P(("grp", "ctx"), None),
            P(),
            P("ctx", None),
            P("ctx", None),
            P("ctx", None),
            P(),
            P(),
            P("ctx", None),
            P(),
            P("ctx", None),
            P("ctx", None),
            P("ctx", None),
        ),
        check_vma=False,
    )
```

```python
import math

import jax
import jax.numpy as jnp
from jax import lax
from jax.experimental import pallas as pl
from jax.experimental.pallas import tpu as pltpu
from jax.sharding import PartitionSpec as P

QUERY_HEADS = 16
KEY_VALUE_HEADS = 8
HEAD_SIZE = 128
PROMPT = 1024
CONT_LEN = 448
BLK = 16


eps = 1e-06
theta = 1000000.0
key_span = 512
masked_score = -1e30


def normed_parts(value_rows):
    inverse = lax.rsqrt(jnp.mean(value_rows * value_rows, axis=-1, keepdims=True) + eps)
    return (value_rows * inverse, inverse)


def norm_back(grad_normed, normed, inverse):
    return inverse * (grad_normed - normed * jnp.mean(grad_normed * normed, axis=-1, keepdims=True))


def layout(block_table, slot_ids):
    natural = block_table[slot_ids // BLK] * BLK + slot_ids % BLK
    beyond = natural - PROMPT
    segment = jnp.where(natural < PROMPT, 0, 1 + beyond // CONT_LEN)
    places = jnp.where(natural < PROMPT, natural, PROMPT + beyond % CONT_LEN)
    return (natural, segment, places)


def rotation(places):
    half_dim = HEAD_SIZE // 2
    frequency = jnp.exp(
        jnp.arange(half_dim, dtype=jnp.float32) * (-2.0 * math.log(theta) / HEAD_SIZE)
    )
    angles = places.astype(jnp.float32)[:, None] * frequency[None, :]
    return (jnp.cos(angles)[:, None, :], jnp.sin(angles)[:, None, :])


def apply_rotation(value_rows, cosine_table, sine_table):
    half_dim = value_rows.shape[-1] // 2
    first_half = value_rows[..., :half_dim]
    second_half = value_rows[..., half_dim:]
    return jnp.concatenate(
        [
            first_half * cosine_table - second_half * sine_table,
            second_half * cosine_table + first_half * sine_table,
        ],
        axis=-1,
    )


def rotate_back(value_rows, cosine_table, sine_table):
    half_dim = value_rows.shape[-1] // 2
    first_half = value_rows[..., :half_dim]
    second_half = value_rows[..., half_dim:]
    return jnp.concatenate(
        [
            first_half * cosine_table + second_half * sine_table,
            second_half * cosine_table - first_half * sine_table,
        ],
        axis=-1,
    )


def allowed_mask(own_nat, own_seg, key_nat, key_seg):
    return (key_nat[None, :] <= own_nat[:, None]) & (
        (key_seg[None, :] == 0) | (key_seg[None, :] == own_seg[:, None])
    )


def span_of():
    return key_span


def over_blocks(advance, running, length):
    block_span_width = span_of()

    def scan_step(inner_state, key_first):
        return (advance(inner_state, key_first, block_span_width), None)

    running, ignored = lax.scan(
        scan_step,
        running,
        jnp.arange(length // block_span_width, dtype=jnp.int32) * block_span_width,
    )
    return running


def attend_block(running, query_head_rows, keys_part, values_part, allowed, softmax_scale):
    row_max, row_sum, accum = running
    raw_scores = (
        jnp.einsum("grtd,ngd->grtn", query_head_rows, keys_part, preferred_element_type=jnp.float32)
        * softmax_scale
    )
    scores = jnp.where(allowed, raw_scores, masked_score)
    new_max = jnp.maximum(row_max, jnp.max(scores, axis=-1))
    rescale = jnp.exp(row_max - new_max)
    weights = jnp.exp(scores - new_max[..., None])
    row_sum = row_sum * rescale + jnp.sum(weights, axis=-1)
    accum = accum * rescale[..., None] + jnp.einsum(
        "grtn,ngd->grtd",
        weights.astype(jnp.bfloat16),
        values_part,
        preferred_element_type=jnp.float32,
    )
    return (new_max, row_sum, accum)


def key_terms(
    grad_scores, weights, query_head_rows, scaled_high, scaled_rest, softmax_scale, block_span_width
):
    grad_keys = (
        jnp.einsum(
            "grtn,grtd->ngd", grad_scores, query_head_rows, preferred_element_type=jnp.float32
        )
        * softmax_scale
    )
    weights_low = weights.astype(jnp.bfloat16)
    grad_values = jnp.einsum(
        "grtn,grtd->ngd", weights_low, scaled_high, preferred_element_type=jnp.float32
    )
    grad_values = grad_values + jnp.einsum(
        "grtn,grtd->ngd", weights_low, scaled_rest, preferred_element_type=jnp.float32
    )
    return jnp.stack(
        [grad_keys.reshape(block_span_width, -1), grad_values.reshape(block_span_width, -1)], axis=1
    )


def shards(
    tokens,
    block_table,
    norm1_gain,
    w_query,
    key_weight,
    value_weight,
    query_gain,
    key_norm_gain,
    w_out,
    norm2_gain,
    w_gate,
    w_up,
    w_down,
    out_grad,
):
    row_total = tokens.shape[0]
    group_length = block_table.shape[0] * BLK
    sharing_count = QUERY_HEADS // KEY_VALUE_HEADS
    softmax_scale = 1.0 / math.sqrt(HEAD_SIZE)
    position = lax.axis_index("ctx")
    all_nat, all_seg, all_places = layout(block_table, jnp.arange(group_length, dtype=jnp.int32))
    own_slots = position * row_total + jnp.arange(row_total, dtype=jnp.int32)
    own_nat, own_seg, own_places = layout(block_table, own_slots)
    cosine_table, sine_table = rotation(own_places)
    query_full, key_full, value_full, out_full = (
        lax.all_gather(w_query, "ctx", axis=0, tiled=True),
        lax.all_gather(key_weight, "ctx", axis=0, tiled=True),
        lax.all_gather(value_weight, "ctx", axis=0, tiled=True),
        lax.all_gather(w_out, "ctx", axis=0, tiled=True),
    )
    inputs = tokens.astype(jnp.float32)
    normed_one, inverse_one = normed_parts(inputs)
    first_hidden = (normed_one * norm1_gain).astype(jnp.bfloat16)
    query_raw = jnp.dot(first_hidden, query_full, preferred_element_type=jnp.float32).reshape(
        row_total, QUERY_HEADS, HEAD_SIZE
    )
    unnormalized_keys = jnp.dot(first_hidden, key_full, preferred_element_type=jnp.float32).reshape(
        row_total, KEY_VALUE_HEADS, HEAD_SIZE
    )
    reduced_value = jnp.dot(first_hidden, value_full, preferred_element_type=jnp.float32).astype(
        jnp.bfloat16
    )
    query_normed, query_inverse = normed_parts(query_raw)
    normalized_keys, key_inverse = normed_parts(unnormalized_keys)
    reduced_query = apply_rotation(query_normed * query_gain, cosine_table, sine_table).astype(
        jnp.bfloat16
    )
    key_low = (
        apply_rotation(normalized_keys * key_norm_gain, cosine_table, sine_table)
        .astype(jnp.bfloat16)
        .reshape(row_total, KEY_VALUE_HEADS * HEAD_SIZE)
    )
    query_head_rows = jnp.transpose(
        reduced_query.reshape(row_total, KEY_VALUE_HEADS, sharing_count, HEAD_SIZE), (1, 2, 0, 3)
    )

    def attend(running, pieces):
        piece_keys, piece_values = pieces

        def advance(inner_state, key_first, block_span_width):
            keys_part = lax.dynamic_slice_in_dim(
                piece_keys, key_first, block_span_width, 0
            ).reshape(block_span_width, KEY_VALUE_HEADS, HEAD_SIZE)
            values_part = lax.dynamic_slice_in_dim(
                piece_values, key_first, block_span_width, 0
            ).reshape(block_span_width, KEY_VALUE_HEADS, HEAD_SIZE)
            key_nat = lax.dynamic_slice_in_dim(all_nat, key_first, block_span_width)
            key_seg = lax.dynamic_slice_in_dim(all_seg, key_first, block_span_width)
            allowed = allowed_mask(own_nat, own_seg, key_nat, key_seg)
            return attend_block(
                inner_state, query_head_rows, keys_part, values_part, allowed, softmax_scale
            )

        return over_blocks(advance, running, piece_keys.shape[0])

    statistic_shape = (KEY_VALUE_HEADS, sharing_count, row_total)
    initial = (
        jnp.full(statistic_shape, masked_score, jnp.float32),
        jnp.zeros(statistic_shape, jnp.float32),
        jnp.zeros(statistic_shape + (HEAD_SIZE,), jnp.float32),
    )
    row_max, row_sum, accum = attend(
        initial,
        (
            lax.all_gather(key_low, "ctx", axis=0, tiled=True),
            lax.all_gather(reduced_value, "ctx", axis=0, tiled=True),
        ),
    )
    mixed_heads = accum / row_sum[..., None]
    flat_low = (
        jnp.transpose(mixed_heads, (2, 0, 1, 3))
        .reshape(row_total, QUERY_HEADS * HEAD_SIZE)
        .astype(jnp.bfloat16)
    )
    resid_one = inputs + jnp.dot(flat_low, out_full, preferred_element_type=jnp.float32)
    gate_full, up_full, down_full = (
        lax.all_gather(w_gate, "ctx", axis=0, tiled=True),
        lax.all_gather(w_up, "ctx", axis=0, tiled=True),
        lax.all_gather(w_down, "ctx", axis=0, tiled=True),
    )
    normed_two, inverse_two = normed_parts(resid_one)
    hidden_two = (normed_two * norm2_gain).astype(jnp.bfloat16)
    gate_proj = jnp.dot(hidden_two, gate_full, preferred_element_type=jnp.float32)
    up_proj = jnp.dot(hidden_two, up_full, preferred_element_type=jnp.float32)
    gate_sigmoid = jax.nn.sigmoid(gate_proj)
    gate_silu = gate_proj * gate_sigmoid
    hidden_low = (gate_silu * up_proj).astype(jnp.bfloat16)
    outcome = resid_one + jnp.dot(hidden_low, down_full, preferred_element_type=jnp.float32)
    gate_full, up_full, down_full = (
        lax.all_gather(w_gate, "ctx", axis=0, tiled=True),
        lax.all_gather(w_up, "ctx", axis=0, tiled=True),
        lax.all_gather(w_down, "ctx", axis=0, tiled=True),
    )
    grad_out = out_grad.astype(jnp.float32)
    grad_down = jnp.einsum("tf,td->fd", hidden_low, out_grad, preferred_element_type=jnp.float32)
    grad_hidden = jnp.einsum("td,fd->tf", out_grad, down_full, preferred_element_type=jnp.float32)
    grad_gate = (
        grad_hidden * up_proj * gate_sigmoid * (1.0 + gate_proj * (1.0 - gate_sigmoid))
    ).astype(jnp.bfloat16)
    grad_up = (grad_hidden * gate_silu).astype(jnp.bfloat16)
    grad_wgate = jnp.einsum("tk,tf->kf", hidden_two, grad_gate, preferred_element_type=jnp.float32)
    grad_wup = jnp.einsum("tk,tf->kf", hidden_two, grad_up, preferred_element_type=jnp.float32)
    grad_two = jnp.einsum(
        "tf,kf->tk", grad_gate, gate_full, preferred_element_type=jnp.float32
    ) + jnp.einsum("tf,kf->tk", grad_up, up_full, preferred_element_type=jnp.float32)
    gain_two_part = jnp.sum(grad_two * normed_two, axis=0)
    grad_resid = grad_out + norm_back(grad_two * norm2_gain, normed_two, inverse_two)
    grad_attn = grad_resid.astype(jnp.bfloat16)
    query_full, key_full, value_full, out_full = (
        lax.all_gather(w_query, "ctx", axis=0, tiled=True),
        lax.all_gather(key_weight, "ctx", axis=0, tiled=True),
        lax.all_gather(value_weight, "ctx", axis=0, tiled=True),
        lax.all_gather(w_out, "ctx", axis=0, tiled=True),
    )
    keys_all, values_all = (
        lax.all_gather(key_low, "ctx", axis=0, tiled=True),
        lax.all_gather(reduced_value, "ctx", axis=0, tiled=True),
    )
    grad_wout = jnp.einsum("tk,td->kd", flat_low, grad_attn, preferred_element_type=jnp.float32)
    flattened_grad = jnp.einsum(
        "td,kd->tk", grad_attn, out_full, preferred_element_type=jnp.float32
    ).astype(jnp.bfloat16)
    head_grads = jnp.transpose(
        flattened_grad.reshape(row_total, KEY_VALUE_HEADS, sharing_count, HEAD_SIZE), (1, 2, 0, 3)
    )
    grad_heads_wide = head_grads.astype(jnp.float32)
    row_delta = jnp.sum(grad_heads_wide * mixed_heads, axis=-1)
    scaled_grad = grad_heads_wide / row_sum[..., None]
    scaled_high = scaled_grad.astype(jnp.bfloat16)
    scaled_rest = (scaled_grad - scaled_high.astype(jnp.float32)).astype(jnp.bfloat16)

    def block_back(key_first, block_span_width):
        keys_part = lax.dynamic_slice_in_dim(keys_all, key_first, block_span_width, 0).reshape(
            block_span_width, KEY_VALUE_HEADS, HEAD_SIZE
        )
        values_part = lax.dynamic_slice_in_dim(values_all, key_first, block_span_width, 0).reshape(
            block_span_width, KEY_VALUE_HEADS, HEAD_SIZE
        )
        key_nat = lax.dynamic_slice_in_dim(all_nat, key_first, block_span_width)
        key_seg = lax.dynamic_slice_in_dim(all_seg, key_first, block_span_width)
        allowed = allowed_mask(own_nat, own_seg, key_nat, key_seg)
        raw_scores = (
            jnp.einsum(
                "grtd,ngd->grtn", query_head_rows, keys_part, preferred_element_type=jnp.float32
            )
            * softmax_scale
        )
        scores = jnp.where(allowed, raw_scores, masked_score)
        weights = jnp.exp(scores - row_max[..., None])
        grad_prob = jnp.einsum(
            "grtd,ngd->grtn", head_grads, values_part, preferred_element_type=jnp.float32
        )
        grad_scores = (weights * (grad_prob - row_delta[..., None]) / row_sum[..., None]).astype(
            jnp.bfloat16
        )
        return (keys_part, grad_scores, weights)

    empty_query = jnp.zeros((KEY_VALUE_HEADS, sharing_count, row_total, HEAD_SIZE), jnp.float32)
    span_back = span_of()

    def pass_step(grad_query, key_first):
        keys_part, grad_scores, weights = block_back(key_first, span_back)
        grad_query = grad_query + jnp.einsum(
            "grtn,ngd->grtd", grad_scores, keys_part, preferred_element_type=jnp.float32
        )
        return (
            grad_query,
            key_terms(
                grad_scores,
                weights,
                query_head_rows,
                scaled_high,
                scaled_rest,
                softmax_scale,
                span_back,
            ),
        )

    grad_query, key_gradient_parts = lax.scan(
        pass_step, empty_query, jnp.arange(group_length // span_back, dtype=jnp.int32) * span_back
    )
    self_terms = lax.psum_scatter(
        key_gradient_parts.reshape(group_length, 2, KEY_VALUE_HEADS * HEAD_SIZE).astype(
            jnp.bfloat16
        ),
        "ctx",
        scatter_dimension=0,
        tiled=True,
    ).astype(jnp.float32)
    grad_query_rows = jnp.transpose(grad_query * softmax_scale, (2, 0, 1, 3)).reshape(
        row_total, QUERY_HEADS, HEAD_SIZE
    )
    grad_query_normed = rotate_back(grad_query_rows, cosine_table, sine_table)
    gain_query_part = jnp.sum(grad_query_normed * query_normed, axis=(0, 1))
    grad_query_raw = (
        norm_back(grad_query_normed * query_gain, query_normed, query_inverse)
        .reshape(row_total, QUERY_HEADS * HEAD_SIZE)
        .astype(jnp.bfloat16)
    )
    key_row_grads = self_terms[:, 0, :].reshape(row_total, KEY_VALUE_HEADS, HEAD_SIZE)
    grad_key_normed = rotate_back(key_row_grads, cosine_table, sine_table)
    gain_key_part = jnp.sum(grad_key_normed * normalized_keys, axis=(0, 1))
    grad_key_raw = (
        norm_back(grad_key_normed * key_norm_gain, normalized_keys, key_inverse)
        .reshape(row_total, KEY_VALUE_HEADS * HEAD_SIZE)
        .astype(jnp.bfloat16)
    )
    grad_value_low = self_terms[:, 1, :].astype(jnp.bfloat16)
    grad_wquery = jnp.einsum(
        "tk,tq->kq", first_hidden, grad_query_raw, preferred_element_type=jnp.float32
    )
    grad_wkey = jnp.einsum(
        "tk,tq->kq", first_hidden, grad_key_raw, preferred_element_type=jnp.float32
    )
    grad_wvalue = jnp.einsum(
        "tk,tq->kq", first_hidden, grad_value_low, preferred_element_type=jnp.float32
    )
    grad_one = jnp.einsum(
        "tq,kq->tk", grad_query_raw, query_full, preferred_element_type=jnp.float32
    )
    grad_one = grad_one + jnp.einsum(
        "tq,kq->tk", grad_key_raw, key_full, preferred_element_type=jnp.float32
    )
    grad_one = grad_one + jnp.einsum(
        "tq,kq->tk", grad_value_low, value_full, preferred_element_type=jnp.float32
    )
    gain_one_part = jnp.sum(grad_one * normed_one, axis=0)
    grad_tokens = grad_resid + norm_back(grad_one * norm1_gain, normed_one, inverse_one)
    shard_grads = (
        lax.psum_scatter(
            grad_wquery.astype(jnp.bfloat16), "ctx", scatter_dimension=0, tiled=True
        ).astype(jnp.float32),
        lax.psum_scatter(
            grad_wkey.astype(jnp.bfloat16), "ctx", scatter_dimension=0, tiled=True
        ).astype(jnp.float32),
        lax.psum_scatter(
            grad_wvalue.astype(jnp.bfloat16), "ctx", scatter_dimension=0, tiled=True
        ).astype(jnp.float32),
        lax.psum_scatter(
            grad_wout.astype(jnp.bfloat16), "ctx", scatter_dimension=0, tiled=True
        ).astype(jnp.float32),
        lax.psum_scatter(
            grad_wgate.astype(jnp.bfloat16), "ctx", scatter_dimension=0, tiled=True
        ).astype(jnp.float32),
        lax.psum_scatter(
            grad_wup.astype(jnp.bfloat16), "ctx", scatter_dimension=0, tiled=True
        ).astype(jnp.float32),
        lax.psum_scatter(
            grad_down.astype(jnp.bfloat16), "ctx", scatter_dimension=0, tiled=True
        ).astype(jnp.float32),
    )
    shard_grads = (
        lax.psum(shard_grads[0].astype(jnp.bfloat16), "grp").astype(jnp.float32),
        lax.psum(shard_grads[1].astype(jnp.bfloat16), "grp").astype(jnp.float32),
        lax.psum(shard_grads[2].astype(jnp.bfloat16), "grp").astype(jnp.float32),
        lax.psum(shard_grads[3].astype(jnp.bfloat16), "grp").astype(jnp.float32),
        lax.psum(shard_grads[4].astype(jnp.bfloat16), "grp").astype(jnp.float32),
        lax.psum(shard_grads[5].astype(jnp.bfloat16), "grp").astype(jnp.float32),
        lax.psum(shard_grads[6].astype(jnp.bfloat16), "grp").astype(jnp.float32),
    )
    gain_grads = lax.psum(
        (gain_one_part, gain_query_part, gain_key_part, gain_two_part), ("grp", "ctx")
    )
    return (
        outcome.astype(jnp.bfloat16),
        grad_tokens,
        gain_grads[0],
        shard_grads[0],
        shard_grads[1],
        shard_grads[2],
        gain_grads[1],
        gain_grads[2],
        shard_grads[3],
        gain_grads[3],
        shard_grads[4],
        shard_grads[5],
        shard_grads[6],
    )


f32 = jnp.float32
bf16 = jnp.bfloat16
AXES = ("grp", "ctx")
N_GRP = 4
N_CTX = 8
SCALE = 1.0 / math.sqrt(HEAD_SIZE)
EXP2_SCALE = math.log2(math.e) / math.sqrt(HEAD_SIZE)
VMEM_LIMIT = 60 * 1024 * 1024
RUN = 8 * BLK
PROMPT_BLOCKS = PROMPT // BLK
CONT_BLOCKS = CONT_LEN // BLK
CHUNK = 5
HELD = RUN + CONT_LEN


def nt(a, b):
    return lax.dot_general(a, b, (((1,), (1,)), ((), ())), preferred_element_type=f32)


def nn(a, b):
    return jnp.dot(a, b, preferred_element_type=f32)


def tn(a, b):
    return lax.dot_general(a, b, (((0,), (0,)), ((), ())), preferred_element_type=f32)


def rows_at(start, size):
    return pl.ds(pl.multiple_of(start, size), size)


def turned(u):
    return pltpu.roll(u, HEAD_SIZE // 2, 1)


def head(i):
    return slice(i * HEAD_SIZE, (i + 1) * HEAD_SIZE)


def params():
    return pltpu.CompilerParams(vmem_limit_bytes=VMEM_LIMIT)


def whole_call(kernel, name, args, outs, scratch=()):
    smem = pl.BlockSpec(memory_space=pltpu.SMEM)
    vmem = pl.BlockSpec(memory_space=pltpu.VMEM)
    return pl.pallas_call(
        kernel,
        in_specs=[smem if a.dtype == jnp.int32 else vmem for a in args],
        out_specs=[vmem] * len(outs),
        out_shape=[jax.ShapeDtypeStruct(s, t) for s, t in outs],
        scratch_shapes=list(scratch),
        compiler_params=params(),
        name=name,
    )(*args)


def deal_kernel(table, rows_ref, *outs):
    for e in range(8):
        for i in range(CHUNK):
            outs[e][i * BLK : (i + 1) * BLK, :] = rows_ref[rows_at(table[e, i] * BLK, BLK), :]


def deal(table, rows):
    shape = (CHUNK * BLK, rows.shape[1])
    return whole_call(deal_kernel, "deal_rows", (table, rows), [(shape, rows.dtype)] * 8)


def deal_all_kernel(table, rows_ref, out_ref):
    for e in range(8):
        for i in range(CHUNK):
            out_ref[e, i * BLK : (i + 1) * BLK, :] = rows_ref[rows_at(table[e, i] * BLK, BLK), :]


def deal_all(table, rows):
    shape = (8, CHUNK * BLK, rows.shape[1])
    return whole_call(deal_all_kernel, "deal_all", (table, rows), [(shape, rows.dtype)])[0]


def place_all_kernel(table, pieces, out_ref, held):
    for e in range(8):
        for i in range(CHUNK):
            held[rows_at(table[e, i] * BLK, BLK), :] = pieces[e, i * BLK : (i + 1) * BLK, :]
    out_ref[...] = held[: out_ref.shape[0], :].astype(out_ref.dtype)


def place_all(table, pieces, n_rows, kind):
    shape = (n_rows, pieces.shape[2])
    return whole_call(
        place_all_kernel,
        "place_all",
        (table, pieces),
        [(shape, kind)],
        [pltpu.VMEM((n_rows + BLK, shape[1]), pieces.dtype)],
    )[0]


def place_kernel(table, *refs):
    pieces, out_ref, held = refs[:8], refs[8], refs[-1]
    for e in range(8):
        for i in range(CHUNK):
            held[rows_at(table[e, i] * BLK, BLK), :] = pieces[e][i * BLK : (i + 1) * BLK, :]
    out_ref[...] = held[: out_ref.shape[0], :].astype(out_ref.dtype)


def place(table, pieces, n_rows, kind):
    shape = (n_rows, pieces[0].shape[1])
    return whole_call(
        place_kernel,
        "place_rows",
        (table, *pieces),
        [(shape, kind)],
        [pltpu.VMEM((n_rows + BLK, shape[1]), pieces[0].dtype)],
    )[0]


def place_norm_kernel(table, *refs):
    gain_ref, out_ref, low_ref, held = refs[8:]
    place_kernel(table, *refs[:8], out_ref, held)
    normed, _ = normed_parts(out_ref[...].astype(f32))
    low_ref[...] = (normed * gain_ref[...]).astype(bf16)


def place_norm(table, pieces, gain, n_rows):
    shape = (n_rows, pieces[0].shape[1])
    return whole_call(
        place_norm_kernel,
        "place_rows_norm",
        (table, *pieces, gain),
        [(shape, bf16), (shape, bf16)],
        [pltpu.VMEM((n_rows + BLK, shape[1]), bf16)],
    )


def gathered_rows(info, pieces, w_ref):
    for e in range(8):
        w_ref[rows_at((info[0] ^ e) * 128, 128), :] = pieces[e][...]


def lane_mean(u):
    ones = jnp.full((HEAD_SIZE, HEAD_SIZE), 1.0 / HEAD_SIZE, bf16)
    high = u.astype(bf16)
    return nn(high, ones) + nn((u - high.astype(f32)).astype(bf16), ones)


def head_normed(u):
    inverse = lax.rsqrt(lane_mean(u * u) + eps)
    return u * inverse, inverse


def query_kernel(info, h_ref, *refs):
    gain_ref, cos_ref, sin_ref, q_ref, raw_ref, w_ref = refs[8:]
    gathered_rows(info, refs[:8], w_ref)
    acc = nn(h_ref[...], w_ref[...])
    raw_ref[...] = acc
    for i in range(2):
        normed, _ = head_normed(acc[:, head(i)])
        u = normed * gain_ref[...]
        q_ref[:, head(i)] = (u * cos_ref[...] + turned(u) * sin_ref[...]).astype(bf16)


def key_value_kernel(info, h_ref, *refs):
    gain_ref, cos_ref, sin_ref, kv_ref, raw_ref, w_ref, send_ref = refs[8:]
    gathered_rows(info, refs[:8], w_ref)
    acc = nn(h_ref[...], w_ref[...])
    raw_ref[...] = acc[:, head(0)]
    normed, _ = head_normed(acc[:, head(0)])
    u = normed * gain_ref[...]
    kv_ref[:, head(0)] = (u * cos_ref[...] + turned(u) * sin_ref[...]).astype(bf16)
    kv_ref[:, head(1)] = acc[:, head(1)].astype(bf16)
    for b in range(2):
        send_ref[b * RUN : (b + 1) * RUN, :] = kv_ref[b * HELD : b * HELD + RUN, :]


def project(kernel, name, info, hidden, pieces, first, gain, cos, sin, raw_width, extra):
    rows, width = hidden.shape

    def still(g, s):
        return (0, 0)

    def moving(g, s):
        return (0, g)

    return pl.pallas_call(
        kernel,
        grid_spec=pltpu.PrefetchScalarGridSpec(
            num_scalar_prefetch=1,
            grid=(4,),
            in_specs=[pl.BlockSpec((rows, width), still)]
            + [pl.BlockSpec((128, 256), lambda g, s: (0, g + first))] * 8
            + [
                pl.BlockSpec((1, HEAD_SIZE), still),
                pl.BlockSpec((rows, HEAD_SIZE), still),
                pl.BlockSpec((rows, HEAD_SIZE), still),
            ],
            out_specs=[
                pl.BlockSpec((rows, 256), moving),
                pl.BlockSpec((rows, raw_width), moving),
                pl.BlockSpec((width, 256), moving),
            ]
            + [pl.BlockSpec((2 * RUN, 256), moving)] * extra,
        ),
        out_shape=[
            jax.ShapeDtypeStruct((rows, 1024), bf16),
            jax.ShapeDtypeStruct((rows, 4 * raw_width), f32),
            jax.ShapeDtypeStruct((width, 1024), bf16),
        ]
        + [jax.ShapeDtypeStruct((2 * RUN, 1024), bf16)] * extra,
        compiler_params=params(),
        name=name,
    )(info, hidden, *pieces, gain, cos, sin)


def seen_in_prompt(info, half):
    key = lax.broadcasted_iota(jnp.int32, (PROMPT, RUN), 0)
    tile = key // RUN
    run = info[3] ^ (tile // 2 + 4 * (tile % 2))
    row = lax.broadcasted_iota(jnp.int32, (PROMPT, RUN), 1) + (info[3] ^ (4 * half)) * RUN
    return run * RUN + key % RUN <= row


def seen_in_own():
    key = lax.broadcasted_iota(jnp.int32, (CONT_LEN, CONT_LEN), 0)
    row = lax.broadcasted_iota(jnp.int32, (CONT_LEN, CONT_LEN), 1)
    return key <= row


LSE_SPAN = 640


def units():
    for b in range(2):
        yield b, b * HELD + RUN, CONT_LEN, b * LSE_SPAN, False
    for b in range(2):
        yield b, b * HELD, RUN, b * LSE_SPAN + 512, True


def attn_fwd_kernel(info, q_ref, kv_ref, p0, p1, p2, p3, o_ref, lse_ref, p_ref):
    for t, p in enumerate((p0, p1, p2, p3)):
        p_ref[t * 2 * RUN : (t + 1) * 2 * RUN, :] = p[...]
    prompt = (p_ref[:, head(0)], jnp.transpose(p_ref[:, head(1)]))
    for b, row0, n, lane, in_prompt in units():
        own = slice(row0, row0 + n)
        tiles = [(*prompt, seen_in_prompt(info, b) if in_prompt else None)]
        if not in_prompt:
            tiles.append((kv_ref[own, head(0)], jnp.transpose(kv_ref[own, head(1)]), seen_in_own()))
        for i in range(2):
            q = q_ref[own, head(i)]
            total = jnp.zeros((1, n), f32)
            mixed = jnp.zeros((HEAD_SIZE, n), f32)
            for keys, values_t, seen in tiles:
                p = jnp.exp2(nt(keys, q) * EXP2_SCALE)
                if seen is not None:
                    p = jnp.where(seen, p, 0.0)
                total = total + jnp.sum(p, axis=0, keepdims=True)
                mixed = mixed + nn(values_t, p.astype(bf16))
            o_ref[own, head(i)] = jnp.transpose(mixed / total).astype(bf16)
            lse_ref[0, i : i + 1, lane : lane + n] = jnp.log2(total)


def attn_specs(rows, *names):
    specs = {
        "wide": pl.BlockSpec((rows, 256), lambda g, s: (0, g)),
        "head": pl.BlockSpec((rows, HEAD_SIZE), lambda g, s: (0, g)),
        "prompt": pl.BlockSpec((2 * RUN, 256), lambda g, s: (0, g)),
        "lse": pl.BlockSpec((1, 8, 2 * LSE_SPAN), lambda g, s: (g, 0, 0)),
        "table": pl.BlockSpec((rows, HEAD_SIZE), lambda g, s: (0, 0)),
        "gain": pl.BlockSpec((1, HEAD_SIZE), lambda g, s: (0, 0)),
        "gains": pl.BlockSpec((8, HEAD_SIZE), lambda g, s: (0, 0)),
    }
    return [specs[n] for n in names]


def attn_fwd(info, q, kv, prompt):
    rows = q.shape[0]
    return pl.pallas_call(
        attn_fwd_kernel,
        grid_spec=pltpu.PrefetchScalarGridSpec(
            num_scalar_prefetch=1,
            grid=(4,),
            in_specs=attn_specs(rows, "wide", "wide", *["prompt"] * 4),
            out_specs=attn_specs(rows, "wide", "lse"),
            scratch_shapes=[pltpu.VMEM((PROMPT, 256), bf16)],
        ),
        out_shape=[
            jax.ShapeDtypeStruct((rows, 1024), bf16),
            jax.ShapeDtypeStruct((4, 8, 2 * LSE_SPAN), f32),
        ],
        compiler_params=params(),
        cost_estimate=pl.CostEstimate(flops=20*10**9, bytes_accessed=10**7, transcendentals=0),
        name="attn_fwd",
    )(info, q, kv, *prompt)


def key_back(grad, raw, cos, sin, gain):
    normed, inverse = normed_parts(raw)
    grad = grad * SCALE
    back = grad * cos - turned(grad) * sin
    part = jnp.sum(back * normed, axis=0, keepdims=True)
    return norm_back(back * gain, normed, inverse).astype(bf16), part


def attn_bwd_kernel(info, q_ref, kv_ref, p0, p1, p2, p3, *refs):
    do_ref, o_ref, lse_ref, rawq_ref, rawk_ref, qg_ref, kg_ref, cos_ref, sin_ref = refs[:9]
    dq_ref, dkv_ref, d0, d1, d2, d3, gains_ref, dk_ref, dv_ref, p_ref = refs[9:]
    for t, p in enumerate((p0, p1, p2, p3)):
        p_ref[t * 2 * RUN : (t + 1) * 2 * RUN, :] = p[...]
    prompt = (p_ref[:, head(0)], jnp.transpose(p_ref[:, head(0)]), p_ref[:, head(1)])

    @pl.when(pl.program_id(0) == 0)
    def first():
        gains_ref[...] = jnp.zeros_like(gains_ref)

    for number, (b, row0, n, lane, in_prompt) in enumerate(units()):
        own = slice(row0, row0 + n)
        cos, sin = cos_ref[own, :], sin_ref[own, :]
        tiles = [(*prompt, seen_in_prompt(info, b) if in_prompt else None, True)]
        if not in_prompt:
            keys = kv_ref[own, head(0)]
            tiles.append((keys, jnp.transpose(keys), kv_ref[own, head(1)], seen_in_own(), False))
        own_dk = own_dv = 0.0
        for i in range(2):
            q, do = q_ref[own, head(i)], do_ref[own, head(i)]
            lse = lse_ref[0, i : i + 1, lane : lane + n]
            product = do.astype(f32) * o_ref[own, head(i)].astype(f32)
            delta = jnp.sum(jnp.transpose(product), axis=0, keepdims=True)
            dq = jnp.zeros((HEAD_SIZE, n), f32)
            for keys, keys_t, values, seen, shared in tiles:
                p = jnp.exp2(nt(keys, q) * EXP2_SCALE - lse)
                if seen is not None:
                    p = jnp.where(seen, p, 0.0)
                ds = (p * (nt(values, do) - delta)).astype(bf16)
                dk, dv = nn(ds, q), nn(p.astype(bf16), do)
                dq = dq + nn(keys_t, ds)
                if not shared:
                    own_dk, own_dv = own_dk + dk, own_dv + dv
                elif number == 0 and i == 0:
                    dk_ref[...] = dk
                    dv_ref[...] = dv
                else:
                    dk_ref[...] += dk
                    dv_ref[...] += dv
            back, part = key_back(jnp.transpose(dq), rawq_ref[own, head(i)], cos, sin, qg_ref[...])
            dq_ref[own, head(i)] = back
            gains_ref[0:1, :] += part
        if not in_prompt:
            back, part = key_back(own_dk, rawk_ref[own, :], cos, sin, kg_ref[...])
            dkv_ref[own, head(0)] = back
            dkv_ref[own, head(1)] = own_dv.astype(bf16)
            gains_ref[1:2, :] += part
        else:
            dkv_ref[own, :] = jnp.zeros((n, 256), bf16)
    for t, ref in enumerate((d0, d1, d2, d3)):
        ref[:, head(0)] = dk_ref[t * 256 : (t + 1) * 256, :].astype(bf16)
        ref[:, head(1)] = dv_ref[t * 256 : (t + 1) * 256, :].astype(bf16)


def attn_bwd(info, q, kv, prompt, do, o, lse, rawq, rawk, qg, kg, cos, sin):
    rows = q.shape[0]
    return pl.pallas_call(
        attn_bwd_kernel,
        grid_spec=pltpu.PrefetchScalarGridSpec(
            num_scalar_prefetch=1,
            grid=(4,),
            in_specs=attn_specs(rows, "wide", "wide", *["prompt"] * 4, "wide", "wide", "lse")
            + attn_specs(rows, "wide", "head", "gain", "gain", "table", "table"),
            out_specs=attn_specs(rows, "wide", "wide", *["prompt"] * 4, "gains"),
            scratch_shapes=[pltpu.VMEM((PROMPT, HEAD_SIZE), f32)] * 2
            + [pltpu.VMEM((PROMPT, 256), bf16)],
        ),
        out_shape=[jax.ShapeDtypeStruct((rows, 1024), bf16)] * 2
        + [jax.ShapeDtypeStruct((2 * RUN, 1024), bf16)] * 4
        + [jax.ShapeDtypeStruct((8, HEAD_SIZE), f32)],
        compiler_params=params(),
        cost_estimate=pl.CostEstimate(flops=45*10**9, bytes_accessed=10**7, transcendentals=0),
        name="attn_bwd",
    )(info, q, kv, *prompt, do, o, lse, rawq, rawk, qg, kg, cos, sin)


def prompt_back_kernel(d0, d1, d2, d3, dkv_ref, raw_ref, kg_ref, cos_ref, sin_ref, out_ref, gains_ref):
    out_ref[...] = dkv_ref[...]
    gains_ref[...] = jnp.zeros_like(gains_ref)
    for b in range(2):
        rows = slice(b * RUN, (b + 1) * RUN)
        own = slice(b * HELD, b * HELD + RUN)
        for h in range(4):
            cols = slice(h * 256, (h + 1) * 256)
            total = sum(d[rows, cols].astype(f32) for d in (d0, d1, d2, d3))
            back, part = key_back(
                total[:, head(0)], raw_ref[own, head(h)], cos_ref[own, :], sin_ref[own, :], kg_ref[...]
            )
            out_ref[own, h * 256 : h * 256 + 128] = back
            out_ref[own, h * 256 + 128 : (h + 1) * 256] = total[:, head(1)].astype(bf16)
            gains_ref[0:1, :] += part


def out_kernel(info, o_ref, *refs):
    pieces, (own_ref, sib_ref, w_ref) = refs[:2], refs[2:]
    for t in range(4):
        w_ref[rows_at((info[4] ^ t) * 256, 256), :] = pieces[t % 2][t // 2]
    half = own_ref.shape[0]
    own_ref[...] = nn(o_ref[:half, :], w_ref[...])
    sib_ref[...] = nn(o_ref[half:, :], w_ref[...]).astype(bf16)


def mlp_kernel(info, h_ref, g_ref, *refs):
    w2, w3 = refs[:10], refs[10:14]
    hid_ref, dgu_ref, out_ref, outs_ref, dh_ref, dhs_ref = refs[14:20]
    w_ref, wd_ref, out_acc, dh_acc = refs[20:]
    step = pl.program_id(0)
    width = h_ref.shape[1]
    ff = hid_ref.shape[1]
    half = out_ref.shape[0]
    for e in range(8):
        row = (info[0] ^ e) * 128
        w_ref[rows_at(row + info[1] * 64, 64), :] = w2[e][...]
        w_ref[rows_at(row + (1 - info[1]) * 64, 64), :] = w2[8 + e // 4][e % 4]
    for t in range(4):

        @pl.when(step == t)
        def take(t=t):
            wd_ref[...] = w3[t][...]

    @pl.when(step == 0)
    def zero():
        for ref in (out_ref, dh_ref, out_acc, dh_acc):
            ref[...] = jnp.zeros_like(ref)

    for b, out, dh in ((0, out_ref, dh_ref), (1, out_acc, dh_acc)):
        rows = slice(b * half, (b + 1) * half)
        both = nn(h_ref[rows, :], w_ref[...])
        gate, up = both[:, :ff], both[:, ff:]
        sig = jax.nn.sigmoid(gate)
        silu = gate * sig
        hid = (silu * up).astype(bf16)
        hid_ref[rows, :] = hid
        dhid = nt(g_ref[rows, :], wd_ref[...])
        dgu_ref[rows, :ff] = (dhid * up * sig * (1.0 + gate * (1.0 - sig))).astype(bf16)
        dgu_ref[rows, ff:] = (dhid * silu).astype(bf16)
        dh[...] += nt(dgu_ref[rows, :], w_ref[...])
        out[...] += nn(hid, wd_ref[...])

    @pl.when(step == 3)
    def finish():
        outs_ref[...] = out_acc[...].astype(bf16)
        dhs_ref[...] = dh_acc[...].astype(bf16)


def mlp(info, hidden, grad, w2, w3, ff):
    rows, width = hidden.shape
    half = rows // 2
    once = pl.Buffered(1)

    def still(shape):
        return pl.BlockSpec(shape, lambda g, s: (0, 0), pipeline_mode=once)

    return pl.pallas_call(
        mlp_kernel,
        grid_spec=pltpu.PrefetchScalarGridSpec(
            num_scalar_prefetch=1,
            grid=(4,),
            in_specs=[still((rows, width))] * 2
            + [pl.BlockSpec((64, 2 * ff), lambda g, s: (0, s[4] ^ g))] * 8
            + [pl.BlockSpec((4, 64, 2 * ff), lambda g, s: (0, 0, s[4] ^ g))] * 2
            + [still(w3[0].shape)] * 4,
            out_specs=[
                pl.BlockSpec((rows, ff), lambda g, s: (0, s[4] ^ g)),
                pl.BlockSpec((rows, 2 * ff), lambda g, s: (0, s[4] ^ g)),
            ]
            + [pl.BlockSpec((half, width), lambda g, s: (0, 0))] * 4,
            scratch_shapes=[
                pltpu.VMEM((width, 2 * ff), bf16),
                pltpu.VMEM((ff, width), bf16),
                pltpu.VMEM((half, width), f32),
                pltpu.VMEM((half, width), f32),
            ],
        ),
        out_shape=[
            jax.ShapeDtypeStruct((rows, 4 * ff), bf16),
            jax.ShapeDtypeStruct((rows, 8 * ff), bf16),
            jax.ShapeDtypeStruct((half, width), f32),
            jax.ShapeDtypeStruct((half, width), bf16),
            jax.ShapeDtypeStruct((half, width), f32),
            jax.ShapeDtypeStruct((half, width), bf16),
        ],
        compiler_params=params(),
        cost_estimate=pl.CostEstimate(flops=38*10**9, bytes_accessed=10**7, transcendentals=0),
        name="feed_forward",
    )(info, hidden, grad, *w2, *w3)


def device_of(y, core, z_hi, z_lo, x):
    return (y * 2 + core) * N_CTX + z_hi * 4 + z_lo * 2 + x


def bits_of(i):
    return ((i >> 4) & 1, (i >> 3) & 1, (i >> 2) & 1, (i >> 1) & 1, i & 1)


def permutation(target, sends=lambda *bits: True):
    devices = range(N_GRP * N_CTX)
    return [(i, device_of(*target(*bits_of(i)))) for i in devices if sends(*bits_of(i))]


def member_device(e):
    def target(y, core, z_hi, z_lo, x):
        m = (z_hi * 4 + z_lo * 2 + x) ^ e
        return (y, m >> 2, core, (m >> 1) & 1, m & 1)

    return target


SPREAD = [permutation(member_device(e)) for e in range(8)]
COLLECT = [[(b, a) for a, b in pairs] for pairs in SPREAD]
HALVES = permutation(
    lambda y, core, z_hi, z_lo, x: (y, z_hi, core, z_lo, x),
    lambda y, core, z_hi, z_lo, x: z_hi != core,
)
CUBES = [
    [device_of(y, m >> 2, z_hi, (m >> 1) & 1, m & 1) for m in range(8)]
    for y in range(2)
    for z_hi in range(2)
]
OVER_Y = permutation(lambda y, core, z_hi, z_lo, x: (1 - y, core, z_hi, z_lo, x))
SIBLING = permutation(lambda y, core, z_hi, z_lo, x: (y, 1 - core, z_hi, z_lo, x))
MIDDLE = permutation(lambda y, core, z_hi, z_lo, x: (y, core, 1 - z_hi, z_lo, x))
MIDDLE_OUT = permutation(
    lambda y, core, z_hi, z_lo, x: (y, core, 1 - z_hi, z_lo, x),
    lambda y, core, z_hi, z_lo, x: z_hi == core,
)
MIDDLE_IN = permutation(
    lambda y, core, z_hi, z_lo, x: (y, core, 1 - z_hi, z_lo, x),
    lambda y, core, z_hi, z_lo, x: z_hi != core,
)
CHIP = [
    permutation(
        lambda y, core, z_hi, z_lo, x, t=t: (y, core, z_hi, z_lo ^ (t >> 1), x ^ (t & 1))
    )
    for t in range(4)
]


def permute(a, pairs):
    return lax.ppermute(a, AXES, pairs)


def pick(a, i, axis=0):
    return lax.dynamic_index_in_dim(a, i, axis, keepdims=False)


def added(*terms):
    return sum(t.astype(f32) for t in terms).astype(bf16)


def after(a, b):
    return lax.optimization_barrier((a, b))[0]


def together(*arrays):
    return lax.optimization_barrier(arrays)


def in_order(first, mine, other):
    return [jnp.where(first, mine, other), jnp.where(first, other, mine)]


def shards_split(
    tokens,
    block_table,
    norm1_gain,
    w_query,
    key_weight,
    value_weight,
    query_gain,
    key_norm_gain,
    w_out,
    norm2_gain,
    w_gate,
    w_up,
    w_down,
    out_grad,
):
    row_total, width = tokens.shape
    n_slots = row_total // BLK
    ff = w_gate.shape[1] // 8
    position = lax.axis_index("ctx").astype(jnp.int32)
    group_index = lax.axis_index("grp").astype(jnp.int32)
    y, core = group_index // 2, group_index % 2
    z_hi, chip = position // 4, position % 4
    z_lo, x = chip // 2, chip % 2
    member = core * 4 + chip
    info = jnp.stack([position, y, core, member, chip])
    at_home = z_hi == core
    qg, kg = query_gain.reshape(1, HEAD_SIZE), key_norm_gain.reshape(1, HEAD_SIZE)

    eight = jnp.arange(8, dtype=jnp.int32)
    five = jnp.arange(CHUNK, dtype=jnp.int32)[None, :]

    def slots_of(m):
        m = m.reshape(-1, 1)
        return jnp.where(five == 0, m, 7 + 7 * (m // 2) + 3 * (m % 2) + five)

    def held_at(natural, m):
        inside = natural - (PROMPT_BLOCKS + CONT_BLOCKS * m)
        valid = (five == 0) | ((inside >= 0) & (inside < CONT_BLOCKS))
        return jnp.where(valid, jnp.where(five == 0, natural - 8 * m, 8 + inside), n_slots), valid

    def look_up(rows, slots):
        match = slots[:, :, None] == jnp.arange(n_slots, dtype=jnp.int32)
        return jnp.sum(jnp.where(match, rows[:, None, :], 0), axis=2)

    tables = block_table.reshape(8, n_slots)
    send_slots = slots_of(position ^ eight)
    from_tables = jnp.concatenate(
        [lax.dynamic_slice_in_dim(tables, member ^ e, 1, 0) for e in range(8)], axis=0
    )
    arrive, _ = held_at(look_up(from_tables, jnp.broadcast_to(slots_of(member), (8, CHUNK))), member)
    leave = jnp.minimum(arrive, n_slots - 1)
    own_table = lax.dynamic_slice_in_dim(tables, position, 1, 0)
    _, valid = held_at(look_up(own_table, send_slots), (position ^ eight).reshape(-1, 1))
    home_slots = jnp.where(valid, send_slots, n_slots)

    def spread(a):
        return [permute(c, pairs) for c, pairs in zip(deal(send_slots, a), SPREAD)]

    def collect(a, kind):
        pieces = [permute(c, pairs) for c, pairs in zip(deal(leave, a), COLLECT)]
        return place(home_slots, pieces, row_total, kind)

    def regrouped(a):
        return jnp.where(at_home, a, permute(a, HALVES))

    def both(a):
        return jnp.concatenate([a, permute(a, SIBLING)], axis=0)

    def columns(w, parts):
        return pick(w.reshape(w.shape[0], 2, 4, -1), core, 1)

    own_one = jnp.concatenate(
        [
            columns(w_query, 2).reshape(-1, 1024),
            jnp.concatenate([columns(key_weight, 2), columns(value_weight, 2)], axis=2).reshape(
                -1, 1024
            ),
        ],
        axis=1,
    )
    own_two = jnp.concatenate([columns(w_gate, 2), columns(w_up, 2)], axis=2)
    own_two = pick(own_two.reshape(2, 64, 8 * ff), y)
    own_out, own_down = w_out, w_down

    def around(a):
        return [a] + [permute(a, CHIP[t]) for t in range(1, 4)]

    one = around(own_one)
    middle_one = permute(own_one, MIDDLE)
    arrived = spread(tokens)
    one = one + around(middle_one)

    cosine, sine = rotation(jnp.arange(PROMPT + CONT_LEN, dtype=jnp.int32))
    cos = jnp.concatenate([cosine[:, 0], cosine[:, 0]], axis=1)
    sin = jnp.concatenate([-sine[:, 0], sine[:, 0]], axis=1)

    def of_rows(table):
        parts = []
        for m in (member, member ^ 4):
            parts += [lax.dynamic_slice_in_dim(table, m * RUN, RUN, 0), table[PROMPT:]]
        return jnp.concatenate(parts, axis=0)

    cos, sin = of_rows(cos), of_rows(sin)

    inputs_low, first_low = place_norm(arrive, arrived, norm1_gain.reshape(1, width), row_total)
    hidden_one = both(first_low)
    own_two, own_three, out_grad = together(
        own_two, jnp.concatenate([w_down, w_out], axis=0), out_grad, first_low
    )[:3]
    middle_three = permute(own_three, MIDDLE_OUT)
    hidden_one, middle_three, own_two, out_grad, *one = together(
        hidden_one, middle_three, own_two, out_grad, *one
    )
    home_three = jnp.where(at_home, own_three, middle_three)
    home_down, home_out = home_three[: 3 * RUN], home_three[3 * RUN :]

    two = around(own_two)
    middle_two = permute(own_two, MIDDLE)
    kv, rawk, w_kv, prompt_kv = project(
        key_value_kernel, "key_value", info, hidden_one, one, 4, kg, cos, sin, HEAD_SIZE, 1
    )
    prompt_kv, home_out, out_grad, hidden_q, middle_two, *two = together(
        prompt_kv, home_out, out_grad, hidden_one, middle_two, *two
    )

    prompt = around(prompt_kv)
    outs = jnp.stack([home_out, permute(home_out, CHIP[2])])
    grad_here = regrouped(out_grad)
    q, rawq, w_q = project(query_kernel, "query", info, hidden_q, one, 0, qg, cos, sin, 256, 0)
    q, outs, grad_here, middle_two, home_down, *prompt = together(
        q, outs, grad_here, middle_two, home_down, *prompt
    )

    two += around(middle_two)
    other_two = [permute(jnp.stack(two[:4]), OVER_Y)]
    outs = [outs, permute(outs, CHIP[1])]
    mixed, lse = attn_fwd(info, q, kv, prompt)
    mixed, home_down, grad_here, *rest = together(mixed, home_down, grad_here, *two, *outs, *other_two)
    two, outs, other_two = rest[:8], rest[8:10], rest[10:]

    other_two.append(permute(jnp.stack(two[4:]), OVER_Y))
    downs = around(home_down)
    chunk_starts = [8 + 7 * (m // 2) + 3 * (m % 2) for m in range(8)]
    grad_here = jnp.concatenate(
        [
            grad_here[: 8 * BLK].reshape(8, BLK, width),
            jnp.stack([grad_here[start * BLK : (start + 4) * BLK] for start in chunk_starts]),
        ],
        axis=1,
    )

    def swap_cube(a):
        return lax.all_to_all(a, AXES, 0, 0, tiled=True, axis_index_groups=CUBES)

    grad_here = swap_cube(grad_here)
    in_turn = jnp.concatenate(
        [lax.dynamic_slice_in_dim(arrive, member ^ e, 1, 0) for e in range(8)], axis=0
    )
    leave_in_turn = jnp.minimum(in_turn, n_slots - 1)
    home_in_turn = jnp.concatenate(
        [lax.dynamic_slice_in_dim(home_slots, position ^ e, 1, 0) for e in range(8)], axis=0
    )

    rows_kind = ((row_total, width), f32), ((row_total, width), bf16)
    out_own, out_sib, w_o = whole_call(
        out_kernel,
        "out_projection",
        (info, mixed, *outs),
        [*rows_kind, ((1024, width), bf16)],
    )
    inputs = inputs_low.astype(f32)
    resid_one = inputs + out_own + permute(out_sib, SIBLING).astype(f32)
    normed_two, inverse_two = normed_parts(resid_one)
    hidden_two = (normed_two * norm2_gain).astype(bf16)
    hidden_two, other_far, *downs = together(hidden_two, other_two[1], *downs)
    other_two = [other_two[0], other_far]
    hidden_two = both(hidden_two)
    grad_low = place_all(in_turn, grad_here, row_total, bf16)
    grad_both = both(grad_low)
    hid, grad_gu, ff_own, ff_sib, back_own, back_sib = mlp(
        info, hidden_two, grad_both, two + other_two, downs, ff
    )
    grad_two = back_own + permute(back_sib, SIBLING).astype(f32)
    gain_two_part = jnp.sum(grad_two * normed_two, axis=0)
    grad_resid = grad_low.astype(f32) + norm_back(grad_two * norm2_gain, normed_two, inverse_two)
    grad_attn = both(grad_resid.astype(bf16))

    def chip_parts(grad):
        grad = grad.reshape(8, -1, grad.shape[-1])
        return [
            jnp.stack([pick(grad, position ^ t), pick(grad, position ^ (4 + t))]) for t in range(4)
        ]

    def sent_to_chips(parts):
        return [permute(parts[t], CHIP[t]) for t in range(1, 4)]

    def from_middle(part):
        return added(pick(part, z_hi), permute(pick(part, 1 - z_hi), MIDDLE))

    def halved(grad, axis, bit, pairs):
        return added(pick(grad, bit, axis), permute(pick(grad, 1 - bit, axis), pairs))

    grad_two_w = tn(hidden_two, grad_gu).astype(bf16).reshape(2, 2, 2, 2, 64, -1)
    keep_two, send_two = pick(grad_two_w, y, 3), pick(grad_two_w, 1 - y, 3)
    send_two = permute(send_two, OVER_Y)
    grad_down = tn(hid, grad_both).astype(bf16).reshape(2, 2, -1, width)
    grad_out = tn(mixed, grad_attn).astype(bf16).reshape(2, 2, -1, width)
    outcome = resid_one + ff_own + permute(ff_sib, SIBLING).astype(f32)
    leaving = deal_all(leave_in_turn, outcome.astype(bf16))
    grad_attn, grad_down, grad_out, leaving, _ = together(
        grad_attn, grad_down, grad_out, leaving, keep_two
    )
    keep_down, send_down = pick(grad_down, x, 1), permute(pick(grad_down, 1 - x, 1), CHIP[1])
    keep_out, send_out = pick(grad_out, z_lo), permute(pick(grad_out, 1 - z_lo), CHIP[2])
    leaving = swap_cube(leaving)
    grad_mixed = nt(grad_attn, w_o).astype(bf16)
    grad_q, grad_kv, *prompt_parts, gains = attn_bwd(
        info, q, kv, prompt, grad_mixed, mixed, lse, rawq, rawk, qg, kg, cos, sin
    )
    grad_q, grad_kv, send_down, send_out, leaving, *prompt_parts = together(
        grad_q, grad_kv, send_down, send_out, leaving, *prompt_parts
    )

    prompt_parts = [prompt_parts[0]] + [permute(prompt_parts[t], CHIP[t]) for t in range(1, 4)]
    grad_wq = tn(hidden_one, grad_q).astype(bf16).reshape(8, 2, 64, -1)
    keep_q, send_q = pick(grad_wq, y, 1), permute(pick(grad_wq, 1 - y, 1), OVER_Y)
    left = regrouped(leaving.reshape(-1, width))
    grad_q, keep_q, send_q, send_down, send_out, send_two, left, *prompt_parts = together(
        grad_q, keep_q, send_q, send_down, send_out, send_two, left, *prompt_parts
    )
    sum_two = added(keep_two, send_two)
    down, out = added(keep_down, send_down), added(keep_out, send_out)
    down = halved(down, 0, z_lo, CHIP[2])
    out = halved(out, 0, x, CHIP[1])
    sum_two = halved(sum_two, 2, x, CHIP[1])
    grad_kv, key_gains = whole_call(
        prompt_back_kernel,
        "prompt_back",
        (*prompt_parts, grad_kv, rawk, kg, cos, sin),
        [(grad_kv.shape, bf16), ((8, HEAD_SIZE), f32)],
    )
    grad_wkv = tn(hidden_one, grad_kv).astype(bf16).reshape(8, 2, 64, -1)
    grad_one = nt(grad_q, w_q) + nt(after(grad_kv, grad_wkv), w_kv)
    grad_one, sum_two = together(grad_one, sum_two)
    grad_one = grad_one[:row_total] + permute(
        grad_one[row_total:].astype(bf16), SIBLING
    ).astype(f32)
    normed_one, inverse_one = normed_parts(inputs)
    gain_one_part = jnp.sum(grad_one * normed_one, axis=0)
    grad_tokens = grad_resid + norm_back(grad_one * norm1_gain, normed_one, inverse_one)
    going = deal_all(leave_in_turn, grad_tokens.astype(bf16))
    gain_grads = jnp.concatenate(
        [gain_one_part, gain_two_part, gains[0], gains[1] + key_gains[0]]
    ).reshape(-1, HEAD_SIZE)
    going, gain_grads, down, out, keep_q, send_q, grad_wkv, left, sum_two = together(
        going, gain_grads, down, out, keep_q, send_q, grad_wkv, left, sum_two
    )
    going = swap_cube(going)
    q_parts = chip_parts(added(keep_q, send_q))
    q_sent = sent_to_chips(q_parts)
    keep_kv, send_kv = pick(grad_wkv, y, 1), permute(pick(grad_wkv, 1 - y, 1), OVER_Y)
    three = jnp.concatenate([down, out], axis=0)
    three = added(three, permute(three, MIDDLE_IN))
    gain_grads = gain_grads + permute(gain_grads, SIBLING)
    outcome = place_all(home_in_turn, left.reshape(8, -1, width), row_total, bf16)
    going, three, gain_grads, outcome, keep_kv, send_kv, sum_two, *q_sent = together(
        going, three, gain_grads, outcome, keep_kv, send_kv, sum_two, *q_sent
    )
    going = regrouped(going.reshape(-1, width))
    sum_two = halved(sum_two, 1, z_lo, CHIP[2])
    gain_grads = gain_grads + permute(gain_grads, CHIP[1])
    kv_parts = chip_parts(added(keep_kv, send_kv))
    kv_sent = sent_to_chips(kv_parts)
    part_q = added(q_parts[0], *q_sent)
    going, gain_grads, sum_two, *kv_sent = together(going, gain_grads, sum_two, *kv_sent)
    gain_grads = gain_grads + permute(gain_grads, CHIP[2])
    grad_tokens = place_all(home_in_turn, going.reshape(8, -1, width), row_total, f32)
    part_kv = added(kv_parts[0], *kv_sent)
    sum_one = jnp.concatenate([part_q, part_kv], axis=2)
    sum_one = added(sum_one[0], permute(sum_one[1], MIDDLE))
    three = added(three, permute(three, OVER_Y))
    sum_two = from_middle(sum_two)
    sum_one, sum_two, three, gain_grads = together(sum_one, sum_two, three, gain_grads)
    sum_two = jnp.concatenate(in_order(y == 0, sum_two, permute(sum_two, OVER_Y)), axis=0)
    gain_grads = gain_grads + permute(gain_grads, OVER_Y)
    sum_one = jnp.concatenate(in_order(y == 0, sum_one, permute(sum_one, OVER_Y)), axis=0)
    total = jnp.where(at_home, three, permute(three, SIBLING)).astype(f32)
    sum_one, sum_two, gain_grads = together(sum_one, sum_two, gain_grads)
    gain_grads = gain_grads + permute(gain_grads, MIDDLE)
    gate_up = jnp.stack(in_order(core == 0, sum_two, permute(sum_two, SIBLING)), axis=1)
    gate_up = gate_up.reshape(-1, 2, 4, 2, ff).astype(f32)
    one_halves = in_order(core == 0, sum_one, permute(sum_one, SIBLING))
    query_halves = [part[:, :1024] for part in one_halves]
    kv_halves = [part[:, 1024:] for part in one_halves]
    kv_grad = jnp.concatenate(kv_halves, axis=1).reshape(-1, 8, 2, HEAD_SIZE).astype(f32)

    gain_grads = gain_grads.reshape(-1)
    return (
        outcome,
        grad_tokens,
        gain_grads[:width],
        jnp.concatenate(query_halves, axis=1).astype(f32),
        kv_grad[:, :, 0].reshape(-1, 1024),
        kv_grad[:, :, 1].reshape(-1, 1024),
        gain_grads[2 * width : 2 * width + HEAD_SIZE],
        gain_grads[2 * width + HEAD_SIZE :],
        total[3 * RUN :],
        gain_grads[width : 2 * width],
        gate_up[:, :, :, 0].reshape(-1, 8 * ff),
        gate_up[:, :, :, 1].reshape(-1, 8 * ff),
        total[: 3 * RUN],
    )


def solution(mesh):
    split = mesh.shape["grp"] == N_GRP and mesh.shape["ctx"] == N_CTX
    return jax.shard_map(
        shards_split if split else shards,
        mesh=mesh,
        in_specs=(
            P(("grp", "ctx"), None),
            P(),
            P(),
            P("ctx", None),
            P("ctx", None),
            P("ctx", None),
            P(),
            P(),
            P("ctx", None),
            P(),
            P("ctx", None),
            P("ctx", None),
            P("ctx", None),
            P(("grp", "ctx"), None),
        ),
        out_specs=(
            P(("grp", "ctx"), None),
            P(("grp", "ctx"), None),
            P(),
            P("ctx", None),
            P("ctx", None),
            P("ctx", None),
            P(),
            P(),
            P("ctx", None),
            P(),
            P("ctx", None),
            P("ctx", None),
            P("ctx", None),
        ),
        check_vma=False,
    )
```

```python
import math

import jax
import jax.numpy as jnp
from jax import lax
from jax.experimental import pallas as pl
from jax.experimental.pallas import tpu as pltpu
from jax.sharding import PartitionSpec as P

QUERY_HEADS = 16
KEY_VALUE_HEADS = 8
HEAD_SIZE = 128
PROMPT = 1024
CONT_LEN = 448
BLK = 16


eps = 1e-06
theta = 1000000.0
key_span = 512
masked_score = -1e30


def normed_parts(value_rows):
    inverse = lax.rsqrt(jnp.mean(value_rows * value_rows, axis=-1, keepdims=True) + eps)
    return (value_rows * inverse, inverse)


def norm_back(grad_normed, normed, inverse):
    return inverse * (grad_normed - normed * jnp.mean(grad_normed * normed, axis=-1, keepdims=True))


def layout(block_table, slot_ids):
    natural = block_table[slot_ids // BLK] * BLK + slot_ids % BLK
    beyond = natural - PROMPT
    segment = jnp.where(natural < PROMPT, 0, 1 + beyond // CONT_LEN)
    places = jnp.where(natural < PROMPT, natural, PROMPT + beyond % CONT_LEN)
    return (natural, segment, places)


def rotation(places):
    half_dim = HEAD_SIZE // 2
    frequency = jnp.exp(
        jnp.arange(half_dim, dtype=jnp.float32) * (-2.0 * math.log(theta) / HEAD_SIZE)
    )
    angles = places.astype(jnp.float32)[:, None] * frequency[None, :]
    return (jnp.cos(angles)[:, None, :], jnp.sin(angles)[:, None, :])


def apply_rotation(value_rows, cosine_table, sine_table):
    half_dim = value_rows.shape[-1] // 2
    first_half = value_rows[..., :half_dim]
    second_half = value_rows[..., half_dim:]
    return jnp.concatenate(
        [
            first_half * cosine_table - second_half * sine_table,
            second_half * cosine_table + first_half * sine_table,
        ],
        axis=-1,
    )


def rotate_back(value_rows, cosine_table, sine_table):
    half_dim = value_rows.shape[-1] // 2
    first_half = value_rows[..., :half_dim]
    second_half = value_rows[..., half_dim:]
    return jnp.concatenate(
        [
            first_half * cosine_table + second_half * sine_table,
            second_half * cosine_table - first_half * sine_table,
        ],
        axis=-1,
    )


def allowed_mask(own_nat, own_seg, key_nat, key_seg):
    return (key_nat[None, :] <= own_nat[:, None]) & (
        (key_seg[None, :] == 0) | (key_seg[None, :] == own_seg[:, None])
    )


def span_of():
    return key_span


def over_blocks(advance, running, length):
    block_span_width = span_of()

    def scan_step(inner_state, key_first):
        return (advance(inner_state, key_first, block_span_width), None)

    running, ignored = lax.scan(
        scan_step,
        running,
        jnp.arange(length // block_span_width, dtype=jnp.int32) * block_span_width,
    )
    return running


def attend_block(running, query_head_rows, keys_part, values_part, allowed, softmax_scale):
    row_max, row_sum, accum = running
    raw_scores = (
        jnp.einsum("grtd,ngd->grtn", query_head_rows, keys_part, preferred_element_type=jnp.float32)
        * softmax_scale
    )
    scores = jnp.where(allowed, raw_scores, masked_score)
    new_max = jnp.maximum(row_max, jnp.max(scores, axis=-1))
    rescale = jnp.exp(row_max - new_max)
    weights = jnp.exp(scores - new_max[..., None])
    row_sum = row_sum * rescale + jnp.sum(weights, axis=-1)
    accum = accum * rescale[..., None] + jnp.einsum(
        "grtn,ngd->grtd",
        weights.astype(jnp.bfloat16),
        values_part,
        preferred_element_type=jnp.float32,
    )
    return (new_max, row_sum, accum)


def key_terms(
    grad_scores, weights, query_head_rows, scaled_high, scaled_rest, softmax_scale, block_span_width
):
    grad_keys = (
        jnp.einsum(
            "grtn,grtd->ngd", grad_scores, query_head_rows, preferred_element_type=jnp.float32
        )
        * softmax_scale
    )
    weights_low = weights.astype(jnp.bfloat16)
    grad_values = jnp.einsum(
        "grtn,grtd->ngd", weights_low, scaled_high, preferred_element_type=jnp.float32
    )
    grad_values = grad_values + jnp.einsum(
        "grtn,grtd->ngd", weights_low, scaled_rest, preferred_element_type=jnp.float32
    )
    return jnp.stack(
        [grad_keys.reshape(block_span_width, -1), grad_values.reshape(block_span_width, -1)], axis=1
    )


def shards(
    tokens,
    block_table,
    norm1_gain,
    w_query,
    key_weight,
    value_weight,
    query_gain,
    key_norm_gain,
    w_out,
    norm2_gain,
    w_gate,
    w_up,
    w_down,
    out_grad,
):
    row_total = tokens.shape[0]
    group_length = block_table.shape[0] * BLK
    sharing_count = QUERY_HEADS // KEY_VALUE_HEADS
    softmax_scale = 1.0 / math.sqrt(HEAD_SIZE)
    position = lax.axis_index("ctx")
    all_nat, all_seg, all_places = layout(block_table, jnp.arange(group_length, dtype=jnp.int32))
    own_slots = position * row_total + jnp.arange(row_total, dtype=jnp.int32)
    own_nat, own_seg, own_places = layout(block_table, own_slots)
    cosine_table, sine_table = rotation(own_places)
    query_full, key_full, value_full, out_full = (
        lax.all_gather(w_query, "ctx", axis=0, tiled=True),
        lax.all_gather(key_weight, "ctx", axis=0, tiled=True),
        lax.all_gather(value_weight, "ctx", axis=0, tiled=True),
        lax.all_gather(w_out, "ctx", axis=0, tiled=True),
    )
    inputs = tokens.astype(jnp.float32)
    normed_one, inverse_one = normed_parts(inputs)
    first_hidden = (normed_one * norm1_gain).astype(jnp.bfloat16)
    query_raw = jnp.dot(first_hidden, query_full, preferred_element_type=jnp.float32).reshape(
        row_total, QUERY_HEADS, HEAD_SIZE
    )
    unnormalized_keys = jnp.dot(first_hidden, key_full, preferred_element_type=jnp.float32).reshape(
        row_total, KEY_VALUE_HEADS, HEAD_SIZE
    )
    reduced_value = jnp.dot(first_hidden, value_full, preferred_element_type=jnp.float32).astype(
        jnp.bfloat16
    )
    query_normed, query_inverse = normed_parts(query_raw)
    normalized_keys, key_inverse = normed_parts(unnormalized_keys)
    reduced_query = apply_rotation(query_normed * query_gain, cosine_table, sine_table).astype(
        jnp.bfloat16
    )
    key_low = (
        apply_rotation(normalized_keys * key_norm_gain, cosine_table, sine_table)
        .astype(jnp.bfloat16)
        .reshape(row_total, KEY_VALUE_HEADS * HEAD_SIZE)
    )
    query_head_rows = jnp.transpose(
        reduced_query.reshape(row_total, KEY_VALUE_HEADS, sharing_count, HEAD_SIZE), (1, 2, 0, 3)
    )

    def attend(running, pieces):
        piece_keys, piece_values = pieces

        def advance(inner_state, key_first, block_span_width):
            keys_part = lax.dynamic_slice_in_dim(
                piece_keys, key_first, block_span_width, 0
            ).reshape(block_span_width, KEY_VALUE_HEADS, HEAD_SIZE)
            values_part = lax.dynamic_slice_in_dim(
                piece_values, key_first, block_span_width, 0
            ).reshape(block_span_width, KEY_VALUE_HEADS, HEAD_SIZE)
            key_nat = lax.dynamic_slice_in_dim(all_nat, key_first, block_span_width)
            key_seg = lax.dynamic_slice_in_dim(all_seg, key_first, block_span_width)
            allowed = allowed_mask(own_nat, own_seg, key_nat, key_seg)
            return attend_block(
                inner_state, query_head_rows, keys_part, values_part, allowed, softmax_scale
            )

        return over_blocks(advance, running, piece_keys.shape[0])

    statistic_shape = (KEY_VALUE_HEADS, sharing_count, row_total)
    initial = (
        jnp.full(statistic_shape, masked_score, jnp.float32),
        jnp.zeros(statistic_shape, jnp.float32),
        jnp.zeros(statistic_shape + (HEAD_SIZE,), jnp.float32),
    )
    row_max, row_sum, accum = attend(
        initial,
        (
            lax.all_gather(key_low, "ctx", axis=0, tiled=True),
            lax.all_gather(reduced_value, "ctx", axis=0, tiled=True),
        ),
    )
    mixed_heads = accum / row_sum[..., None]
    flat_low = (
        jnp.transpose(mixed_heads, (2, 0, 1, 3))
        .reshape(row_total, QUERY_HEADS * HEAD_SIZE)
        .astype(jnp.bfloat16)
    )
    resid_one = inputs + jnp.dot(flat_low, out_full, preferred_element_type=jnp.float32)
    gate_full, up_full, down_full = (
        lax.all_gather(w_gate, "ctx", axis=0, tiled=True),
        lax.all_gather(w_up, "ctx", axis=0, tiled=True),
        lax.all_gather(w_down, "ctx", axis=0, tiled=True),
    )
    normed_two, inverse_two = normed_parts(resid_one)
    hidden_two = (normed_two * norm2_gain).astype(jnp.bfloat16)
    gate_proj = jnp.dot(hidden_two, gate_full, preferred_element_type=jnp.float32)
    up_proj = jnp.dot(hidden_two, up_full, preferred_element_type=jnp.float32)
    gate_sigmoid = jax.nn.sigmoid(gate_proj)
    gate_silu = gate_proj * gate_sigmoid
    hidden_low = (gate_silu * up_proj).astype(jnp.bfloat16)
    outcome = resid_one + jnp.dot(hidden_low, down_full, preferred_element_type=jnp.float32)
    gate_full, up_full, down_full = (
        lax.all_gather(w_gate, "ctx", axis=0, tiled=True),
        lax.all_gather(w_up, "ctx", axis=0, tiled=True),
        lax.all_gather(w_down, "ctx", axis=0, tiled=True),
    )
    grad_out = out_grad.astype(jnp.float32)
    grad_down = jnp.einsum("tf,td->fd", hidden_low, out_grad, preferred_element_type=jnp.float32)
    grad_hidden = jnp.einsum("td,fd->tf", out_grad, down_full, preferred_element_type=jnp.float32)
    grad_gate = (
        grad_hidden * up_proj * gate_sigmoid * (1.0 + gate_proj * (1.0 - gate_sigmoid))
    ).astype(jnp.bfloat16)
    grad_up = (grad_hidden * gate_silu).astype(jnp.bfloat16)
    grad_wgate = jnp.einsum("tk,tf->kf", hidden_two, grad_gate, preferred_element_type=jnp.float32)
    grad_wup = jnp.einsum("tk,tf->kf", hidden_two, grad_up, preferred_element_type=jnp.float32)
    grad_two = jnp.einsum(
        "tf,kf->tk", grad_gate, gate_full, preferred_element_type=jnp.float32
    ) + jnp.einsum("tf,kf->tk", grad_up, up_full, preferred_element_type=jnp.float32)
    gain_two_part = jnp.sum(grad_two * normed_two, axis=0)
    grad_resid = grad_out + norm_back(grad_two * norm2_gain, normed_two, inverse_two)
    grad_attn = grad_resid.astype(jnp.bfloat16)
    query_full, key_full, value_full, out_full = (
        lax.all_gather(w_query, "ctx", axis=0, tiled=True),
        lax.all_gather(key_weight, "ctx", axis=0, tiled=True),
        lax.all_gather(value_weight, "ctx", axis=0, tiled=True),
        lax.all_gather(w_out, "ctx", axis=0, tiled=True),
    )
    keys_all, values_all = (
        lax.all_gather(key_low, "ctx", axis=0, tiled=True),
        lax.all_gather(reduced_value, "ctx", axis=0, tiled=True),
    )
    grad_wout = jnp.einsum("tk,td->kd", flat_low, grad_attn, preferred_element_type=jnp.float32)
    flattened_grad = jnp.einsum(
        "td,kd->tk", grad_attn, out_full, preferred_element_type=jnp.float32
    ).astype(jnp.bfloat16)
    head_grads = jnp.transpose(
        flattened_grad.reshape(row_total, KEY_VALUE_HEADS, sharing_count, HEAD_SIZE), (1, 2, 0, 3)
    )
    grad_heads_wide = head_grads.astype(jnp.float32)
    row_delta = jnp.sum(grad_heads_wide * mixed_heads, axis=-1)
    scaled_grad = grad_heads_wide / row_sum[..., None]
    scaled_high = scaled_grad.astype(jnp.bfloat16)
    scaled_rest = (scaled_grad - scaled_high.astype(jnp.float32)).astype(jnp.bfloat16)

    def block_back(key_first, block_span_width):
        keys_part = lax.dynamic_slice_in_dim(keys_all, key_first, block_span_width, 0).reshape(
            block_span_width, KEY_VALUE_HEADS, HEAD_SIZE
        )
        values_part = lax.dynamic_slice_in_dim(values_all, key_first, block_span_width, 0).reshape(
            block_span_width, KEY_VALUE_HEADS, HEAD_SIZE
        )
        key_nat = lax.dynamic_slice_in_dim(all_nat, key_first, block_span_width)
        key_seg = lax.dynamic_slice_in_dim(all_seg, key_first, block_span_width)
        allowed = allowed_mask(own_nat, own_seg, key_nat, key_seg)
        raw_scores = (
            jnp.einsum(
                "grtd,ngd->grtn", query_head_rows, keys_part, preferred_element_type=jnp.float32
            )
            * softmax_scale
        )
        scores = jnp.where(allowed, raw_scores, masked_score)
        weights = jnp.exp(scores - row_max[..., None])
        grad_prob = jnp.einsum(
            "grtd,ngd->grtn", head_grads, values_part, preferred_element_type=jnp.float32
        )
        grad_scores = (weights * (grad_prob - row_delta[..., None]) / row_sum[..., None]).astype(
            jnp.bfloat16
        )
        return (keys_part, grad_scores, weights)

    empty_query = jnp.zeros((KEY_VALUE_HEADS, sharing_count, row_total, HEAD_SIZE), jnp.float32)
    span_back = span_of()

    def pass_step(grad_query, key_first):
        keys_part, grad_scores, weights = block_back(key_first, span_back)
        grad_query = grad_query + jnp.einsum(
            "grtn,ngd->grtd", grad_scores, keys_part, preferred_element_type=jnp.float32
        )
        return (
            grad_query,
            key_terms(
                grad_scores,
                weights,
                query_head_rows,
                scaled_high,
                scaled_rest,
                softmax_scale,
                span_back,
            ),
        )

    grad_query, key_gradient_parts = lax.scan(
        pass_step, empty_query, jnp.arange(group_length // span_back, dtype=jnp.int32) * span_back
    )
    self_terms = lax.psum_scatter(
        key_gradient_parts.reshape(group_length, 2, KEY_VALUE_HEADS * HEAD_SIZE).astype(
            jnp.bfloat16
        ),
        "ctx",
        scatter_dimension=0,
        tiled=True,
    ).astype(jnp.float32)
    grad_query_rows = jnp.transpose(grad_query * softmax_scale, (2, 0, 1, 3)).reshape(
        row_total, QUERY_HEADS, HEAD_SIZE
    )
    grad_query_normed = rotate_back(grad_query_rows, cosine_table, sine_table)
    gain_query_part = jnp.sum(grad_query_normed * query_normed, axis=(0, 1))
    grad_query_raw = (
        norm_back(grad_query_normed * query_gain, query_normed, query_inverse)
        .reshape(row_total, QUERY_HEADS * HEAD_SIZE)
        .astype(jnp.bfloat16)
    )
    key_row_grads = self_terms[:, 0, :].reshape(row_total, KEY_VALUE_HEADS, HEAD_SIZE)
    grad_key_normed = rotate_back(key_row_grads, cosine_table, sine_table)
    gain_key_part = jnp.sum(grad_key_normed * normalized_keys, axis=(0, 1))
    grad_key_raw = (
        norm_back(grad_key_normed * key_norm_gain, normalized_keys, key_inverse)
        .reshape(row_total, KEY_VALUE_HEADS * HEAD_SIZE)
        .astype(jnp.bfloat16)
    )
    grad_value_low = self_terms[:, 1, :].astype(jnp.bfloat16)
    grad_wquery = jnp.einsum(
        "tk,tq->kq", first_hidden, grad_query_raw, preferred_element_type=jnp.float32
    )
    grad_wkey = jnp.einsum(
        "tk,tq->kq", first_hidden, grad_key_raw, preferred_element_type=jnp.float32
    )
    grad_wvalue = jnp.einsum(
        "tk,tq->kq", first_hidden, grad_value_low, preferred_element_type=jnp.float32
    )
    grad_one = jnp.einsum(
        "tq,kq->tk", grad_query_raw, query_full, preferred_element_type=jnp.float32
    )
    grad_one = grad_one + jnp.einsum(
        "tq,kq->tk", grad_key_raw, key_full, preferred_element_type=jnp.float32
    )
    grad_one = grad_one + jnp.einsum(
        "tq,kq->tk", grad_value_low, value_full, preferred_element_type=jnp.float32
    )
    gain_one_part = jnp.sum(grad_one * normed_one, axis=0)
    grad_tokens = grad_resid + norm_back(grad_one * norm1_gain, normed_one, inverse_one)
    shard_grads = (
        lax.psum_scatter(
            grad_wquery.astype(jnp.bfloat16), "ctx", scatter_dimension=0, tiled=True
        ).astype(jnp.float32),
        lax.psum_scatter(
            grad_wkey.astype(jnp.bfloat16), "ctx", scatter_dimension=0, tiled=True
        ).astype(jnp.float32),
        lax.psum_scatter(
            grad_wvalue.astype(jnp.bfloat16), "ctx", scatter_dimension=0, tiled=True
        ).astype(jnp.float32),
        lax.psum_scatter(
            grad_wout.astype(jnp.bfloat16), "ctx", scatter_dimension=0, tiled=True
        ).astype(jnp.float32),
        lax.psum_scatter(
            grad_wgate.astype(jnp.bfloat16), "ctx", scatter_dimension=0, tiled=True
        ).astype(jnp.float32),
        lax.psum_scatter(
            grad_wup.astype(jnp.bfloat16), "ctx", scatter_dimension=0, tiled=True
        ).astype(jnp.float32),
        lax.psum_scatter(
            grad_down.astype(jnp.bfloat16), "ctx", scatter_dimension=0, tiled=True
        ).astype(jnp.float32),
    )
    shard_grads = (
        lax.psum(shard_grads[0].astype(jnp.bfloat16), "grp").astype(jnp.float32),
        lax.psum(shard_grads[1].astype(jnp.bfloat16), "grp").astype(jnp.float32),
        lax.psum(shard_grads[2].astype(jnp.bfloat16), "grp").astype(jnp.float32),
        lax.psum(shard_grads[3].astype(jnp.bfloat16), "grp").astype(jnp.float32),
        lax.psum(shard_grads[4].astype(jnp.bfloat16), "grp").astype(jnp.float32),
        lax.psum(shard_grads[5].astype(jnp.bfloat16), "grp").astype(jnp.float32),
        lax.psum(shard_grads[6].astype(jnp.bfloat16), "grp").astype(jnp.float32),
    )
    gain_grads = lax.psum(
        (gain_one_part, gain_query_part, gain_key_part, gain_two_part), ("grp", "ctx")
    )
    return (
        outcome.astype(jnp.bfloat16),
        grad_tokens,
        gain_grads[0],
        shard_grads[0],
        shard_grads[1],
        shard_grads[2],
        gain_grads[1],
        gain_grads[2],
        shard_grads[3],
        gain_grads[3],
        shard_grads[4],
        shard_grads[5],
        shard_grads[6],
    )


f32 = jnp.float32
bf16 = jnp.bfloat16
AXES = ("grp", "ctx")
N_GRP = 4
N_CTX = 8
SCALE = 1.0 / math.sqrt(HEAD_SIZE)
EXP2_SCALE = math.log2(math.e) / math.sqrt(HEAD_SIZE)
VMEM_LIMIT = 60 * 1024 * 1024
RUN = 8 * BLK
PROMPT_BLOCKS = PROMPT // BLK
CONT_BLOCKS = CONT_LEN // BLK
CHUNK = 5
HELD = RUN + CONT_LEN


def nt(a, b):
    return lax.dot_general(a, b, (((1,), (1,)), ((), ())), preferred_element_type=f32)


def nn(a, b):
    return jnp.dot(a, b, preferred_element_type=f32)


def tn(a, b):
    return lax.dot_general(a, b, (((0,), (0,)), ((), ())), preferred_element_type=f32)


def rows_at(start, size):
    return pl.ds(pl.multiple_of(start, size), size)


def turned(u):
    return pltpu.roll(u, HEAD_SIZE // 2, 1)


def head(i):
    return slice(i * HEAD_SIZE, (i + 1) * HEAD_SIZE)


def params():
    return pltpu.CompilerParams(vmem_limit_bytes=VMEM_LIMIT)


def whole_call(kernel, name, args, outs, scratch=()):
    smem = pl.BlockSpec(memory_space=pltpu.SMEM)
    vmem = pl.BlockSpec(memory_space=pltpu.VMEM)
    return pl.pallas_call(
        kernel,
        in_specs=[smem if a.dtype == jnp.int32 else vmem for a in args],
        out_specs=[vmem] * len(outs),
        out_shape=[jax.ShapeDtypeStruct(s, t) for s, t in outs],
        scratch_shapes=list(scratch),
        compiler_params=params(),
        name=name,
    )(*args)


def deal_kernel(table, rows_ref, *outs):
    for e in range(8):
        for i in range(CHUNK):
            outs[e][i * BLK : (i + 1) * BLK, :] = rows_ref[rows_at(table[e, i] * BLK, BLK), :]


def deal(table, rows):
    shape = (CHUNK * BLK, rows.shape[1])
    return whole_call(deal_kernel, "deal_rows", (table, rows), [(shape, rows.dtype)] * 8)


def deal_all_kernel(table, rows_ref, out_ref):
    for e in range(8):
        for i in range(CHUNK):
            out_ref[e, i * BLK : (i + 1) * BLK, :] = rows_ref[rows_at(table[e, i] * BLK, BLK), :]


def deal_all(table, rows):
    shape = (8, CHUNK * BLK, rows.shape[1])
    return whole_call(deal_all_kernel, "deal_all", (table, rows), [(shape, rows.dtype)])[0]


def place_all_kernel(table, pieces, out_ref, held):
    for e in range(8):
        for i in range(CHUNK):
            held[rows_at(table[e, i] * BLK, BLK), :] = pieces[e, i * BLK : (i + 1) * BLK, :]
    out_ref[...] = held[: out_ref.shape[0], :].astype(out_ref.dtype)


def place_all(table, pieces, n_rows, kind):
    shape = (n_rows, pieces.shape[2])
    return whole_call(
        place_all_kernel,
        "place_all",
        (table, pieces),
        [(shape, kind)],
        [pltpu.VMEM((n_rows + BLK, shape[1]), pieces.dtype)],
    )[0]


def place_kernel(table, *refs):
    pieces, out_ref, held = refs[:8], refs[8], refs[-1]
    for e in range(8):
        for i in range(CHUNK):
            held[rows_at(table[e, i] * BLK, BLK), :] = pieces[e][i * BLK : (i + 1) * BLK, :]
    out_ref[...] = held[: out_ref.shape[0], :].astype(out_ref.dtype)


def place(table, pieces, n_rows, kind):
    shape = (n_rows, pieces[0].shape[1])
    return whole_call(
        place_kernel,
        "place_rows",
        (table, *pieces),
        [(shape, kind)],
        [pltpu.VMEM((n_rows + BLK, shape[1]), pieces[0].dtype)],
    )[0]


def place_norm_kernel(table, *refs):
    gain_ref, out_ref, low_ref, held = refs[8:]
    place_kernel(table, *refs[:8], out_ref, held)
    normed, _ = normed_parts(out_ref[...].astype(f32))
    low_ref[...] = (normed * gain_ref[...]).astype(bf16)


def place_norm(table, pieces, gain, n_rows):
    shape = (n_rows, pieces[0].shape[1])
    return whole_call(
        place_norm_kernel,
        "place_rows_norm",
        (table, *pieces, gain),
        [(shape, bf16), (shape, bf16)],
        [pltpu.VMEM((n_rows + BLK, shape[1]), bf16)],
    )


def gathered_rows(info, pieces, w_ref):
    for e in range(8):
        w_ref[rows_at((info[0] ^ e) * 128, 128), :] = pieces[e][...]


def lane_mean(u):
    ones = jnp.full((HEAD_SIZE, HEAD_SIZE), 1.0 / HEAD_SIZE, bf16)
    high = u.astype(bf16)
    return nn(high, ones) + nn((u - high.astype(f32)).astype(bf16), ones)


def head_normed(u):
    inverse = lax.rsqrt(lane_mean(u * u) + eps)
    return u * inverse, inverse


def query_kernel(info, h_ref, *refs):
    gain_ref, cos_ref, sin_ref, q_ref, raw_ref, w_ref = refs[8:]
    gathered_rows(info, refs[:8], w_ref)
    acc = nn(h_ref[...], w_ref[...])
    raw_ref[...] = acc
    for i in range(2):
        normed, _ = head_normed(acc[:, head(i)])
        u = normed * gain_ref[...]
        q_ref[:, head(i)] = (u * cos_ref[...] + turned(u) * sin_ref[...]).astype(bf16)


def key_value_kernel(info, h_ref, *refs):
    gain_ref, cos_ref, sin_ref, kv_ref, raw_ref, w_ref, send_ref = refs[8:]
    gathered_rows(info, refs[:8], w_ref)
    acc = nn(h_ref[...], w_ref[...])
    raw_ref[...] = acc[:, head(0)]
    normed, _ = head_normed(acc[:, head(0)])
    u = normed * gain_ref[...]
    kv_ref[:, head(0)] = (u * cos_ref[...] + turned(u) * sin_ref[...]).astype(bf16)
    kv_ref[:, head(1)] = acc[:, head(1)].astype(bf16)
    for b in range(2):
        send_ref[b * RUN : (b + 1) * RUN, :] = kv_ref[b * HELD : b * HELD + RUN, :]


def project(kernel, name, info, hidden, pieces, first, gain, cos, sin, raw_width, extra):
    rows, width = hidden.shape

    def still(g, s):
        return (0, 0)

    def moving(g, s):
        return (0, g)

    return pl.pallas_call(
        kernel,
        grid_spec=pltpu.PrefetchScalarGridSpec(
            num_scalar_prefetch=1,
            grid=(4,),
            in_specs=[pl.BlockSpec((rows, width), still)]
            + [pl.BlockSpec((128, 256), lambda g, s: (0, g + first))] * 8
            + [
                pl.BlockSpec((1, HEAD_SIZE), still),
                pl.BlockSpec((rows, HEAD_SIZE), still),
                pl.BlockSpec((rows, HEAD_SIZE), still),
            ],
            out_specs=[
                pl.BlockSpec((rows, 256), moving),
                pl.BlockSpec((rows, raw_width), moving),
                pl.BlockSpec((width, 256), moving),
            ]
            + [pl.BlockSpec((2 * RUN, 256), moving)] * extra,
        ),
        out_shape=[
            jax.ShapeDtypeStruct((rows, 1024), bf16),
            jax.ShapeDtypeStruct((rows, 4 * raw_width), f32),
            jax.ShapeDtypeStruct((width, 1024), bf16),
        ]
        + [jax.ShapeDtypeStruct((2 * RUN, 1024), bf16)] * extra,
        compiler_params=params(),
        name=name,
    )(info, hidden, *pieces, gain, cos, sin)


def seen_in_prompt(info, half):
    key = lax.broadcasted_iota(jnp.int32, (PROMPT, RUN), 0)
    tile = key // RUN
    run = info[3] ^ (tile // 2 + 4 * (tile % 2))
    row = lax.broadcasted_iota(jnp.int32, (PROMPT, RUN), 1) + (info[3] ^ (4 * half)) * RUN
    return run * RUN + key % RUN <= row


def seen_in_own():
    key = lax.broadcasted_iota(jnp.int32, (CONT_LEN, CONT_LEN), 0)
    row = lax.broadcasted_iota(jnp.int32, (CONT_LEN, CONT_LEN), 1)
    return key <= row


LSE_SPAN = 640


def units():
    for b in range(2):
        yield b, b * HELD + RUN, CONT_LEN, b * LSE_SPAN, False
    for b in range(2):
        yield b, b * HELD, RUN, b * LSE_SPAN + 512, True


def attn_fwd_kernel(info, q_ref, kv_ref, p0, p1, p2, p3, o_ref, lse_ref, p_ref):
    for t, p in enumerate((p0, p1, p2, p3)):
        p_ref[t * 2 * RUN : (t + 1) * 2 * RUN, :] = p[...]
    prompt = (p_ref[:, head(0)], jnp.transpose(p_ref[:, head(1)]))
    for b, row0, n, lane, in_prompt in units():
        own = slice(row0, row0 + n)
        tiles = [(*prompt, seen_in_prompt(info, b) if in_prompt else None)]
        if not in_prompt:
            tiles.append((kv_ref[own, head(0)], jnp.transpose(kv_ref[own, head(1)]), seen_in_own()))
        for i in range(2):
            q = q_ref[own, head(i)]
            total = jnp.zeros((1, n), f32)
            mixed = jnp.zeros((HEAD_SIZE, n), f32)
            for keys, values_t, seen in tiles:
                p = jnp.exp2(nt(keys, q) * EXP2_SCALE)
                if seen is not None:
                    p = jnp.where(seen, p, 0.0)
                total = total + jnp.sum(p, axis=0, keepdims=True)
                mixed = mixed + nn(values_t, p.astype(bf16))
            o_ref[own, head(i)] = jnp.transpose(mixed / total).astype(bf16)
            lse_ref[0, i : i + 1, lane : lane + n] = jnp.log2(total)


def attn_specs(rows, *names):
    specs = {
        "wide": pl.BlockSpec((rows, 256), lambda g, s: (0, g)),
        "head": pl.BlockSpec((rows, HEAD_SIZE), lambda g, s: (0, g)),
        "prompt": pl.BlockSpec((2 * RUN, 256), lambda g, s: (0, g)),
        "lse": pl.BlockSpec((1, 8, 2 * LSE_SPAN), lambda g, s: (g, 0, 0)),
        "table": pl.BlockSpec((rows, HEAD_SIZE), lambda g, s: (0, 0)),
        "gain": pl.BlockSpec((1, HEAD_SIZE), lambda g, s: (0, 0)),
        "gains": pl.BlockSpec((8, HEAD_SIZE), lambda g, s: (0, 0)),
    }
    return [specs[n] for n in names]


def attn_fwd(info, q, kv, prompt):
    rows = q.shape[0]
    return pl.pallas_call(
        attn_fwd_kernel,
        grid_spec=pltpu.PrefetchScalarGridSpec(
            num_scalar_prefetch=1,
            grid=(4,),
            in_specs=attn_specs(rows, "wide", "wide", *["prompt"] * 4),
            out_specs=attn_specs(rows, "wide", "lse"),
            scratch_shapes=[pltpu.VMEM((PROMPT, 256), bf16)],
        ),
        out_shape=[
            jax.ShapeDtypeStruct((rows, 1024), bf16),
            jax.ShapeDtypeStruct((4, 8, 2 * LSE_SPAN), f32),
        ],
        compiler_params=params(),
        cost_estimate=pl.CostEstimate(flops=20*10**9, bytes_accessed=10**7, transcendentals=0),
        name="attn_fwd",
    )(info, q, kv, *prompt)


def key_back(grad, raw, cos, sin, gain):
    normed, inverse = normed_parts(raw)
    grad = grad * SCALE
    back = grad * cos - turned(grad) * sin
    part = jnp.sum(back * normed, axis=0, keepdims=True)
    return norm_back(back * gain, normed, inverse).astype(bf16), part


def attn_bwd_kernel(info, q_ref, kv_ref, p0, p1, p2, p3, *refs):
    do_ref, o_ref, lse_ref, rawq_ref, rawk_ref, qg_ref, kg_ref, cos_ref, sin_ref = refs[:9]
    dq_ref, dkv_ref, d0, d1, d2, d3, gains_ref, dk_ref, dv_ref, p_ref = refs[9:]
    for t, p in enumerate((p0, p1, p2, p3)):
        p_ref[t * 2 * RUN : (t + 1) * 2 * RUN, :] = p[...]
    prompt = (p_ref[:, head(0)], jnp.transpose(p_ref[:, head(0)]), p_ref[:, head(1)])

    @pl.when(pl.program_id(0) == 0)
    def first():
        gains_ref[...] = jnp.zeros_like(gains_ref)

    for number, (b, row0, n, lane, in_prompt) in enumerate(units()):
        own = slice(row0, row0 + n)
        cos, sin = cos_ref[own, :], sin_ref[own, :]
        tiles = [(*prompt, seen_in_prompt(info, b) if in_prompt else None, True)]
        if not in_prompt:
            keys = kv_ref[own, head(0)]
            tiles.append((keys, jnp.transpose(keys), kv_ref[own, head(1)], seen_in_own(), False))
        own_dk = own_dv = 0.0
        for i in range(2):
            q, do = q_ref[own, head(i)], do_ref[own, head(i)]
            lse = lse_ref[0, i : i + 1, lane : lane + n]
            product = do.astype(f32) * o_ref[own, head(i)].astype(f32)
            delta = jnp.sum(jnp.transpose(product), axis=0, keepdims=True)
            dq = jnp.zeros((HEAD_SIZE, n), f32)
            for keys, keys_t, values, seen, shared in tiles:
                p = jnp.exp2(nt(keys, q) * EXP2_SCALE - lse)
                if seen is not None:
                    p = jnp.where(seen, p, 0.0)
                ds = (p * (nt(values, do) - delta)).astype(bf16)
                dk, dv = nn(ds, q), nn(p.astype(bf16), do)
                dq = dq + nn(keys_t, ds)
                if not shared:
                    own_dk, own_dv = own_dk + dk, own_dv + dv
                elif number == 0 and i == 0:
                    dk_ref[...] = dk
                    dv_ref[...] = dv
                else:
                    dk_ref[...] += dk
                    dv_ref[...] += dv
            back, part = key_back(jnp.transpose(dq), rawq_ref[own, head(i)], cos, sin, qg_ref[...])
            dq_ref[own, head(i)] = back
            gains_ref[0:1, :] += part
        if not in_prompt:
            back, part = key_back(own_dk, rawk_ref[own, :], cos, sin, kg_ref[...])
            dkv_ref[own, head(0)] = back
            dkv_ref[own, head(1)] = own_dv.astype(bf16)
            gains_ref[1:2, :] += part
        else:
            dkv_ref[own, :] = jnp.zeros((n, 256), bf16)
    for t, ref in enumerate((d0, d1, d2, d3)):
        ref[:, head(0)] = dk_ref[t * 256 : (t + 1) * 256, :].astype(bf16)
        ref[:, head(1)] = dv_ref[t * 256 : (t + 1) * 256, :].astype(bf16)


def attn_bwd(info, q, kv, prompt, do, o, lse, rawq, rawk, qg, kg, cos, sin):
    rows = q.shape[0]
    return pl.pallas_call(
        attn_bwd_kernel,
        grid_spec=pltpu.PrefetchScalarGridSpec(
            num_scalar_prefetch=1,
            grid=(4,),
            in_specs=attn_specs(rows, "wide", "wide", *["prompt"] * 4, "wide", "wide", "lse")
            + attn_specs(rows, "wide", "head", "gain", "gain", "table", "table"),
            out_specs=attn_specs(rows, "wide", "wide", *["prompt"] * 4, "gains"),
            scratch_shapes=[pltpu.VMEM((PROMPT, HEAD_SIZE), f32)] * 2
            + [pltpu.VMEM((PROMPT, 256), bf16)],
        ),
        out_shape=[jax.ShapeDtypeStruct((rows, 1024), bf16)] * 2
        + [jax.ShapeDtypeStruct((2 * RUN, 1024), bf16)] * 4
        + [jax.ShapeDtypeStruct((8, HEAD_SIZE), f32)],
        compiler_params=params(),
        cost_estimate=pl.CostEstimate(flops=45*10**9, bytes_accessed=10**7, transcendentals=0),
        name="attn_bwd",
    )(info, q, kv, *prompt, do, o, lse, rawq, rawk, qg, kg, cos, sin)


def prompt_back_kernel(d0, d1, d2, d3, dkv_ref, raw_ref, kg_ref, cos_ref, sin_ref, out_ref, gains_ref):
    out_ref[...] = dkv_ref[...]
    gains_ref[...] = jnp.zeros_like(gains_ref)
    for b in range(2):
        rows = slice(b * RUN, (b + 1) * RUN)
        own = slice(b * HELD, b * HELD + RUN)
        for h in range(4):
            cols = slice(h * 256, (h + 1) * 256)
            total = sum(d[rows, cols].astype(f32) for d in (d0, d1, d2, d3))
            back, part = key_back(
                total[:, head(0)], raw_ref[own, head(h)], cos_ref[own, :], sin_ref[own, :], kg_ref[...]
            )
            out_ref[own, h * 256 : h * 256 + 128] = back
            out_ref[own, h * 256 + 128 : (h + 1) * 256] = total[:, head(1)].astype(bf16)
            gains_ref[0:1, :] += part


def out_kernel(info, o_ref, *refs):
    pieces, (own_ref, sib_ref, w_ref) = refs[:2], refs[2:]
    for t in range(4):
        w_ref[rows_at((info[4] ^ t) * 256, 256), :] = pieces[t % 2][t // 2]
    half = own_ref.shape[0]
    own_ref[...] = nn(o_ref[:half, :], w_ref[...])
    sib_ref[...] = nn(o_ref[half:, :], w_ref[...]).astype(bf16)


def mlp_kernel(info, h_own, h_sib, g_own, g_sib, *refs):
    w2, w3 = refs[:10], refs[10:14]
    hid_ref, dgu_ref, out_ref, outs_ref, dh_ref, dhs_ref = refs[14:20]
    w_ref, wd_ref, out_acc, dh_acc = refs[20:]
    step = pl.program_id(0)
    ff = hid_ref.shape[1]
    half = out_ref.shape[0]
    for e in range(8):
        row = (info[0] ^ e) * 128
        w_ref[rows_at(row + info[1] * 64, 64), :] = w2[e][...]
        w_ref[rows_at(row + (1 - info[1]) * 64, 64), :] = w2[8 + e // 4][e % 4]
    for t in range(4):

        @pl.when(step == t)
        def take(t=t):
            wd_ref[...] = w3[t][...]

    @pl.when(step == 0)
    def zero():
        for ref in (out_ref, dh_ref, out_acc, dh_acc):
            ref[...] = jnp.zeros_like(ref)

    sides = ((h_own, g_own, out_ref, dh_ref), (h_sib, g_sib, out_acc, dh_acc))
    for b, (h_ref, g_ref, out, dh) in enumerate(sides):
        rows = slice(b * half, (b + 1) * half)
        both = nn(h_ref[...], w_ref[...])
        gate, up = both[:, :ff], both[:, ff:]
        sig = jax.nn.sigmoid(gate)
        silu = gate * sig
        hid = (silu * up).astype(bf16)
        hid_ref[rows, :] = hid
        dhid = nt(g_ref[...], wd_ref[...])
        dgu_ref[rows, :ff] = (dhid * up * sig * (1.0 + gate * (1.0 - sig))).astype(bf16)
        dgu_ref[rows, ff:] = (dhid * silu).astype(bf16)
        dh[...] += nt(dgu_ref[rows, :], w_ref[...])
        out[...] += nn(hid, wd_ref[...])

    @pl.when(step == 3)
    def finish():
        outs_ref[...] = out_acc[...].astype(bf16)
        dhs_ref[...] = dh_acc[...].astype(bf16)


def mlp(info, hidden, grad, w2, w3, ff):
    half, width = hidden[0].shape
    rows = 2 * half
    once = pl.Buffered(1)

    def still(shape):
        return pl.BlockSpec(shape, lambda g, s: (0, 0), pipeline_mode=once)

    return pl.pallas_call(
        mlp_kernel,
        grid_spec=pltpu.PrefetchScalarGridSpec(
            num_scalar_prefetch=1,
            grid=(4,),
            in_specs=[still((half, width))] * 4
            + [pl.BlockSpec((64, 2 * ff), lambda g, s: (0, s[4] ^ g))] * 8
            + [pl.BlockSpec((4, 64, 2 * ff), lambda g, s: (0, 0, s[4] ^ g))] * 2
            + [still(w3[0].shape)] * 4,
            out_specs=[
                pl.BlockSpec((rows, ff), lambda g, s: (0, s[4] ^ g)),
                pl.BlockSpec((rows, 2 * ff), lambda g, s: (0, s[4] ^ g)),
            ]
            + [pl.BlockSpec((half, width), lambda g, s: (0, 0))] * 4,
            scratch_shapes=[
                pltpu.VMEM((width, 2 * ff), bf16),
                pltpu.VMEM((ff, width), bf16),
                pltpu.VMEM((half, width), f32),
                pltpu.VMEM((half, width), f32),
            ],
        ),
        out_shape=[
            jax.ShapeDtypeStruct((rows, 4 * ff), bf16),
            jax.ShapeDtypeStruct((rows, 8 * ff), bf16),
            jax.ShapeDtypeStruct((half, width), f32),
            jax.ShapeDtypeStruct((half, width), bf16),
            jax.ShapeDtypeStruct((half, width), f32),
            jax.ShapeDtypeStruct((half, width), bf16),
        ],
        compiler_params=params(),
        cost_estimate=pl.CostEstimate(flops=38*10**9, bytes_accessed=10**7, transcendentals=0),
        name="feed_forward",
    )(info, *hidden, *grad, *w2, *w3)


def gate_up_kernel(info, own_ref, sib_ref, gate_ref, up_ref):
    ff = own_ref.shape[1] // 8
    for first, (low, high) in ((0, (own_ref, sib_ref)), (1, (sib_ref, own_ref))):

        @pl.when(info[2] == first)
        def write(low=low, high=high):
            for c, ref in enumerate((low, high)):
                for b in range(4):
                    cols = slice((c * 4 + b) * ff, (c * 4 + b + 1) * ff)
                    gate_ref[:, cols] = ref[:, 2 * b * ff : (2 * b + 1) * ff].astype(f32)
                    up_ref[:, cols] = ref[:, (2 * b + 1) * ff : (2 * b + 2) * ff].astype(f32)


def attn_weights_kernel(info, own_ref, sib_ref, query_ref, key_ref, value_ref):
    for first, (low, high) in ((0, (own_ref, sib_ref)), (1, (sib_ref, own_ref))):

        @pl.when(info[2] == first)
        def write(low=low, high=high):
            for c, ref in enumerate((low, high)):
                query_ref[:, c * 1024 : (c + 1) * 1024] = ref[:, :1024].astype(f32)
                for h in range(4):
                    start = 1024 + h * 256
                    to = head(c * 4 + h)
                    key_ref[:, to] = ref[:, start : start + 128].astype(f32)
                    value_ref[:, to] = ref[:, start + 128 : start + 256].astype(f32)


def device_of(y, core, z_hi, z_lo, x):
    return (y * 2 + core) * N_CTX + z_hi * 4 + z_lo * 2 + x


def bits_of(i):
    return ((i >> 4) & 1, (i >> 3) & 1, (i >> 2) & 1, (i >> 1) & 1, i & 1)


def permutation(target, sends=lambda *bits: True):
    devices = range(N_GRP * N_CTX)
    return [(i, device_of(*target(*bits_of(i)))) for i in devices if sends(*bits_of(i))]


def member_device(e):
    def target(y, core, z_hi, z_lo, x):
        m = (z_hi * 4 + z_lo * 2 + x) ^ e
        return (y, m >> 2, core, (m >> 1) & 1, m & 1)

    return target


SPREAD = [permutation(member_device(e)) for e in range(8)]
COLLECT = [[(b, a) for a, b in pairs] for pairs in SPREAD]
HALVES = permutation(
    lambda y, core, z_hi, z_lo, x: (y, z_hi, core, z_lo, x),
    lambda y, core, z_hi, z_lo, x: z_hi != core,
)
CUBES = [
    [device_of(y, m >> 2, z_hi, (m >> 1) & 1, m & 1) for m in range(8)]
    for y in range(2)
    for z_hi in range(2)
]
OVER_Y = permutation(lambda y, core, z_hi, z_lo, x: (1 - y, core, z_hi, z_lo, x))
SIBLING = permutation(lambda y, core, z_hi, z_lo, x: (y, 1 - core, z_hi, z_lo, x))
OVER_Y_HOME = permutation(
    lambda y, core, z_hi, z_lo, x: (1 - y, core, z_hi, z_lo, x),
    lambda y, core, z_hi, z_lo, x: z_hi == core,
)
MIDDLE = permutation(lambda y, core, z_hi, z_lo, x: (y, core, 1 - z_hi, z_lo, x))
MIDDLE_OUT = permutation(
    lambda y, core, z_hi, z_lo, x: (y, core, 1 - z_hi, z_lo, x),
    lambda y, core, z_hi, z_lo, x: z_hi == core,
)
MIDDLE_IN = permutation(
    lambda y, core, z_hi, z_lo, x: (y, core, 1 - z_hi, z_lo, x),
    lambda y, core, z_hi, z_lo, x: z_hi != core,
)
CHIP = [
    permutation(
        lambda y, core, z_hi, z_lo, x, t=t: (y, core, z_hi, z_lo ^ (t >> 1), x ^ (t & 1))
    )
    for t in range(4)
]


def permute(a, pairs):
    return lax.ppermute(a, AXES, pairs)


def pick(a, i, axis=0):
    return lax.dynamic_index_in_dim(a, i, axis, keepdims=False)


def added(*terms):
    return sum(t.astype(f32) for t in terms).astype(bf16)


def after(a, b):
    return lax.optimization_barrier((a, b))[0]


def together(*arrays):
    return lax.optimization_barrier(arrays)


def in_order(first, mine, other):
    return [jnp.where(first, mine, other), jnp.where(first, other, mine)]


def shards_split(
    tokens,
    block_table,
    norm1_gain,
    w_query,
    key_weight,
    value_weight,
    query_gain,
    key_norm_gain,
    w_out,
    norm2_gain,
    w_gate,
    w_up,
    w_down,
    out_grad,
):
    row_total, width = tokens.shape
    n_slots = row_total // BLK
    ff = w_gate.shape[1] // 8
    position = lax.axis_index("ctx").astype(jnp.int32)
    group_index = lax.axis_index("grp").astype(jnp.int32)
    y, core = group_index // 2, group_index % 2
    z_hi, chip = position // 4, position % 4
    z_lo, x = chip // 2, chip % 2
    member = core * 4 + chip
    info = jnp.stack([position, y, core, member, chip])
    at_home = z_hi == core
    qg, kg = query_gain.reshape(1, HEAD_SIZE), key_norm_gain.reshape(1, HEAD_SIZE)

    eight = jnp.arange(8, dtype=jnp.int32)
    five = jnp.arange(CHUNK, dtype=jnp.int32)[None, :]

    def slots_of(m):
        m = m.reshape(-1, 1)
        return jnp.where(five == 0, m, 7 + 7 * (m // 2) + 3 * (m % 2) + five)

    def held_at(natural, m):
        inside = natural - (PROMPT_BLOCKS + CONT_BLOCKS * m)
        valid = (five == 0) | ((inside >= 0) & (inside < CONT_BLOCKS))
        return jnp.where(valid, jnp.where(five == 0, natural - 8 * m, 8 + inside), n_slots), valid

    def look_up(rows, slots):
        match = slots[:, :, None] == jnp.arange(n_slots, dtype=jnp.int32)
        return jnp.sum(jnp.where(match, rows[:, None, :], 0), axis=2)

    tables = block_table.reshape(8, n_slots)
    send_slots = slots_of(position ^ eight)
    from_tables = jnp.concatenate(
        [lax.dynamic_slice_in_dim(tables, member ^ e, 1, 0) for e in range(8)], axis=0
    )
    arrive, _ = held_at(look_up(from_tables, jnp.broadcast_to(slots_of(member), (8, CHUNK))), member)
    leave = jnp.minimum(arrive, n_slots - 1)
    own_table = lax.dynamic_slice_in_dim(tables, position, 1, 0)
    _, valid = held_at(look_up(own_table, send_slots), (position ^ eight).reshape(-1, 1))
    home_slots = jnp.where(valid, send_slots, n_slots)

    def spread(a):
        return [permute(c, pairs) for c, pairs in zip(deal(send_slots, a), SPREAD)]

    def collect(a, kind):
        pieces = [permute(c, pairs) for c, pairs in zip(deal(leave, a), COLLECT)]
        return place(home_slots, pieces, row_total, kind)

    def regrouped(a):
        return jnp.where(at_home, a, permute(a, HALVES))

    def both(a):
        return jnp.concatenate([a, permute(a, SIBLING)], axis=0)

    def columns(w, parts):
        return pick(w.reshape(w.shape[0], 2, 4, -1), core, 1)

    own_one = jnp.concatenate(
        [
            columns(w_query, 2).reshape(-1, 1024),
            jnp.concatenate([columns(key_weight, 2), columns(value_weight, 2)], axis=2).reshape(
                -1, 1024
            ),
        ],
        axis=1,
    )
    own_two = jnp.concatenate([columns(w_gate, 2), columns(w_up, 2)], axis=2)
    own_two = pick(own_two.reshape(2, 64, 8 * ff), y)
    own_out, own_down = w_out, w_down

    def around(a):
        return [a] + [permute(a, CHIP[t]) for t in range(1, 4)]

    one = around(own_one)
    middle_one = permute(own_one, MIDDLE)
    arrived = spread(tokens)
    one = one + around(middle_one)

    cosine, sine = rotation(jnp.arange(PROMPT + CONT_LEN, dtype=jnp.int32))
    cos = jnp.concatenate([cosine[:, 0], cosine[:, 0]], axis=1)
    sin = jnp.concatenate([-sine[:, 0], sine[:, 0]], axis=1)

    def of_rows(table):
        parts = []
        for m in (member, member ^ 4):
            parts += [lax.dynamic_slice_in_dim(table, m * RUN, RUN, 0), table[PROMPT:]]
        return jnp.concatenate(parts, axis=0)

    cos, sin = of_rows(cos), of_rows(sin)

    inputs_low, first_low = place_norm(arrive, arrived, norm1_gain.reshape(1, width), row_total)
    hidden_one = both(first_low)
    own_two, own_three, out_grad = together(
        own_two, jnp.concatenate([w_down, w_out], axis=0), out_grad, first_low
    )[:3]
    middle_three = permute(own_three, MIDDLE_OUT)
    hidden_one, middle_three, own_two, out_grad, *one = together(
        hidden_one, middle_three, own_two, out_grad, *one
    )
    home_three = jnp.where(at_home, own_three, middle_three)
    home_down, home_out = home_three[: 3 * RUN], home_three[3 * RUN :]

    two = around(own_two)
    middle_two = permute(own_two, MIDDLE)
    outs = jnp.stack([home_out, permute(home_out, CHIP[2])])
    kv, rawk, w_kv, prompt_kv = project(
        key_value_kernel, "key_value", info, hidden_one, one, 4, kg, cos, sin, HEAD_SIZE, 1
    )
    prompt_kv, outs, out_grad, hidden_q, middle_two, *two = together(
        prompt_kv, outs, out_grad, hidden_one, middle_two, *two
    )

    prompt = around(prompt_kv)
    outs = [outs, permute(outs, CHIP[1])]
    grad_here = regrouped(out_grad)
    q, rawq, w_q = project(query_kernel, "query", info, hidden_q, one, 0, qg, cos, sin, 256, 0)
    q, grad_here, middle_two, home_down, *rest = together(
        q, grad_here, middle_two, home_down, *outs, *prompt
    )
    outs, prompt = rest[:2], rest[2:]

    two += around(middle_two)
    other_two = [permute(jnp.stack(two[:4]), OVER_Y)]
    mixed, lse = attn_fwd(info, q, kv, prompt)
    mixed, home_down, grad_here, *rest = together(mixed, home_down, grad_here, *two, *other_two)
    two, other_two = rest[:8], rest[8:]

    other_two.append(permute(jnp.stack(two[4:]), OVER_Y))
    downs = around(home_down)
    chunk_starts = [8 + 7 * (m // 2) + 3 * (m % 2) for m in range(8)]
    grad_here = jnp.concatenate(
        [
            grad_here[: 8 * BLK].reshape(8, BLK, width),
            jnp.stack([grad_here[start * BLK : (start + 4) * BLK] for start in chunk_starts]),
        ],
        axis=1,
    )

    def swap_cube(a):
        return lax.all_to_all(a, AXES, 0, 0, tiled=True, axis_index_groups=CUBES)

    grad_here = swap_cube(grad_here)
    in_turn = jnp.concatenate(
        [lax.dynamic_slice_in_dim(arrive, member ^ e, 1, 0) for e in range(8)], axis=0
    )
    leave_in_turn = jnp.minimum(in_turn, n_slots - 1)
    home_in_turn = jnp.concatenate(
        [lax.dynamic_slice_in_dim(home_slots, position ^ e, 1, 0) for e in range(8)], axis=0
    )

    rows_kind = ((row_total, width), f32), ((row_total, width), bf16)
    out_own, out_sib, w_o = whole_call(
        out_kernel,
        "out_projection",
        (info, mixed, *outs),
        [*rows_kind, ((1024, width), bf16)],
    )
    inputs = inputs_low.astype(f32)
    resid_one = inputs + out_own + permute(out_sib, SIBLING).astype(f32)
    normed_two, inverse_two = normed_parts(resid_one)
    hidden_two = (normed_two * norm2_gain).astype(bf16)
    hidden_two, other_far, *downs = together(hidden_two, other_two[1], *downs)
    other_two = [other_two[0], other_far]
    hidden_two = [hidden_two, permute(hidden_two, SIBLING)]
    grad_low = place_all(in_turn, grad_here, row_total, bf16)
    grad_both = [grad_low, permute(grad_low, SIBLING)]
    hid, grad_gu, ff_own, ff_sib, back_own, back_sib = mlp(
        info, hidden_two, grad_both, two + other_two, downs, ff
    )
    hidden_two = jnp.concatenate(hidden_two, axis=0)
    grad_both = jnp.concatenate(grad_both, axis=0)
    grad_two = back_own + permute(back_sib, SIBLING).astype(f32)
    gain_two_part = jnp.sum(grad_two * normed_two, axis=0)
    grad_resid = grad_low.astype(f32) + norm_back(grad_two * norm2_gain, normed_two, inverse_two)
    grad_attn = both(grad_resid.astype(bf16))

    def chip_parts(grad):
        grad = grad.reshape(8, -1, grad.shape[-1])
        return [
            jnp.stack([pick(grad, position ^ t), pick(grad, position ^ (4 + t))]) for t in range(4)
        ]

    def sent_to_chips(parts):
        return [permute(parts[t], CHIP[t]) for t in range(1, 4)]

    def from_middle(part):
        return added(pick(part, z_hi), permute(pick(part, 1 - z_hi), MIDDLE))

    def halved(grad, axis, bit, pairs):
        return added(pick(grad, bit, axis), permute(pick(grad, 1 - bit, axis), pairs))

    grad_two_w = tn(hidden_two, grad_gu).astype(bf16).reshape(2, 2, 2, 2, 64, -1)
    keep_two, send_two = pick(grad_two_w, y, 3), pick(grad_two_w, 1 - y, 3)
    send_two = permute(send_two, OVER_Y)
    grad_down = tn(hid, grad_both).astype(bf16).reshape(2, 2, -1, width)
    grad_out = tn(mixed, grad_attn).astype(bf16).reshape(2, 2, -1, width)
    outcome = resid_one + ff_own + permute(ff_sib, SIBLING).astype(f32)
    leaving = deal_all(leave_in_turn, outcome.astype(bf16))
    grad_attn, grad_down, grad_out, leaving, _ = together(
        grad_attn, grad_down, grad_out, leaving, keep_two
    )
    keep_down, send_down = pick(grad_down, x, 1), permute(pick(grad_down, 1 - x, 1), CHIP[1])
    keep_out, send_out = pick(grad_out, z_lo), permute(pick(grad_out, 1 - z_lo), CHIP[2])
    leaving = swap_cube(leaving)
    grad_mixed = nt(grad_attn, w_o).astype(bf16)
    grad_q, grad_kv, *prompt_parts, gains = attn_bwd(
        info, q, kv, prompt, grad_mixed, mixed, lse, rawq, rawk, qg, kg, cos, sin
    )
    grad_q, grad_kv, send_down, send_out, leaving, *prompt_parts = together(
        grad_q, grad_kv, send_down, send_out, leaving, *prompt_parts
    )

    prompt_parts = [prompt_parts[0]] + [permute(prompt_parts[t], CHIP[t]) for t in range(1, 4)]
    grad_wq = tn(hidden_one, grad_q).astype(bf16).reshape(8, 2, 64, -1)
    keep_q, send_q = pick(grad_wq, y, 1), permute(pick(grad_wq, 1 - y, 1), OVER_Y)
    grad_q, keep_q, send_q, send_down, send_out, send_two, leaving, *prompt_parts = together(
        grad_q, keep_q, send_q, send_down, send_out, send_two, leaving, *prompt_parts
    )
    left = regrouped(leaving.reshape(-1, width))
    sum_two = added(keep_two, send_two)
    down, out = added(keep_down, send_down), added(keep_out, send_out)
    down = halved(down, 0, z_lo, CHIP[2])
    out = halved(out, 0, x, CHIP[1])
    sum_two = halved(sum_two, 2, x, CHIP[1])
    grad_kv, key_gains = whole_call(
        prompt_back_kernel,
        "prompt_back",
        (*prompt_parts, grad_kv, rawk, kg, cos, sin),
        [(grad_kv.shape, bf16), ((8, HEAD_SIZE), f32)],
    )
    grad_wkv = tn(hidden_one, grad_kv).astype(bf16).reshape(8, 2, 64, -1)
    grad_one = nt(grad_q, w_q) + nt(after(grad_kv, grad_wkv), w_kv)
    grad_one, sum_two = together(grad_one, sum_two)
    grad_one = grad_one[:row_total] + permute(
        grad_one[row_total:].astype(bf16), SIBLING
    ).astype(f32)
    normed_one, inverse_one = normed_parts(inputs)
    gain_one_part = jnp.sum(grad_one * normed_one, axis=0)
    grad_tokens = grad_resid + norm_back(grad_one * norm1_gain, normed_one, inverse_one)
    going = deal_all(leave_in_turn, grad_tokens.astype(bf16))
    gain_grads = jnp.concatenate(
        [gain_one_part, gain_two_part, gains[0], gains[1] + key_gains[0]]
    ).reshape(-1, HEAD_SIZE)
    going, gain_grads, down, out, keep_q, send_q, grad_wkv, left, sum_two = together(
        going, gain_grads, down, out, keep_q, send_q, grad_wkv, left, sum_two
    )
    going = swap_cube(going)
    q_parts = chip_parts(added(keep_q, send_q))
    q_sent = sent_to_chips(q_parts)
    keep_kv, send_kv = pick(grad_wkv, y, 1), permute(pick(grad_wkv, 1 - y, 1), OVER_Y)
    three = jnp.concatenate([down, out], axis=0)
    three = added(three, permute(three, MIDDLE_IN))
    gain_grads = gain_grads + permute(gain_grads, SIBLING)
    outcome = place_all(home_in_turn, left.reshape(8, -1, width), row_total, bf16)
    going, gain_grads, outcome, keep_kv, send_kv, sum_two, *q_sent = together(
        going, gain_grads, outcome, keep_kv, send_kv, sum_two, *q_sent
    )
    going = regrouped(going.reshape(-1, width))
    sum_two = halved(sum_two, 1, z_lo, CHIP[2])
    gain_grads = gain_grads + permute(gain_grads, CHIP[1])
    kv_parts = chip_parts(added(keep_kv, send_kv))
    kv_sent = sent_to_chips(kv_parts)
    part_q = added(q_parts[0], *q_sent)
    going, gain_grads, sum_two, three, *kv_sent = together(
        going, gain_grads, sum_two, three, *kv_sent
    )
    gain_grads = gain_grads + permute(gain_grads, CHIP[2])
    grad_tokens = place_all(home_in_turn, going.reshape(8, -1, width), row_total, f32)
    part_kv = added(kv_parts[0], *kv_sent)
    sum_one = jnp.concatenate([part_q, part_kv], axis=2)
    sum_one = added(sum_one[0], permute(sum_one[1], MIDDLE))
    three = added(three, permute(three, OVER_Y_HOME))
    sum_two = from_middle(sum_two)
    sum_one, sum_two, three, gain_grads = together(sum_one, sum_two, three, gain_grads)
    sum_two = jnp.concatenate(in_order(y == 0, sum_two, permute(sum_two, OVER_Y)), axis=0)
    gain_grads = gain_grads + permute(gain_grads, OVER_Y)
    sum_one = jnp.concatenate(in_order(y == 0, sum_one, permute(sum_one, OVER_Y)), axis=0)
    total = jnp.where(at_home, three, permute(three, SIBLING)).astype(f32)
    sum_one, sum_two, gain_grads = together(sum_one, sum_two, gain_grads)
    gain_grads = gain_grads + permute(gain_grads, MIDDLE)
    shard = sum_two.shape[0]
    gate_grad, up_grad = whole_call(
        gate_up_kernel,
        "gate_up_gradients",
        (info, sum_two, permute(sum_two, SIBLING)),
        [((shard, 8 * ff), f32)] * 2,
    )
    query_grad, key_grad, value_grad = whole_call(
        attn_weights_kernel,
        "attn_weight_gradients",
        (info, sum_one, permute(sum_one, SIBLING)),
        [((shard, 2048), f32), ((shard, 1024), f32), ((shard, 1024), f32)],
    )
    gain_grads = gain_grads.reshape(-1)
    return (
        outcome,
        grad_tokens,
        gain_grads[:width],
        query_grad,
        key_grad,
        value_grad,
        gain_grads[2 * width : 2 * width + HEAD_SIZE],
        gain_grads[2 * width + HEAD_SIZE :],
        total[3 * RUN :],
        gain_grads[width : 2 * width],
        gate_grad,
        up_grad,
        total[: 3 * RUN],
    )


def solution(mesh):
    split = mesh.shape["grp"] == N_GRP and mesh.shape["ctx"] == N_CTX
    return jax.shard_map(
        shards_split if split else shards,
        mesh=mesh,
        in_specs=(
            P(("grp", "ctx"), None),
            P(),
            P(),
            P("ctx", None),
            P("ctx", None),
            P("ctx", None),
            P(),
            P(),
            P("ctx", None),
            P(),
            P("ctx", None),
            P("ctx", None),
            P("ctx", None),
            P(("grp", "ctx"), None),
        ),
        out_specs=(
            P(("grp", "ctx"), None),
            P(("grp", "ctx"), None),
            P(),
            P("ctx", None),
            P("ctx", None),
            P("ctx", None),
            P(),
            P(),
            P("ctx", None),
            P(),
            P("ctx", None),
            P("ctx", None),
            P("ctx", None),
        ),
        check_vma=False,
    )
```

```python
import math

import jax
import jax.numpy as jnp
from jax import lax
from jax.experimental import pallas as pl
from jax.experimental.pallas import tpu as pltpu
from jax.sharding import PartitionSpec as P

QUERY_HEADS = 16
KEY_VALUE_HEADS = 8
HEAD_SIZE = 128
PROMPT = 1024
CONT_LEN = 448
BLK = 16


eps = 1e-06
theta = 1000000.0
key_span = 512
masked_score = -1e30


def normed_parts(value_rows):
    inverse = lax.rsqrt(jnp.mean(value_rows * value_rows, axis=-1, keepdims=True) + eps)
    return (value_rows * inverse, inverse)


def norm_back(grad_normed, normed, inverse):
    return inverse * (grad_normed - normed * jnp.mean(grad_normed * normed, axis=-1, keepdims=True))


def layout(block_table, slot_ids):
    natural = block_table[slot_ids // BLK] * BLK + slot_ids % BLK
    beyond = natural - PROMPT
    segment = jnp.where(natural < PROMPT, 0, 1 + beyond // CONT_LEN)
    places = jnp.where(natural < PROMPT, natural, PROMPT + beyond % CONT_LEN)
    return (natural, segment, places)


def rotation(places):
    half_dim = HEAD_SIZE // 2
    frequency = jnp.exp(
        jnp.arange(half_dim, dtype=jnp.float32) * (-2.0 * math.log(theta) / HEAD_SIZE)
    )
    angles = places.astype(jnp.float32)[:, None] * frequency[None, :]
    return (jnp.cos(angles)[:, None, :], jnp.sin(angles)[:, None, :])


def apply_rotation(value_rows, cosine_table, sine_table):
    half_dim = value_rows.shape[-1] // 2
    first_half = value_rows[..., :half_dim]
    second_half = value_rows[..., half_dim:]
    return jnp.concatenate(
        [
            first_half * cosine_table - second_half * sine_table,
            second_half * cosine_table + first_half * sine_table,
        ],
        axis=-1,
    )


def rotate_back(value_rows, cosine_table, sine_table):
    half_dim = value_rows.shape[-1] // 2
    first_half = value_rows[..., :half_dim]
    second_half = value_rows[..., half_dim:]
    return jnp.concatenate(
        [
            first_half * cosine_table + second_half * sine_table,
            second_half * cosine_table - first_half * sine_table,
        ],
        axis=-1,
    )


def allowed_mask(own_nat, own_seg, key_nat, key_seg):
    return (key_nat[None, :] <= own_nat[:, None]) & (
        (key_seg[None, :] == 0) | (key_seg[None, :] == own_seg[:, None])
    )


def span_of():
    return key_span


def over_blocks(advance, running, length):
    block_span_width = span_of()

    def scan_step(inner_state, key_first):
        return (advance(inner_state, key_first, block_span_width), None)

    running, ignored = lax.scan(
        scan_step,
        running,
        jnp.arange(length // block_span_width, dtype=jnp.int32) * block_span_width,
    )
    return running


def attend_block(running, query_head_rows, keys_part, values_part, allowed, softmax_scale):
    row_max, row_sum, accum = running
    raw_scores = (
        jnp.einsum("grtd,ngd->grtn", query_head_rows, keys_part, preferred_element_type=jnp.float32)
        * softmax_scale
    )
    scores = jnp.where(allowed, raw_scores, masked_score)
    new_max = jnp.maximum(row_max, jnp.max(scores, axis=-1))
    rescale = jnp.exp(row_max - new_max)
    weights = jnp.exp(scores - new_max[..., None])
    row_sum = row_sum * rescale + jnp.sum(weights, axis=-1)
    accum = accum * rescale[..., None] + jnp.einsum(
        "grtn,ngd->grtd",
        weights.astype(jnp.bfloat16),
        values_part,
        preferred_element_type=jnp.float32,
    )
    return (new_max, row_sum, accum)


def key_terms(
    grad_scores, weights, query_head_rows, scaled_high, scaled_rest, softmax_scale, block_span_width
):
    grad_keys = (
        jnp.einsum(
            "grtn,grtd->ngd", grad_scores, query_head_rows, preferred_element_type=jnp.float32
        )
        * softmax_scale
    )
    weights_low = weights.astype(jnp.bfloat16)
    grad_values = jnp.einsum(
        "grtn,grtd->ngd", weights_low, scaled_high, preferred_element_type=jnp.float32
    )
    grad_values = grad_values + jnp.einsum(
        "grtn,grtd->ngd", weights_low, scaled_rest, preferred_element_type=jnp.float32
    )
    return jnp.stack(
        [grad_keys.reshape(block_span_width, -1), grad_values.reshape(block_span_width, -1)], axis=1
    )


def shards(
    tokens,
    block_table,
    norm1_gain,
    w_query,
    key_weight,
    value_weight,
    query_gain,
    key_norm_gain,
    w_out,
    norm2_gain,
    w_gate,
    w_up,
    w_down,
    out_grad,
):
    row_total = tokens.shape[0]
    group_length = block_table.shape[0] * BLK
    sharing_count = QUERY_HEADS // KEY_VALUE_HEADS
    softmax_scale = 1.0 / math.sqrt(HEAD_SIZE)
    position = lax.axis_index("ctx")
    all_nat, all_seg, all_places = layout(block_table, jnp.arange(group_length, dtype=jnp.int32))
    own_slots = position * row_total + jnp.arange(row_total, dtype=jnp.int32)
    own_nat, own_seg, own_places = layout(block_table, own_slots)
    cosine_table, sine_table = rotation(own_places)
    query_full, key_full, value_full, out_full = (
        lax.all_gather(w_query, "ctx", axis=0, tiled=True),
        lax.all_gather(key_weight, "ctx", axis=0, tiled=True),
        lax.all_gather(value_weight, "ctx", axis=0, tiled=True),
        lax.all_gather(w_out, "ctx", axis=0, tiled=True),
    )
    inputs = tokens.astype(jnp.float32)
    normed_one, inverse_one = normed_parts(inputs)
    first_hidden = (normed_one * norm1_gain).astype(jnp.bfloat16)
    query_raw = jnp.dot(first_hidden, query_full, preferred_element_type=jnp.float32).reshape(
        row_total, QUERY_HEADS, HEAD_SIZE
    )
    unnormalized_keys = jnp.dot(first_hidden, key_full, preferred_element_type=jnp.float32).reshape(
        row_total, KEY_VALUE_HEADS, HEAD_SIZE
    )
    reduced_value = jnp.dot(first_hidden, value_full, preferred_element_type=jnp.float32).astype(
        jnp.bfloat16
    )
    query_normed, query_inverse = normed_parts(query_raw)
    normalized_keys, key_inverse = normed_parts(unnormalized_keys)
    reduced_query = apply_rotation(query_normed * query_gain, cosine_table, sine_table).astype(
        jnp.bfloat16
    )
    key_low = (
        apply_rotation(normalized_keys * key_norm_gain, cosine_table, sine_table)
        .astype(jnp.bfloat16)
        .reshape(row_total, KEY_VALUE_HEADS * HEAD_SIZE)
    )
    query_head_rows = jnp.transpose(
        reduced_query.reshape(row_total, KEY_VALUE_HEADS, sharing_count, HEAD_SIZE), (1, 2, 0, 3)
    )

    def attend(running, pieces):
        piece_keys, piece_values = pieces

        def advance(inner_state, key_first, block_span_width):
            keys_part = lax.dynamic_slice_in_dim(
                piece_keys, key_first, block_span_width, 0
            ).reshape(block_span_width, KEY_VALUE_HEADS, HEAD_SIZE)
            values_part = lax.dynamic_slice_in_dim(
                piece_values, key_first, block_span_width, 0
            ).reshape(block_span_width, KEY_VALUE_HEADS, HEAD_SIZE)
            key_nat = lax.dynamic_slice_in_dim(all_nat, key_first, block_span_width)
            key_seg = lax.dynamic_slice_in_dim(all_seg, key_first, block_span_width)
            allowed = allowed_mask(own_nat, own_seg, key_nat, key_seg)
            return attend_block(
                inner_state, query_head_rows, keys_part, values_part, allowed, softmax_scale
            )

        return over_blocks(advance, running, piece_keys.shape[0])

    statistic_shape = (KEY_VALUE_HEADS, sharing_count, row_total)
    initial = (
        jnp.full(statistic_shape, masked_score, jnp.float32),
        jnp.zeros(statistic_shape, jnp.float32),
        jnp.zeros(statistic_shape + (HEAD_SIZE,), jnp.float32),
    )
    row_max, row_sum, accum = attend(
        initial,
        (
            lax.all_gather(key_low, "ctx", axis=0, tiled=True),
            lax.all_gather(reduced_value, "ctx", axis=0, tiled=True),
        ),
    )
    mixed_heads = accum / row_sum[..., None]
    flat_low = (
        jnp.transpose(mixed_heads, (2, 0, 1, 3))
        .reshape(row_total, QUERY_HEADS * HEAD_SIZE)
        .astype(jnp.bfloat16)
    )
    resid_one = inputs + jnp.dot(flat_low, out_full, preferred_element_type=jnp.float32)
    gate_full, up_full, down_full = (
        lax.all_gather(w_gate, "ctx", axis=0, tiled=True),
        lax.all_gather(w_up, "ctx", axis=0, tiled=True),
        lax.all_gather(w_down, "ctx", axis=0, tiled=True),
    )
    normed_two, inverse_two = normed_parts(resid_one)
    hidden_two = (normed_two * norm2_gain).astype(jnp.bfloat16)
    gate_proj = jnp.dot(hidden_two, gate_full, preferred_element_type=jnp.float32)
    up_proj = jnp.dot(hidden_two, up_full, preferred_element_type=jnp.float32)
    gate_sigmoid = jax.nn.sigmoid(gate_proj)
    gate_silu = gate_proj * gate_sigmoid
    hidden_low = (gate_silu * up_proj).astype(jnp.bfloat16)
    outcome = resid_one + jnp.dot(hidden_low, down_full, preferred_element_type=jnp.float32)
    gate_full, up_full, down_full = (
        lax.all_gather(w_gate, "ctx", axis=0, tiled=True),
        lax.all_gather(w_up, "ctx", axis=0, tiled=True),
        lax.all_gather(w_down, "ctx", axis=0, tiled=True),
    )
    grad_out = out_grad.astype(jnp.float32)
    grad_down = jnp.einsum("tf,td->fd", hidden_low, out_grad, preferred_element_type=jnp.float32)
    grad_hidden = jnp.einsum("td,fd->tf", out_grad, down_full, preferred_element_type=jnp.float32)
    grad_gate = (
        grad_hidden * up_proj * gate_sigmoid * (1.0 + gate_proj * (1.0 - gate_sigmoid))
    ).astype(jnp.bfloat16)
    grad_up = (grad_hidden * gate_silu).astype(jnp.bfloat16)
    grad_wgate = jnp.einsum("tk,tf->kf", hidden_two, grad_gate, preferred_element_type=jnp.float32)
    grad_wup = jnp.einsum("tk,tf->kf", hidden_two, grad_up, preferred_element_type=jnp.float32)
    grad_two = jnp.einsum(
        "tf,kf->tk", grad_gate, gate_full, preferred_element_type=jnp.float32
    ) + jnp.einsum("tf,kf->tk", grad_up, up_full, preferred_element_type=jnp.float32)
    gain_two_part = jnp.sum(grad_two * normed_two, axis=0)
    grad_resid = grad_out + norm_back(grad_two * norm2_gain, normed_two, inverse_two)
    grad_attn = grad_resid.astype(jnp.bfloat16)
    query_full, key_full, value_full, out_full = (
        lax.all_gather(w_query, "ctx", axis=0, tiled=True),
        lax.all_gather(key_weight, "ctx", axis=0, tiled=True),
        lax.all_gather(value_weight, "ctx", axis=0, tiled=True),
        lax.all_gather(w_out, "ctx", axis=0, tiled=True),
    )
    keys_all, values_all = (
        lax.all_gather(key_low, "ctx", axis=0, tiled=True),
        lax.all_gather(reduced_value, "ctx", axis=0, tiled=True),
    )
    grad_wout = jnp.einsum("tk,td->kd", flat_low, grad_attn, preferred_element_type=jnp.float32)
    flattened_grad = jnp.einsum(
        "td,kd->tk", grad_attn, out_full, preferred_element_type=jnp.float32
    ).astype(jnp.bfloat16)
    head_grads = jnp.transpose(
        flattened_grad.reshape(row_total, KEY_VALUE_HEADS, sharing_count, HEAD_SIZE), (1, 2, 0, 3)
    )
    grad_heads_wide = head_grads.astype(jnp.float32)
    row_delta = jnp.sum(grad_heads_wide * mixed_heads, axis=-1)
    scaled_grad = grad_heads_wide / row_sum[..., None]
    scaled_high = scaled_grad.astype(jnp.bfloat16)
    scaled_rest = (scaled_grad - scaled_high.astype(jnp.float32)).astype(jnp.bfloat16)

    def block_back(key_first, block_span_width):
        keys_part = lax.dynamic_slice_in_dim(keys_all, key_first, block_span_width, 0).reshape(
            block_span_width, KEY_VALUE_HEADS, HEAD_SIZE
        )
        values_part = lax.dynamic_slice_in_dim(values_all, key_first, block_span_width, 0).reshape(
            block_span_width, KEY_VALUE_HEADS, HEAD_SIZE
        )
        key_nat = lax.dynamic_slice_in_dim(all_nat, key_first, block_span_width)
        key_seg = lax.dynamic_slice_in_dim(all_seg, key_first, block_span_width)
        allowed = allowed_mask(own_nat, own_seg, key_nat, key_seg)
        raw_scores = (
            jnp.einsum(
                "grtd,ngd->grtn", query_head_rows, keys_part, preferred_element_type=jnp.float32
            )
            * softmax_scale
        )
        scores = jnp.where(allowed, raw_scores, masked_score)
        weights = jnp.exp(scores - row_max[..., None])
        grad_prob = jnp.einsum(
            "grtd,ngd->grtn", head_grads, values_part, preferred_element_type=jnp.float32
        )
        grad_scores = (weights * (grad_prob - row_delta[..., None]) / row_sum[..., None]).astype(
            jnp.bfloat16
        )
        return (keys_part, grad_scores, weights)

    empty_query = jnp.zeros((KEY_VALUE_HEADS, sharing_count, row_total, HEAD_SIZE), jnp.float32)
    span_back = span_of()

    def pass_step(grad_query, key_first):
        keys_part, grad_scores, weights = block_back(key_first, span_back)
        grad_query = grad_query + jnp.einsum(
            "grtn,ngd->grtd", grad_scores, keys_part, preferred_element_type=jnp.float32
        )
        return (
            grad_query,
            key_terms(
                grad_scores,
                weights,
                query_head_rows,
                scaled_high,
                scaled_rest,
                softmax_scale,
                span_back,
            ),
        )

    grad_query, key_gradient_parts = lax.scan(
        pass_step, empty_query, jnp.arange(group_length // span_back, dtype=jnp.int32) * span_back
    )
    self_terms = lax.psum_scatter(
        key_gradient_parts.reshape(group_length, 2, KEY_VALUE_HEADS * HEAD_SIZE).astype(
            jnp.bfloat16
        ),
        "ctx",
        scatter_dimension=0,
        tiled=True,
    ).astype(jnp.float32)
    grad_query_rows = jnp.transpose(grad_query * softmax_scale, (2, 0, 1, 3)).reshape(
        row_total, QUERY_HEADS, HEAD_SIZE
    )
    grad_query_normed = rotate_back(grad_query_rows, cosine_table, sine_table)
    gain_query_part = jnp.sum(grad_query_normed * query_normed, axis=(0, 1))
    grad_query_raw = (
        norm_back(grad_query_normed * query_gain, query_normed, query_inverse)
        .reshape(row_total, QUERY_HEADS * HEAD_SIZE)
        .astype(jnp.bfloat16)
    )
    key_row_grads = self_terms[:, 0, :].reshape(row_total, KEY_VALUE_HEADS, HEAD_SIZE)
    grad_key_normed = rotate_back(key_row_grads, cosine_table, sine_table)
    gain_key_part = jnp.sum(grad_key_normed * normalized_keys, axis=(0, 1))
    grad_key_raw = (
        norm_back(grad_key_normed * key_norm_gain, normalized_keys, key_inverse)
        .reshape(row_total, KEY_VALUE_HEADS * HEAD_SIZE)
        .astype(jnp.bfloat16)
    )
    grad_value_low = self_terms[:, 1, :].astype(jnp.bfloat16)
    grad_wquery = jnp.einsum(
        "tk,tq->kq", first_hidden, grad_query_raw, preferred_element_type=jnp.float32
    )
    grad_wkey = jnp.einsum(
        "tk,tq->kq", first_hidden, grad_key_raw, preferred_element_type=jnp.float32
    )
    grad_wvalue = jnp.einsum(
        "tk,tq->kq", first_hidden, grad_value_low, preferred_element_type=jnp.float32
    )
    grad_one = jnp.einsum(
        "tq,kq->tk", grad_query_raw, query_full, preferred_element_type=jnp.float32
    )
    grad_one = grad_one + jnp.einsum(
        "tq,kq->tk", grad_key_raw, key_full, preferred_element_type=jnp.float32
    )
    grad_one = grad_one + jnp.einsum(
        "tq,kq->tk", grad_value_low, value_full, preferred_element_type=jnp.float32
    )
    gain_one_part = jnp.sum(grad_one * normed_one, axis=0)
    grad_tokens = grad_resid + norm_back(grad_one * norm1_gain, normed_one, inverse_one)
    shard_grads = (
        lax.psum_scatter(
            grad_wquery.astype(jnp.bfloat16), "ctx", scatter_dimension=0, tiled=True
        ).astype(jnp.float32),
        lax.psum_scatter(
            grad_wkey.astype(jnp.bfloat16), "ctx", scatter_dimension=0, tiled=True
        ).astype(jnp.float32),
        lax.psum_scatter(
            grad_wvalue.astype(jnp.bfloat16), "ctx", scatter_dimension=0, tiled=True
        ).astype(jnp.float32),
        lax.psum_scatter(
            grad_wout.astype(jnp.bfloat16), "ctx", scatter_dimension=0, tiled=True
        ).astype(jnp.float32),
        lax.psum_scatter(
            grad_wgate.astype(jnp.bfloat16), "ctx", scatter_dimension=0, tiled=True
        ).astype(jnp.float32),
        lax.psum_scatter(
            grad_wup.astype(jnp.bfloat16), "ctx", scatter_dimension=0, tiled=True
        ).astype(jnp.float32),
        lax.psum_scatter(
            grad_down.astype(jnp.bfloat16), "ctx", scatter_dimension=0, tiled=True
        ).astype(jnp.float32),
    )
    shard_grads = (
        lax.psum(shard_grads[0].astype(jnp.bfloat16), "grp").astype(jnp.float32),
        lax.psum(shard_grads[1].astype(jnp.bfloat16), "grp").astype(jnp.float32),
        lax.psum(shard_grads[2].astype(jnp.bfloat16), "grp").astype(jnp.float32),
        lax.psum(shard_grads[3].astype(jnp.bfloat16), "grp").astype(jnp.float32),
        lax.psum(shard_grads[4].astype(jnp.bfloat16), "grp").astype(jnp.float32),
        lax.psum(shard_grads[5].astype(jnp.bfloat16), "grp").astype(jnp.float32),
        lax.psum(shard_grads[6].astype(jnp.bfloat16), "grp").astype(jnp.float32),
    )
    gain_grads = lax.psum(
        (gain_one_part, gain_query_part, gain_key_part, gain_two_part), ("grp", "ctx")
    )
    return (
        outcome.astype(jnp.bfloat16),
        grad_tokens,
        gain_grads[0],
        shard_grads[0],
        shard_grads[1],
        shard_grads[2],
        gain_grads[1],
        gain_grads[2],
        shard_grads[3],
        gain_grads[3],
        shard_grads[4],
        shard_grads[5],
        shard_grads[6],
    )


f32 = jnp.float32
bf16 = jnp.bfloat16
AXES = ("grp", "ctx")
N_GRP = 4
N_CTX = 8
SCALE = 1.0 / math.sqrt(HEAD_SIZE)
EXP2_SCALE = math.log2(math.e) / math.sqrt(HEAD_SIZE)
VMEM_LIMIT = 60 * 1024 * 1024
RUN = 8 * BLK
PROMPT_BLOCKS = PROMPT // BLK
CONT_BLOCKS = CONT_LEN // BLK
CHUNK = 5
HELD = RUN + CONT_LEN


def nt(a, b):
    return lax.dot_general(a, b, (((1,), (1,)), ((), ())), preferred_element_type=f32)


def nn(a, b):
    return jnp.dot(a, b, preferred_element_type=f32)


def tn(a, b):
    return lax.dot_general(a, b, (((0,), (0,)), ((), ())), preferred_element_type=f32)


def rows_at(start, size):
    return pl.ds(pl.multiple_of(start, size), size)


def turned(u):
    return pltpu.roll(u, HEAD_SIZE // 2, 1)


def head(i):
    return slice(i * HEAD_SIZE, (i + 1) * HEAD_SIZE)


def params():
    return pltpu.CompilerParams(vmem_limit_bytes=VMEM_LIMIT)


def whole_call(kernel, name, args, outs, scratch=()):
    smem = pl.BlockSpec(memory_space=pltpu.SMEM)
    vmem = pl.BlockSpec(memory_space=pltpu.VMEM)
    return pl.pallas_call(
        kernel,
        in_specs=[smem if a.dtype == jnp.int32 else vmem for a in args],
        out_specs=[vmem] * len(outs),
        out_shape=[jax.ShapeDtypeStruct(s, t) for s, t in outs],
        scratch_shapes=list(scratch),
        compiler_params=params(),
        name=name,
    )(*args)


def deal_kernel(table, rows_ref, *outs):
    for e in range(8):
        for i in range(CHUNK):
            outs[e][i * BLK : (i + 1) * BLK, :] = rows_ref[rows_at(table[e, i] * BLK, BLK), :]


def deal(table, rows):
    shape = (CHUNK * BLK, rows.shape[1])
    return whole_call(deal_kernel, "deal_rows", (table, rows), [(shape, rows.dtype)] * 8)


def deal_all_kernel(table, rows_ref, out_ref):
    for e in range(8):
        for i in range(CHUNK):
            out_ref[e, i * BLK : (i + 1) * BLK, :] = rows_ref[rows_at(table[e, i] * BLK, BLK), :]


def deal_all(table, rows):
    shape = (8, CHUNK * BLK, rows.shape[1])
    return whole_call(deal_all_kernel, "deal_all", (table, rows), [(shape, rows.dtype)])[0]


def place_all_kernel(table, pieces, out_ref, held):
    for e in range(8):
        for i in range(CHUNK):
            held[rows_at(table[e, i] * BLK, BLK), :] = pieces[e, i * BLK : (i + 1) * BLK, :]
    out_ref[...] = held[: out_ref.shape[0], :].astype(out_ref.dtype)


def place_all(table, pieces, n_rows, kind):
    shape = (n_rows, pieces.shape[2])
    return whole_call(
        place_all_kernel,
        "place_all",
        (table, pieces),
        [(shape, kind)],
        [pltpu.VMEM((n_rows + BLK, shape[1]), pieces.dtype)],
    )[0]


def place_kernel(table, *refs):
    pieces, out_ref, held = refs[:8], refs[8], refs[-1]
    for e in range(8):
        for i in range(CHUNK):
            held[rows_at(table[e, i] * BLK, BLK), :] = pieces[e][i * BLK : (i + 1) * BLK, :]
    out_ref[...] = held[: out_ref.shape[0], :].astype(out_ref.dtype)


def place(table, pieces, n_rows, kind):
    shape = (n_rows, pieces[0].shape[1])
    return whole_call(
        place_kernel,
        "place_rows",
        (table, *pieces),
        [(shape, kind)],
        [pltpu.VMEM((n_rows + BLK, shape[1]), pieces[0].dtype)],
    )[0]


def place_norm_kernel(table, *refs):
    gain_ref, out_ref, low_ref, held = refs[8:]
    place_kernel(table, *refs[:8], out_ref, held)
    normed, _ = normed_parts(out_ref[...].astype(f32))
    low_ref[...] = (normed * gain_ref[...]).astype(bf16)


def place_norm(table, pieces, gain, n_rows):
    shape = (n_rows, pieces[0].shape[1])
    return whole_call(
        place_norm_kernel,
        "place_rows_norm",
        (table, *pieces, gain),
        [(shape, bf16), (shape, bf16)],
        [pltpu.VMEM((n_rows + BLK, shape[1]), bf16)],
    )


def gathered_rows(info, pieces, w_ref):
    for e in range(8):
        w_ref[rows_at((info[0] ^ e) * 128, 128), :] = pieces[e][...]


def lane_mean(u):
    ones = jnp.full((HEAD_SIZE, HEAD_SIZE), 1.0 / HEAD_SIZE, bf16)
    high = u.astype(bf16)
    return nn(high, ones) + nn((u - high.astype(f32)).astype(bf16), ones)


def head_normed(u):
    inverse = lax.rsqrt(lane_mean(u * u) + eps)
    return u * inverse, inverse


def query_kernel(info, h_ref, *refs):
    gain_ref, cos_ref, sin_ref, q_ref, raw_ref, w_ref = refs[8:]
    gathered_rows(info, refs[:8], w_ref)
    acc = nn(h_ref[...], w_ref[...])
    raw_ref[...] = acc
    for i in range(2):
        normed, _ = head_normed(acc[:, head(i)])
        u = normed * gain_ref[...]
        q_ref[:, head(i)] = (u * cos_ref[...] + turned(u) * sin_ref[...]).astype(bf16)


def key_value_kernel(info, h_ref, *refs):
    gain_ref, cos_ref, sin_ref, kv_ref, raw_ref, w_ref, send_ref = refs[8:]
    gathered_rows(info, refs[:8], w_ref)
    acc = nn(h_ref[...], w_ref[...])
    raw_ref[...] = acc[:, head(0)]
    normed, _ = head_normed(acc[:, head(0)])
    u = normed * gain_ref[...]
    kv_ref[:, head(0)] = (u * cos_ref[...] + turned(u) * sin_ref[...]).astype(bf16)
    kv_ref[:, head(1)] = acc[:, head(1)].astype(bf16)
    for b in range(2):
        send_ref[b * RUN : (b + 1) * RUN, :] = kv_ref[b * HELD : b * HELD + RUN, :]


def project(kernel, name, info, hidden, pieces, first, gain, cos, sin, raw_width, extra):
    rows, width = hidden.shape

    def still(g, s):
        return (0, 0)

    def moving(g, s):
        return (0, g)

    return pl.pallas_call(
        kernel,
        grid_spec=pltpu.PrefetchScalarGridSpec(
            num_scalar_prefetch=1,
            grid=(4,),
            in_specs=[pl.BlockSpec((rows, width), still)]
            + [pl.BlockSpec((128, 256), lambda g, s: (0, g + first))] * 8
            + [
                pl.BlockSpec((1, HEAD_SIZE), still),
                pl.BlockSpec((rows, HEAD_SIZE), still),
                pl.BlockSpec((rows, HEAD_SIZE), still),
            ],
            out_specs=[
                pl.BlockSpec((rows, 256), moving),
                pl.BlockSpec((rows, raw_width), moving),
                pl.BlockSpec((width, 256), moving),
            ]
            + [pl.BlockSpec((2 * RUN, 256), moving)] * extra,
        ),
        out_shape=[
            jax.ShapeDtypeStruct((rows, 1024), bf16),
            jax.ShapeDtypeStruct((rows, 4 * raw_width), f32),
            jax.ShapeDtypeStruct((width, 1024), bf16),
        ]
        + [jax.ShapeDtypeStruct((2 * RUN, 1024), bf16)] * extra,
        compiler_params=params(),
        name=name,
    )(info, hidden, *pieces, gain, cos, sin)


def seen_in_prompt(info, half):
    key = lax.broadcasted_iota(jnp.int32, (PROMPT, RUN), 0)
    tile = key // RUN
    run = info[3] ^ (tile // 2 + 4 * (tile % 2))
    row = lax.broadcasted_iota(jnp.int32, (PROMPT, RUN), 1) + (info[3] ^ (4 * half)) * RUN
    return run * RUN + key % RUN <= row


def seen_in_own():
    key = lax.broadcasted_iota(jnp.int32, (CONT_LEN, CONT_LEN), 0)
    row = lax.broadcasted_iota(jnp.int32, (CONT_LEN, CONT_LEN), 1)
    return key <= row


LSE_SPAN = 640


def units():
    for b in range(2):
        yield b, b * HELD + RUN, CONT_LEN, b * LSE_SPAN, False
    for b in range(2):
        yield b, b * HELD, RUN, b * LSE_SPAN + 512, True


def attn_fwd_kernel(info, q_ref, kv_ref, p0, p1, p2, p3, o_ref, lse_ref, p_ref):
    for t, p in enumerate((p0, p1, p2, p3)):
        p_ref[t * 2 * RUN : (t + 1) * 2 * RUN, :] = p[...]
    prompt = (p_ref[:, head(0)], jnp.transpose(p_ref[:, head(1)]))
    for b, row0, n, lane, in_prompt in units():
        own = slice(row0, row0 + n)
        tiles = [(*prompt, seen_in_prompt(info, b) if in_prompt else None)]
        if not in_prompt:
            tiles.append((kv_ref[own, head(0)], jnp.transpose(kv_ref[own, head(1)]), seen_in_own()))
        for i in range(2):
            q = q_ref[own, head(i)]
            total = jnp.zeros((1, n), f32)
            mixed = jnp.zeros((HEAD_SIZE, n), f32)
            for keys, values_t, seen in tiles:
                p = jnp.exp2(nt(keys, q) * EXP2_SCALE)
                if seen is not None:
                    p = jnp.where(seen, p, 0.0)
                total = total + jnp.sum(p, axis=0, keepdims=True)
                mixed = mixed + nn(values_t, p.astype(bf16))
            o_ref[own, head(i)] = jnp.transpose(mixed / total).astype(bf16)
            lse_ref[0, i : i + 1, lane : lane + n] = jnp.log2(total)


def attn_specs(rows, *names):
    specs = {
        "wide": pl.BlockSpec((rows, 256), lambda g, s: (0, g)),
        "head": pl.BlockSpec((rows, HEAD_SIZE), lambda g, s: (0, g)),
        "prompt": pl.BlockSpec((2 * RUN, 256), lambda g, s: (0, g)),
        "lse": pl.BlockSpec((1, 8, 2 * LSE_SPAN), lambda g, s: (g, 0, 0)),
        "table": pl.BlockSpec((rows, HEAD_SIZE), lambda g, s: (0, 0)),
        "gain": pl.BlockSpec((1, HEAD_SIZE), lambda g, s: (0, 0)),
        "gains": pl.BlockSpec((8, HEAD_SIZE), lambda g, s: (0, 0)),
    }
    return [specs[n] for n in names]


def attn_fwd(info, q, kv, prompt):
    rows = q.shape[0]
    return pl.pallas_call(
        attn_fwd_kernel,
        grid_spec=pltpu.PrefetchScalarGridSpec(
            num_scalar_prefetch=1,
            grid=(4,),
            in_specs=attn_specs(rows, "wide", "wide", *["prompt"] * 4),
            out_specs=attn_specs(rows, "wide", "lse"),
            scratch_shapes=[pltpu.VMEM((PROMPT, 256), bf16)],
        ),
        out_shape=[
            jax.ShapeDtypeStruct((rows, 1024), bf16),
            jax.ShapeDtypeStruct((4, 8, 2 * LSE_SPAN), f32),
        ],
        compiler_params=params(),
        cost_estimate=pl.CostEstimate(flops=20*10**9, bytes_accessed=10**7, transcendentals=0),
        name="attn_fwd",
    )(info, q, kv, *prompt)


def key_back(grad, raw, cos, sin, gain):
    normed, inverse = normed_parts(raw)
    grad = grad * SCALE
    back = grad * cos - turned(grad) * sin
    part = jnp.sum(back * normed, axis=0, keepdims=True)
    return norm_back(back * gain, normed, inverse).astype(bf16), part


def attn_bwd_kernel(info, q_ref, kv_ref, p0, p1, p2, p3, *refs):
    do_ref, o_ref, lse_ref, rawq_ref, rawk_ref, qg_ref, kg_ref, cos_ref, sin_ref = refs[:9]
    dq_ref, dkv_ref, d0, d1, d2, d3, gains_ref, dk_ref, dv_ref, p_ref = refs[9:]
    for t, p in enumerate((p0, p1, p2, p3)):
        p_ref[t * 2 * RUN : (t + 1) * 2 * RUN, :] = p[...]
    prompt = (p_ref[:, head(0)], jnp.transpose(p_ref[:, head(0)]), p_ref[:, head(1)])

    @pl.when(pl.program_id(0) == 0)
    def first():
        gains_ref[...] = jnp.zeros_like(gains_ref)

    for number, (b, row0, n, lane, in_prompt) in enumerate(units()):
        own = slice(row0, row0 + n)
        cos, sin = cos_ref[own, :], sin_ref[own, :]
        tiles = [(*prompt, seen_in_prompt(info, b) if in_prompt else None, True)]
        if not in_prompt:
            keys = kv_ref[own, head(0)]
            tiles.append((keys, jnp.transpose(keys), kv_ref[own, head(1)], seen_in_own(), False))
        own_dk = own_dv = 0.0
        for i in range(2):
            q, do = q_ref[own, head(i)], do_ref[own, head(i)]
            lse = lse_ref[0, i : i + 1, lane : lane + n]
            product = do.astype(f32) * o_ref[own, head(i)].astype(f32)
            delta = jnp.sum(jnp.transpose(product), axis=0, keepdims=True)
            dq = jnp.zeros((HEAD_SIZE, n), f32)
            for keys, keys_t, values, seen, shared in tiles:
                p = jnp.exp2(nt(keys, q) * EXP2_SCALE - lse)
                if seen is not None:
                    p = jnp.where(seen, p, 0.0)
                ds = (p * (nt(values, do) - delta)).astype(bf16)
                dk, dv = nn(ds, q), nn(p.astype(bf16), do)
                dq = dq + nn(keys_t, ds)
                if not shared:
                    own_dk, own_dv = own_dk + dk, own_dv + dv
                elif number == 0 and i == 0:
                    dk_ref[...] = dk
                    dv_ref[...] = dv
                else:
                    dk_ref[...] += dk
                    dv_ref[...] += dv
            back, part = key_back(jnp.transpose(dq), rawq_ref[own, head(i)], cos, sin, qg_ref[...])
            dq_ref[own, head(i)] = back
            gains_ref[0:1, :] += part
        if not in_prompt:
            back, part = key_back(own_dk, rawk_ref[own, :], cos, sin, kg_ref[...])
            dkv_ref[own, head(0)] = back
            dkv_ref[own, head(1)] = own_dv.astype(bf16)
            gains_ref[1:2, :] += part
        else:
            dkv_ref[own, :] = jnp.zeros((n, 256), bf16)
    for t, ref in enumerate((d0, d1, d2, d3)):
        ref[:, head(0)] = dk_ref[t * 256 : (t + 1) * 256, :].astype(bf16)
        ref[:, head(1)] = dv_ref[t * 256 : (t + 1) * 256, :].astype(bf16)


def attn_bwd(info, q, kv, prompt, do, o, lse, rawq, rawk, qg, kg, cos, sin):
    rows = q.shape[0]
    return pl.pallas_call(
        attn_bwd_kernel,
        grid_spec=pltpu.PrefetchScalarGridSpec(
            num_scalar_prefetch=1,
            grid=(4,),
            in_specs=attn_specs(rows, "wide", "wide", *["prompt"] * 4, "wide", "wide", "lse")
            + attn_specs(rows, "wide", "head", "gain", "gain", "table", "table"),
            out_specs=attn_specs(rows, "wide", "wide", *["prompt"] * 4, "gains"),
            scratch_shapes=[pltpu.VMEM((PROMPT, HEAD_SIZE), f32)] * 2
            + [pltpu.VMEM((PROMPT, 256), bf16)],
        ),
        out_shape=[jax.ShapeDtypeStruct((rows, 1024), bf16)] * 2
        + [jax.ShapeDtypeStruct((2 * RUN, 1024), bf16)] * 4
        + [jax.ShapeDtypeStruct((8, HEAD_SIZE), f32)],
        compiler_params=params(),
        cost_estimate=pl.CostEstimate(flops=45*10**9, bytes_accessed=10**7, transcendentals=0),
        name="attn_bwd",
    )(info, q, kv, *prompt, do, o, lse, rawq, rawk, qg, kg, cos, sin)


def prompt_back_kernel(d0, d1, d2, d3, dkv_ref, raw_ref, kg_ref, cos_ref, sin_ref, out_ref, gains_ref):
    out_ref[...] = dkv_ref[...]
    gains_ref[...] = jnp.zeros_like(gains_ref)
    for b in range(2):
        rows = slice(b * RUN, (b + 1) * RUN)
        own = slice(b * HELD, b * HELD + RUN)
        for h in range(4):
            cols = slice(h * 256, (h + 1) * 256)
            total = sum(d[rows, cols].astype(f32) for d in (d0, d1, d2, d3))
            back, part = key_back(
                total[:, head(0)], raw_ref[own, head(h)], cos_ref[own, :], sin_ref[own, :], kg_ref[...]
            )
            out_ref[own, h * 256 : h * 256 + 128] = back
            out_ref[own, h * 256 + 128 : (h + 1) * 256] = total[:, head(1)].astype(bf16)
            gains_ref[0:1, :] += part


def out_kernel(info, o_ref, *refs):
    pieces, (own_ref, sib_ref, w_ref) = refs[:2], refs[2:]
    for t in range(4):
        w_ref[rows_at((info[4] ^ t) * 256, 256), :] = pieces[t % 2][t // 2]
    half = own_ref.shape[0]
    own_ref[...] = nn(o_ref[:half, :], w_ref[...])
    sib_ref[...] = nn(o_ref[half:, :], w_ref[...]).astype(bf16)


def mlp_kernel(info, h_own, h_sib, g_own, g_sib, *refs):
    w2, w3 = refs[:10], refs[10:14]
    hid_ref, dgu_ref, out_ref, outs_ref, dh_ref, dhs_ref = refs[14:20]
    w_ref, wd_ref, out_acc, dh_acc = refs[20:]
    step = pl.program_id(0)
    ff = hid_ref.shape[1]
    half = out_ref.shape[0]
    for e in range(8):
        row = (info[0] ^ e) * 128
        w_ref[rows_at(row + info[1] * 64, 64), :] = w2[e][...]
        w_ref[rows_at(row + (1 - info[1]) * 64, 64), :] = w2[8 + e // 4][e % 4]
    for t in range(4):

        @pl.when(step == t)
        def take(t=t):
            wd_ref[...] = w3[t][...]

    @pl.when(step == 0)
    def zero():
        for ref in (out_ref, dh_ref, out_acc, dh_acc):
            ref[...] = jnp.zeros_like(ref)

    sides = ((h_own, g_own, out_ref, dh_ref), (h_sib, g_sib, out_acc, dh_acc))
    for b, (h_ref, g_ref, out, dh) in enumerate(sides):
        rows = slice(b * half, (b + 1) * half)
        both = nn(h_ref[...], w_ref[...])
        gate, up = both[:, :ff], both[:, ff:]
        sig = jax.nn.sigmoid(gate)
        silu = gate * sig
        hid = (silu * up).astype(bf16)
        hid_ref[rows, :] = hid
        dhid = nt(g_ref[...], wd_ref[...])
        dgu_ref[rows, :ff] = (dhid * up * sig * (1.0 + gate * (1.0 - sig))).astype(bf16)
        dgu_ref[rows, ff:] = (dhid * silu).astype(bf16)
        dh[...] += nt(dgu_ref[rows, :], w_ref[...])
        out[...] += nn(hid, wd_ref[...])

    @pl.when(step == 3)
    def finish():
        outs_ref[...] = out_acc[...].astype(bf16)
        dhs_ref[...] = dh_acc[...].astype(bf16)


def mlp(info, hidden, grad, w2, w3, ff):
    half, width = hidden[0].shape
    rows = 2 * half
    once = pl.Buffered(1)

    def still(shape):
        return pl.BlockSpec(shape, lambda g, s: (0, 0), pipeline_mode=once)

    return pl.pallas_call(
        mlp_kernel,
        grid_spec=pltpu.PrefetchScalarGridSpec(
            num_scalar_prefetch=1,
            grid=(4,),
            in_specs=[still((half, width))] * 4
            + [pl.BlockSpec((64, 2 * ff), lambda g, s: (0, s[4] ^ g))] * 8
            + [pl.BlockSpec((4, 64, 2 * ff), lambda g, s: (0, 0, s[4] ^ g))] * 2
            + [still(w3[0].shape)] * 4,
            out_specs=[
                pl.BlockSpec((rows, ff), lambda g, s: (0, s[4] ^ g)),
                pl.BlockSpec((rows, 2 * ff), lambda g, s: (0, s[4] ^ g)),
            ]
            + [pl.BlockSpec((half, width), lambda g, s: (0, 0))] * 4,
            scratch_shapes=[
                pltpu.VMEM((width, 2 * ff), bf16),
                pltpu.VMEM((ff, width), bf16),
                pltpu.VMEM((half, width), f32),
                pltpu.VMEM((half, width), f32),
            ],
        ),
        out_shape=[
            jax.ShapeDtypeStruct((rows, 4 * ff), bf16),
            jax.ShapeDtypeStruct((rows, 8 * ff), bf16),
            jax.ShapeDtypeStruct((half, width), f32),
            jax.ShapeDtypeStruct((half, width), bf16),
            jax.ShapeDtypeStruct((half, width), f32),
            jax.ShapeDtypeStruct((half, width), bf16),
        ],
        compiler_params=params(),
        cost_estimate=pl.CostEstimate(flops=38*10**9, bytes_accessed=10**7, transcendentals=0),
        name="feed_forward",
    )(info, *hidden, *grad, *w2, *w3)


def gate_up_kernel(info, own_ref, sib_ref, gate_ref, up_ref):
    ff = own_ref.shape[1] // 8
    for first, (low, high) in ((0, (own_ref, sib_ref)), (1, (sib_ref, own_ref))):

        @pl.when(info[2] == first)
        def write(low=low, high=high):
            for c, ref in enumerate((low, high)):
                for b in range(4):
                    cols = slice((c * 4 + b) * ff, (c * 4 + b + 1) * ff)
                    gate_ref[:, cols] = ref[:, 2 * b * ff : (2 * b + 1) * ff].astype(f32)
                    up_ref[:, cols] = ref[:, (2 * b + 1) * ff : (2 * b + 2) * ff].astype(f32)


def attn_weights_kernel(info, own_ref, sib_ref, query_ref, key_ref, value_ref):
    for first, (low, high) in ((0, (own_ref, sib_ref)), (1, (sib_ref, own_ref))):

        @pl.when(info[2] == first)
        def write(low=low, high=high):
            for c, ref in enumerate((low, high)):
                query_ref[:, c * 1024 : (c + 1) * 1024] = ref[:, :1024].astype(f32)
                for h in range(4):
                    start = 1024 + h * 256
                    to = head(c * 4 + h)
                    key_ref[:, to] = ref[:, start : start + 128].astype(f32)
                    value_ref[:, to] = ref[:, start + 128 : start + 256].astype(f32)


def device_of(y, core, z_hi, z_lo, x):
    return (y * 2 + core) * N_CTX + z_hi * 4 + z_lo * 2 + x


def bits_of(i):
    return ((i >> 4) & 1, (i >> 3) & 1, (i >> 2) & 1, (i >> 1) & 1, i & 1)


def permutation(target, sends=lambda *bits: True):
    devices = range(N_GRP * N_CTX)
    return [(i, device_of(*target(*bits_of(i)))) for i in devices if sends(*bits_of(i))]


def member_device(e):
    def target(y, core, z_hi, z_lo, x):
        m = (z_hi * 4 + z_lo * 2 + x) ^ e
        return (y, m >> 2, core, (m >> 1) & 1, m & 1)

    return target


SPREAD = [permutation(member_device(e)) for e in range(8)]
COLLECT = [[(b, a) for a, b in pairs] for pairs in SPREAD]
HALVES = permutation(
    lambda y, core, z_hi, z_lo, x: (y, z_hi, core, z_lo, x),
    lambda y, core, z_hi, z_lo, x: z_hi != core,
)
CUBES = [
    [device_of(y, m >> 2, z_hi, (m >> 1) & 1, m & 1) for m in range(8)]
    for y in range(2)
    for z_hi in range(2)
]
OVER_Y = permutation(lambda y, core, z_hi, z_lo, x: (1 - y, core, z_hi, z_lo, x))
SIBLING = permutation(lambda y, core, z_hi, z_lo, x: (y, 1 - core, z_hi, z_lo, x))
OVER_Y_HOME = permutation(
    lambda y, core, z_hi, z_lo, x: (1 - y, core, z_hi, z_lo, x),
    lambda y, core, z_hi, z_lo, x: z_hi == core,
)
MIDDLE = permutation(lambda y, core, z_hi, z_lo, x: (y, core, 1 - z_hi, z_lo, x))
MIDDLE_OUT = permutation(
    lambda y, core, z_hi, z_lo, x: (y, core, 1 - z_hi, z_lo, x),
    lambda y, core, z_hi, z_lo, x: z_hi == core,
)
MIDDLE_IN = permutation(
    lambda y, core, z_hi, z_lo, x: (y, core, 1 - z_hi, z_lo, x),
    lambda y, core, z_hi, z_lo, x: z_hi != core,
)
CHIP = [
    permutation(
        lambda y, core, z_hi, z_lo, x, t=t: (y, core, z_hi, z_lo ^ (t >> 1), x ^ (t & 1))
    )
    for t in range(4)
]


def permute(a, pairs):
    return lax.ppermute(a, AXES, pairs)


def pick(a, i, axis=0):
    return lax.dynamic_index_in_dim(a, i, axis, keepdims=False)


def added(*terms):
    return sum(t.astype(f32) for t in terms).astype(bf16)


def after(a, b):
    return lax.optimization_barrier((a, b))[0]


def together(*arrays):
    return lax.optimization_barrier(arrays)


def in_order(first, mine, other):
    return [jnp.where(first, mine, other), jnp.where(first, other, mine)]


def shards_split(
    tokens,
    block_table,
    norm1_gain,
    w_query,
    key_weight,
    value_weight,
    query_gain,
    key_norm_gain,
    w_out,
    norm2_gain,
    w_gate,
    w_up,
    w_down,
    out_grad,
):
    row_total, width = tokens.shape
    n_slots = row_total // BLK
    ff = w_gate.shape[1] // 8
    position = lax.axis_index("ctx").astype(jnp.int32)
    group_index = lax.axis_index("grp").astype(jnp.int32)
    y, core = group_index // 2, group_index % 2
    z_hi, chip = position // 4, position % 4
    z_lo, x = chip // 2, chip % 2
    member = core * 4 + chip
    info = jnp.stack([position, y, core, member, chip])
    at_home = z_hi == core
    qg, kg = query_gain.reshape(1, HEAD_SIZE), key_norm_gain.reshape(1, HEAD_SIZE)

    eight = jnp.arange(8, dtype=jnp.int32)
    five = jnp.arange(CHUNK, dtype=jnp.int32)[None, :]

    def slots_of(m):
        m = m.reshape(-1, 1)
        return jnp.where(five == 0, m, 7 + 7 * (m // 2) + 3 * (m % 2) + five)

    def held_at(natural, m):
        inside = natural - (PROMPT_BLOCKS + CONT_BLOCKS * m)
        valid = (five == 0) | ((inside >= 0) & (inside < CONT_BLOCKS))
        return jnp.where(valid, jnp.where(five == 0, natural - 8 * m, 8 + inside), n_slots), valid

    def look_up(rows, slots):
        match = slots[:, :, None] == jnp.arange(n_slots, dtype=jnp.int32)
        return jnp.sum(jnp.where(match, rows[:, None, :], 0), axis=2)

    tables = block_table.reshape(8, n_slots)
    send_slots = slots_of(position ^ eight)
    from_tables = jnp.concatenate(
        [lax.dynamic_slice_in_dim(tables, member ^ e, 1, 0) for e in range(8)], axis=0
    )
    arrive, _ = held_at(look_up(from_tables, jnp.broadcast_to(slots_of(member), (8, CHUNK))), member)
    leave = jnp.minimum(arrive, n_slots - 1)
    own_table = lax.dynamic_slice_in_dim(tables, position, 1, 0)
    _, valid = held_at(look_up(own_table, send_slots), (position ^ eight).reshape(-1, 1))
    home_slots = jnp.where(valid, send_slots, n_slots)

    def spread(a):
        return [permute(c, pairs) for c, pairs in zip(deal(send_slots, a), SPREAD)]

    def collect(a, kind):
        pieces = [permute(c, pairs) for c, pairs in zip(deal(leave, a), COLLECT)]
        return place(home_slots, pieces, row_total, kind)

    def regrouped(a):
        return jnp.where(at_home, a, permute(a, HALVES))

    def both(a):
        return jnp.concatenate([a, permute(a, SIBLING)], axis=0)

    def columns(w, parts):
        return pick(w.reshape(w.shape[0], 2, 4, -1), core, 1)

    own_one = jnp.concatenate(
        [
            columns(w_query, 2).reshape(-1, 1024),
            jnp.concatenate([columns(key_weight, 2), columns(value_weight, 2)], axis=2).reshape(
                -1, 1024
            ),
        ],
        axis=1,
    )
    own_two = jnp.concatenate([columns(w_gate, 2), columns(w_up, 2)], axis=2)
    own_two = pick(own_two.reshape(2, 64, 8 * ff), y)
    own_out, own_down = w_out, w_down

    def around(a):
        return [a] + [permute(a, CHIP[t]) for t in range(1, 4)]

    one = around(own_one)
    middle_one = permute(own_one, MIDDLE)
    arrived = spread(tokens)
    one = one + around(middle_one)

    cosine, sine = rotation(jnp.arange(PROMPT + CONT_LEN, dtype=jnp.int32))
    cos = jnp.concatenate([cosine[:, 0], cosine[:, 0]], axis=1)
    sin = jnp.concatenate([-sine[:, 0], sine[:, 0]], axis=1)

    def of_rows(table):
        parts = []
        for m in (member, member ^ 4):
            parts += [lax.dynamic_slice_in_dim(table, m * RUN, RUN, 0), table[PROMPT:]]
        return jnp.concatenate(parts, axis=0)

    cos, sin = of_rows(cos), of_rows(sin)

    inputs_low, first_low = place_norm(arrive, arrived, norm1_gain.reshape(1, width), row_total)
    hidden_one = both(first_low)
    own_two, w_out, w_down, out_grad = together(own_two, w_out, w_down, out_grad, first_low)[:4]
    middle_out = permute(after(w_out, one[:4]), MIDDLE_OUT)
    hidden_one, middle_out, own_two, w_down, out_grad, *one = together(
        hidden_one, middle_out, own_two, w_down, out_grad, *one
    )
    home_out = jnp.where(at_home, w_out, middle_out)

    two = around(own_two)
    middle_two = permute(own_two, MIDDLE)
    outs = jnp.stack([home_out, permute(home_out, CHIP[2])])
    kv, rawk, w_kv, prompt_kv = project(
        key_value_kernel, "key_value", info, hidden_one, one, 4, kg, cos, sin, HEAD_SIZE, 1
    )
    prompt_kv, outs, out_grad, hidden_q, middle_two, *two = together(
        prompt_kv, outs, out_grad, hidden_one, middle_two, *two
    )

    prompt = around(prompt_kv)
    outs = [outs, permute(outs, CHIP[1])]
    grad_here = regrouped(out_grad)
    q, rawq, w_q = project(query_kernel, "query", info, hidden_q, one, 0, qg, cos, sin, 256, 0)
    q, grad_here, middle_two, w_down, *rest = together(
        q, grad_here, middle_two, w_down, *outs, *prompt
    )
    outs, prompt = rest[:2], rest[2:]

    two += around(middle_two)
    other_two = [permute(jnp.stack(two[:4]), OVER_Y)]
    middle_down = permute(w_down, MIDDLE_OUT)
    mixed, lse = attn_fwd(info, q, kv, prompt)
    home_down = jnp.where(at_home, w_down, middle_down)
    mixed, home_down, grad_here, *rest = together(mixed, home_down, grad_here, *two, *other_two)
    two, other_two = rest[:8], rest[8:]

    other_two.append(permute(jnp.stack(two[4:]), OVER_Y))
    downs = around(home_down)
    chunk_starts = [8 + 7 * (m // 2) + 3 * (m % 2) for m in range(8)]
    grad_here = jnp.concatenate(
        [
            grad_here[: 8 * BLK].reshape(8, BLK, width),
            jnp.stack([grad_here[start * BLK : (start + 4) * BLK] for start in chunk_starts]),
        ],
        axis=1,
    )

    def swap_cube(a):
        return lax.all_to_all(a, AXES, 0, 0, tiled=True, axis_index_groups=CUBES)

    grad_here = swap_cube(grad_here)
    in_turn = jnp.concatenate(
        [lax.dynamic_slice_in_dim(arrive, member ^ e, 1, 0) for e in range(8)], axis=0
    )
    leave_in_turn = jnp.minimum(in_turn, n_slots - 1)
    home_in_turn = jnp.concatenate(
        [lax.dynamic_slice_in_dim(home_slots, position ^ e, 1, 0) for e in range(8)], axis=0
    )

    rows_kind = ((row_total, width), f32), ((row_total, width), bf16)
    out_own, out_sib, w_o = whole_call(
        out_kernel,
        "out_projection",
        (info, mixed, *outs),
        [*rows_kind, ((1024, width), bf16)],
    )
    inputs = inputs_low.astype(f32)
    resid_one = inputs + out_own + permute(out_sib, SIBLING).astype(f32)
    normed_two, inverse_two = normed_parts(resid_one)
    hidden_two = (normed_two * norm2_gain).astype(bf16)
    hidden_two, other_far, *downs = together(hidden_two, other_two[1], *downs)
    other_two = [other_two[0], other_far]
    hidden_two = [hidden_two, permute(hidden_two, SIBLING)]
    grad_low = place_all(in_turn, grad_here, row_total, bf16)
    grad_both = [grad_low, permute(grad_low, SIBLING)]
    hid, grad_gu, ff_own, ff_sib, back_own, back_sib = mlp(
        info, hidden_two, grad_both, two + other_two, downs, ff
    )
    hidden_two = jnp.concatenate(hidden_two, axis=0)
    grad_both = jnp.concatenate(grad_both, axis=0)
    grad_two = back_own + permute(back_sib, SIBLING).astype(f32)
    gain_two_part = jnp.sum(grad_two * normed_two, axis=0)
    grad_resid = grad_low.astype(f32) + norm_back(grad_two * norm2_gain, normed_two, inverse_two)
    grad_attn = both(grad_resid.astype(bf16))

    def chip_parts(grad):
        grad = grad.reshape(8, -1, grad.shape[-1])
        return [
            jnp.stack([pick(grad, position ^ t), pick(grad, position ^ (4 + t))]) for t in range(4)
        ]

    def sent_to_chips(parts):
        return [permute(parts[t], CHIP[t]) for t in range(1, 4)]

    def from_middle(part):
        return added(pick(part, z_hi), permute(pick(part, 1 - z_hi), MIDDLE))

    def halved(grad, axis, bit, pairs):
        return added(pick(grad, bit, axis), permute(pick(grad, 1 - bit, axis), pairs))

    grad_two_w = tn(hidden_two, grad_gu).astype(bf16).reshape(2, 2, 2, 2, 64, -1)
    keep_two, send_two = pick(grad_two_w, y, 3), pick(grad_two_w, 1 - y, 3)
    send_two = permute(send_two, OVER_Y)
    grad_down = tn(hid, grad_both).astype(bf16).reshape(2, 2, -1, width)
    grad_out = tn(mixed, grad_attn).astype(bf16).reshape(2, 2, -1, width)
    outcome = resid_one + ff_own + permute(ff_sib, SIBLING).astype(f32)
    leaving = deal_all(leave_in_turn, outcome.astype(bf16))
    grad_attn, grad_down, grad_out, leaving, _ = together(
        grad_attn, grad_down, grad_out, leaving, keep_two
    )
    keep_down, send_down = pick(grad_down, x, 1), permute(pick(grad_down, 1 - x, 1), CHIP[1])
    keep_out, send_out = pick(grad_out, z_lo), permute(pick(grad_out, 1 - z_lo), CHIP[2])
    leaving = swap_cube(leaving)
    grad_mixed = nt(grad_attn, w_o).astype(bf16)
    grad_q, grad_kv, *prompt_parts, gains = attn_bwd(
        info, q, kv, prompt, grad_mixed, mixed, lse, rawq, rawk, qg, kg, cos, sin
    )
    grad_q, grad_kv, send_down, send_out, leaving, *prompt_parts = together(
        grad_q, grad_kv, send_down, send_out, leaving, *prompt_parts
    )

    prompt_parts = [prompt_parts[0]] + [permute(prompt_parts[t], CHIP[t]) for t in range(1, 4)]
    grad_wq = tn(hidden_one, grad_q).astype(bf16).reshape(8, 2, 64, -1)
    keep_q, send_q = pick(grad_wq, y, 1), permute(pick(grad_wq, 1 - y, 1), OVER_Y)
    grad_q, keep_q, send_q, send_down, send_out, send_two, leaving, *prompt_parts = together(
        grad_q, keep_q, send_q, send_down, send_out, send_two, leaving, *prompt_parts
    )
    left = regrouped(leaving.reshape(-1, width))
    sum_two = added(keep_two, send_two)
    down, out = added(keep_down, send_down), added(keep_out, send_out)
    down = halved(down, 0, z_lo, CHIP[2])
    out = halved(out, 0, x, CHIP[1])
    sum_two = halved(sum_two, 2, x, CHIP[1])
    grad_kv, key_gains = whole_call(
        prompt_back_kernel,
        "prompt_back",
        (*prompt_parts, grad_kv, rawk, kg, cos, sin),
        [(grad_kv.shape, bf16), ((8, HEAD_SIZE), f32)],
    )
    grad_wkv = tn(hidden_one, grad_kv).astype(bf16).reshape(8, 2, 64, -1)
    grad_one = nt(grad_q, w_q) + nt(after(grad_kv, grad_wkv), w_kv)
    grad_one, sum_two = together(grad_one, sum_two)
    grad_one = grad_one[:row_total] + permute(
        grad_one[row_total:].astype(bf16), SIBLING
    ).astype(f32)
    normed_one, inverse_one = normed_parts(inputs)
    gain_one_part = jnp.sum(grad_one * normed_one, axis=0)
    grad_tokens = grad_resid + norm_back(grad_one * norm1_gain, normed_one, inverse_one)
    going = deal_all(leave_in_turn, grad_tokens.astype(bf16))
    gain_grads = jnp.concatenate(
        [gain_one_part, gain_two_part, gains[0], gains[1] + key_gains[0]]
    ).reshape(-1, HEAD_SIZE)
    going, gain_grads, down, out, keep_q, send_q, grad_wkv, left, sum_two = together(
        going, gain_grads, down, out, keep_q, send_q, grad_wkv, left, sum_two
    )
    going = swap_cube(going)
    q_parts = chip_parts(added(keep_q, send_q))
    q_sent = sent_to_chips(q_parts)
    keep_kv, send_kv = pick(grad_wkv, y, 1), permute(pick(grad_wkv, 1 - y, 1), OVER_Y)
    three = jnp.concatenate([down, out], axis=0)
    three = added(three, permute(three, MIDDLE_IN))
    gain_grads = gain_grads + permute(gain_grads, SIBLING)
    outcome = place_all(home_in_turn, left.reshape(8, -1, width), row_total, bf16)
    going, gain_grads, outcome, keep_kv, send_kv, sum_two, *q_sent = together(
        going, gain_grads, outcome, keep_kv, send_kv, sum_two, *q_sent
    )
    going = regrouped(going.reshape(-1, width))
    sum_two = halved(sum_two, 1, z_lo, CHIP[2])
    gain_grads = gain_grads + permute(gain_grads, CHIP[1])
    kv_parts = chip_parts(added(keep_kv, send_kv))
    kv_sent = sent_to_chips(kv_parts)
    part_q = added(q_parts[0], *q_sent)
    going, gain_grads, sum_two, three, *kv_sent = together(
        going, gain_grads, sum_two, three, *kv_sent
    )
    gain_grads = gain_grads + permute(gain_grads, CHIP[2])
    grad_tokens = place_all(home_in_turn, going.reshape(8, -1, width), row_total, f32)
    part_kv = added(kv_parts[0], *kv_sent)
    sum_one = jnp.concatenate([part_q, part_kv], axis=2)
    sum_one = added(sum_one[0], permute(sum_one[1], MIDDLE))
    three = added(three, permute(three, OVER_Y_HOME))
    sum_two = from_middle(sum_two)
    sum_one, sum_two, three, gain_grads = together(sum_one, sum_two, three, gain_grads)
    sum_two = jnp.concatenate(in_order(y == 0, sum_two, permute(sum_two, OVER_Y)), axis=0)
    gain_grads = gain_grads + permute(gain_grads, OVER_Y)
    sum_one = jnp.concatenate(in_order(y == 0, sum_one, permute(sum_one, OVER_Y)), axis=0)
    total = jnp.where(at_home, three, permute(three, SIBLING)).astype(f32)
    sum_one, sum_two, gain_grads = together(sum_one, sum_two, gain_grads)
    gain_grads = gain_grads + permute(gain_grads, MIDDLE)
    shard = sum_two.shape[0]
    gate_grad, up_grad = whole_call(
        gate_up_kernel,
        "gate_up_gradients",
        (info, sum_two, permute(sum_two, SIBLING)),
        [((shard, 8 * ff), f32)] * 2,
    )
    query_grad, key_grad, value_grad = whole_call(
        attn_weights_kernel,
        "attn_weight_gradients",
        (info, sum_one, permute(sum_one, SIBLING)),
        [((shard, 2048), f32), ((shard, 1024), f32), ((shard, 1024), f32)],
    )
    gain_grads = gain_grads.reshape(-1)
    return (
        outcome,
        grad_tokens,
        gain_grads[:width],
        query_grad,
        key_grad,
        value_grad,
        gain_grads[2 * width : 2 * width + HEAD_SIZE],
        gain_grads[2 * width + HEAD_SIZE :],
        total[3 * RUN :],
        gain_grads[width : 2 * width],
        gate_grad,
        up_grad,
        total[: 3 * RUN],
    )


def solution(mesh):
    split = mesh.shape["grp"] == N_GRP and mesh.shape["ctx"] == N_CTX
    return jax.shard_map(
        shards_split if split else shards,
        mesh=mesh,
        in_specs=(
            P(("grp", "ctx"), None),
            P(),
            P(),
            P("ctx", None),
            P("ctx", None),
            P("ctx", None),
            P(),
            P(),
            P("ctx", None),
            P(),
            P("ctx", None),
            P("ctx", None),
            P("ctx", None),
            P(("grp", "ctx"), None),
        ),
        out_specs=(
            P(("grp", "ctx"), None),
            P(("grp", "ctx"), None),
            P(),
            P("ctx", None),
            P("ctx", None),
            P("ctx", None),
            P(),
            P(),
            P("ctx", None),
            P(),
            P("ctx", None),
            P("ctx", None),
            P("ctx", None),
        ),
        check_vma=False,
    )
```

```python
import math

import jax
import jax.numpy as jnp
from jax import lax
from jax.experimental import pallas as pl
from jax.experimental.pallas import tpu as pltpu
from jax.sharding import PartitionSpec as P

QUERY_HEADS = 16
KEY_VALUE_HEADS = 8
HEAD_SIZE = 128
PROMPT = 1024
CONT_LEN = 448
BLK = 16


eps = 1e-06
theta = 1000000.0
key_span = 512
masked_score = -1e30


def normed_parts(value_rows):
    inverse = lax.rsqrt(jnp.mean(value_rows * value_rows, axis=-1, keepdims=True) + eps)
    return (value_rows * inverse, inverse)


def norm_back(grad_normed, normed, inverse):
    return inverse * (grad_normed - normed * jnp.mean(grad_normed * normed, axis=-1, keepdims=True))


def layout(block_table, slot_ids):
    natural = block_table[slot_ids // BLK] * BLK + slot_ids % BLK
    beyond = natural - PROMPT
    segment = jnp.where(natural < PROMPT, 0, 1 + beyond // CONT_LEN)
    places = jnp.where(natural < PROMPT, natural, PROMPT + beyond % CONT_LEN)
    return (natural, segment, places)


def rotation(places):
    half_dim = HEAD_SIZE // 2
    frequency = jnp.exp(
        jnp.arange(half_dim, dtype=jnp.float32) * (-2.0 * math.log(theta) / HEAD_SIZE)
    )
    angles = places.astype(jnp.float32)[:, None] * frequency[None, :]
    return (jnp.cos(angles)[:, None, :], jnp.sin(angles)[:, None, :])


def apply_rotation(value_rows, cosine_table, sine_table):
    half_dim = value_rows.shape[-1] // 2
    first_half = value_rows[..., :half_dim]
    second_half = value_rows[..., half_dim:]
    return jnp.concatenate(
        [
            first_half * cosine_table - second_half * sine_table,
            second_half * cosine_table + first_half * sine_table,
        ],
        axis=-1,
    )


def rotate_back(value_rows, cosine_table, sine_table):
    half_dim = value_rows.shape[-1] // 2
    first_half = value_rows[..., :half_dim]
    second_half = value_rows[..., half_dim:]
    return jnp.concatenate(
        [
            first_half * cosine_table + second_half * sine_table,
            second_half * cosine_table - first_half * sine_table,
        ],
        axis=-1,
    )


def allowed_mask(own_nat, own_seg, key_nat, key_seg):
    return (key_nat[None, :] <= own_nat[:, None]) & (
        (key_seg[None, :] == 0) | (key_seg[None, :] == own_seg[:, None])
    )


def span_of():
    return key_span


def over_blocks(advance, running, length):
    block_span_width = span_of()

    def scan_step(inner_state, key_first):
        return (advance(inner_state, key_first, block_span_width), None)

    running, ignored = lax.scan(
        scan_step,
        running,
        jnp.arange(length // block_span_width, dtype=jnp.int32) * block_span_width,
    )
    return running


def attend_block(running, query_head_rows, keys_part, values_part, allowed, softmax_scale):
    row_max, row_sum, accum = running
    raw_scores = (
        jnp.einsum("grtd,ngd->grtn", query_head_rows, keys_part, preferred_element_type=jnp.float32)
        * softmax_scale
    )
    scores = jnp.where(allowed, raw_scores, masked_score)
    new_max = jnp.maximum(row_max, jnp.max(scores, axis=-1))
    rescale = jnp.exp(row_max - new_max)
    weights = jnp.exp(scores - new_max[..., None])
    row_sum = row_sum * rescale + jnp.sum(weights, axis=-1)
    accum = accum * rescale[..., None] + jnp.einsum(
        "grtn,ngd->grtd",
        weights.astype(jnp.bfloat16),
        values_part,
        preferred_element_type=jnp.float32,
    )
    return (new_max, row_sum, accum)


def key_terms(
    grad_scores, weights, query_head_rows, scaled_high, scaled_rest, softmax_scale, block_span_width
):
    grad_keys = (
        jnp.einsum(
            "grtn,grtd->ngd", grad_scores, query_head_rows, preferred_element_type=jnp.float32
        )
        * softmax_scale
    )
    weights_low = weights.astype(jnp.bfloat16)
    grad_values = jnp.einsum(
        "grtn,grtd->ngd", weights_low, scaled_high, preferred_element_type=jnp.float32
    )
    grad_values = grad_values + jnp.einsum(
        "grtn,grtd->ngd", weights_low, scaled_rest, preferred_element_type=jnp.float32
    )
    return jnp.stack(
        [grad_keys.reshape(block_span_width, -1), grad_values.reshape(block_span_width, -1)], axis=1
    )


def shards(
    tokens,
    block_table,
    norm1_gain,
    w_query,
    key_weight,
    value_weight,
    query_gain,
    key_norm_gain,
    w_out,
    norm2_gain,
    w_gate,
    w_up,
    w_down,
    out_grad,
):
    row_total = tokens.shape[0]
    group_length = block_table.shape[0] * BLK
    sharing_count = QUERY_HEADS // KEY_VALUE_HEADS
    softmax_scale = 1.0 / math.sqrt(HEAD_SIZE)
    position = lax.axis_index("ctx")
    all_nat, all_seg, all_places = layout(block_table, jnp.arange(group_length, dtype=jnp.int32))
    own_slots = position * row_total + jnp.arange(row_total, dtype=jnp.int32)
    own_nat, own_seg, own_places = layout(block_table, own_slots)
    cosine_table, sine_table = rotation(own_places)
    query_full, key_full, value_full, out_full = (
        lax.all_gather(w_query, "ctx", axis=0, tiled=True),
        lax.all_gather(key_weight, "ctx", axis=0, tiled=True),
        lax.all_gather(value_weight, "ctx", axis=0, tiled=True),
        lax.all_gather(w_out, "ctx", axis=0, tiled=True),
    )
    inputs = tokens.astype(jnp.float32)
    normed_one, inverse_one = normed_parts(inputs)
    first_hidden = (normed_one * norm1_gain).astype(jnp.bfloat16)
    query_raw = jnp.dot(first_hidden, query_full, preferred_element_type=jnp.float32).reshape(
        row_total, QUERY_HEADS, HEAD_SIZE
    )
    unnormalized_keys = jnp.dot(first_hidden, key_full, preferred_element_type=jnp.float32).reshape(
        row_total, KEY_VALUE_HEADS, HEAD_SIZE
    )
    reduced_value = jnp.dot(first_hidden, value_full, preferred_element_type=jnp.float32).astype(
        jnp.bfloat16
    )
    query_normed, query_inverse = normed_parts(query_raw)
    normalized_keys, key_inverse = normed_parts(unnormalized_keys)
    reduced_query = apply_rotation(query_normed * query_gain, cosine_table, sine_table).astype(
        jnp.bfloat16
    )
    key_low = (
        apply_rotation(normalized_keys * key_norm_gain, cosine_table, sine_table)
        .astype(jnp.bfloat16)
        .reshape(row_total, KEY_VALUE_HEADS * HEAD_SIZE)
    )
    query_head_rows = jnp.transpose(
        reduced_query.reshape(row_total, KEY_VALUE_HEADS, sharing_count, HEAD_SIZE), (1, 2, 0, 3)
    )

    def attend(running, pieces):
        piece_keys, piece_values = pieces

        def advance(inner_state, key_first, block_span_width):
            keys_part = lax.dynamic_slice_in_dim(
                piece_keys, key_first, block_span_width, 0
            ).reshape(block_span_width, KEY_VALUE_HEADS, HEAD_SIZE)
            values_part = lax.dynamic_slice_in_dim(
                piece_values, key_first, block_span_width, 0
            ).reshape(block_span_width, KEY_VALUE_HEADS, HEAD_SIZE)
            key_nat = lax.dynamic_slice_in_dim(all_nat, key_first, block_span_width)
            key_seg = lax.dynamic_slice_in_dim(all_seg, key_first, block_span_width)
            allowed = allowed_mask(own_nat, own_seg, key_nat, key_seg)
            return attend_block(
                inner_state, query_head_rows, keys_part, values_part, allowed, softmax_scale
            )

        return over_blocks(advance, running, piece_keys.shape[0])

    statistic_shape = (KEY_VALUE_HEADS, sharing_count, row_total)
    initial = (
        jnp.full(statistic_shape, masked_score, jnp.float32),
        jnp.zeros(statistic_shape, jnp.float32),
        jnp.zeros(statistic_shape + (HEAD_SIZE,), jnp.float32),
    )
    row_max, row_sum, accum = attend(
        initial,
        (
            lax.all_gather(key_low, "ctx", axis=0, tiled=True),
            lax.all_gather(reduced_value, "ctx", axis=0, tiled=True),
        ),
    )
    mixed_heads = accum / row_sum[..., None]
    flat_low = (
        jnp.transpose(mixed_heads, (2, 0, 1, 3))
        .reshape(row_total, QUERY_HEADS * HEAD_SIZE)
        .astype(jnp.bfloat16)
    )
    resid_one = inputs + jnp.dot(flat_low, out_full, preferred_element_type=jnp.float32)
    gate_full, up_full, down_full = (
        lax.all_gather(w_gate, "ctx", axis=0, tiled=True),
        lax.all_gather(w_up, "ctx", axis=0, tiled=True),
        lax.all_gather(w_down, "ctx", axis=0, tiled=True),
    )
    normed_two, inverse_two = normed_parts(resid_one)
    hidden_two = (normed_two * norm2_gain).astype(jnp.bfloat16)
    gate_proj = jnp.dot(hidden_two, gate_full, preferred_element_type=jnp.float32)
    up_proj = jnp.dot(hidden_two, up_full, preferred_element_type=jnp.float32)
    gate_sigmoid = jax.nn.sigmoid(gate_proj)
    gate_silu = gate_proj * gate_sigmoid
    hidden_low = (gate_silu * up_proj).astype(jnp.bfloat16)
    outcome = resid_one + jnp.dot(hidden_low, down_full, preferred_element_type=jnp.float32)
    gate_full, up_full, down_full = (
        lax.all_gather(w_gate, "ctx", axis=0, tiled=True),
        lax.all_gather(w_up, "ctx", axis=0, tiled=True),
        lax.all_gather(w_down, "ctx", axis=0, tiled=True),
    )
    grad_out = out_grad.astype(jnp.float32)
    grad_down = jnp.einsum("tf,td->fd", hidden_low, out_grad, preferred_element_type=jnp.float32)
    grad_hidden = jnp.einsum("td,fd->tf", out_grad, down_full, preferred_element_type=jnp.float32)
    grad_gate = (
        grad_hidden * up_proj * gate_sigmoid * (1.0 + gate_proj * (1.0 - gate_sigmoid))
    ).astype(jnp.bfloat16)
    grad_up = (grad_hidden * gate_silu).astype(jnp.bfloat16)
    grad_wgate = jnp.einsum("tk,tf->kf", hidden_two, grad_gate, preferred_element_type=jnp.float32)
    grad_wup = jnp.einsum("tk,tf->kf", hidden_two, grad_up, preferred_element_type=jnp.float32)
    grad_two = jnp.einsum(
        "tf,kf->tk", grad_gate, gate_full, preferred_element_type=jnp.float32
    ) + jnp.einsum("tf,kf->tk", grad_up, up_full, preferred_element_type=jnp.float32)
    gain_two_part = jnp.sum(grad_two * normed_two, axis=0)
    grad_resid = grad_out + norm_back(grad_two * norm2_gain, normed_two, inverse_two)
    grad_attn = grad_resid.astype(jnp.bfloat16)
    query_full, key_full, value_full, out_full = (
        lax.all_gather(w_query, "ctx", axis=0, tiled=True),
        lax.all_gather(key_weight, "ctx", axis=0, tiled=True),
        lax.all_gather(value_weight, "ctx", axis=0, tiled=True),
        lax.all_gather(w_out, "ctx", axis=0, tiled=True),
    )
    keys_all, values_all = (
        lax.all_gather(key_low, "ctx", axis=0, tiled=True),
        lax.all_gather(reduced_value, "ctx", axis=0, tiled=True),
    )
    grad_wout = jnp.einsum("tk,td->kd", flat_low, grad_attn, preferred_element_type=jnp.float32)
    flattened_grad = jnp.einsum(
        "td,kd->tk", grad_attn, out_full, preferred_element_type=jnp.float32
    ).astype(jnp.bfloat16)
    head_grads = jnp.transpose(
        flattened_grad.reshape(row_total, KEY_VALUE_HEADS, sharing_count, HEAD_SIZE), (1, 2, 0, 3)
    )
    grad_heads_wide = head_grads.astype(jnp.float32)
    row_delta = jnp.sum(grad_heads_wide * mixed_heads, axis=-1)
    scaled_grad = grad_heads_wide / row_sum[..., None]
    scaled_high = scaled_grad.astype(jnp.bfloat16)
    scaled_rest = (scaled_grad - scaled_high.astype(jnp.float32)).astype(jnp.bfloat16)

    def block_back(key_first, block_span_width):
        keys_part = lax.dynamic_slice_in_dim(keys_all, key_first, block_span_width, 0).reshape(
            block_span_width, KEY_VALUE_HEADS, HEAD_SIZE
        )
        values_part = lax.dynamic_slice_in_dim(values_all, key_first, block_span_width, 0).reshape(
            block_span_width, KEY_VALUE_HEADS, HEAD_SIZE
        )
        key_nat = lax.dynamic_slice_in_dim(all_nat, key_first, block_span_width)
        key_seg = lax.dynamic_slice_in_dim(all_seg, key_first, block_span_width)
        allowed = allowed_mask(own_nat, own_seg, key_nat, key_seg)
        raw_scores = (
            jnp.einsum(
                "grtd,ngd->grtn", query_head_rows, keys_part, preferred_element_type=jnp.float32
            )
            * softmax_scale
        )
        scores = jnp.where(allowed, raw_scores, masked_score)
        weights = jnp.exp(scores - row_max[..., None])
        grad_prob = jnp.einsum(
            "grtd,ngd->grtn", head_grads, values_part, preferred_element_type=jnp.float32
        )
        grad_scores = (weights * (grad_prob - row_delta[..., None]) / row_sum[..., None]).astype(
            jnp.bfloat16
        )
        return (keys_part, grad_scores, weights)

    empty_query = jnp.zeros((KEY_VALUE_HEADS, sharing_count, row_total, HEAD_SIZE), jnp.float32)
    span_back = span_of()

    def pass_step(grad_query, key_first):
        keys_part, grad_scores, weights = block_back(key_first, span_back)
        grad_query = grad_query + jnp.einsum(
            "grtn,ngd->grtd", grad_scores, keys_part, preferred_element_type=jnp.float32
        )
        return (
            grad_query,
            key_terms(
                grad_scores,
                weights,
                query_head_rows,
                scaled_high,
                scaled_rest,
                softmax_scale,
                span_back,
            ),
        )

    grad_query, key_gradient_parts = lax.scan(
        pass_step, empty_query, jnp.arange(group_length // span_back, dtype=jnp.int32) * span_back
    )
    self_terms = lax.psum_scatter(
        key_gradient_parts.reshape(group_length, 2, KEY_VALUE_HEADS * HEAD_SIZE).astype(
            jnp.bfloat16
        ),
        "ctx",
        scatter_dimension=0,
        tiled=True,
    ).astype(jnp.float32)
    grad_query_rows = jnp.transpose(grad_query * softmax_scale, (2, 0, 1, 3)).reshape(
        row_total, QUERY_HEADS, HEAD_SIZE
    )
    grad_query_normed = rotate_back(grad_query_rows, cosine_table, sine_table)
    gain_query_part = jnp.sum(grad_query_normed * query_normed, axis=(0, 1))
    grad_query_raw = (
        norm_back(grad_query_normed * query_gain, query_normed, query_inverse)
        .reshape(row_total, QUERY_HEADS * HEAD_SIZE)
        .astype(jnp.bfloat16)
    )
    key_row_grads = self_terms[:, 0, :].reshape(row_total, KEY_VALUE_HEADS, HEAD_SIZE)
    grad_key_normed = rotate_back(key_row_grads, cosine_table, sine_table)
    gain_key_part = jnp.sum(grad_key_normed * normalized_keys, axis=(0, 1))
    grad_key_raw = (
        norm_back(grad_key_normed * key_norm_gain, normalized_keys, key_inverse)
        .reshape(row_total, KEY_VALUE_HEADS * HEAD_SIZE)
        .astype(jnp.bfloat16)
    )
    grad_value_low = self_terms[:, 1, :].astype(jnp.bfloat16)
    grad_wquery = jnp.einsum(
        "tk,tq->kq", first_hidden, grad_query_raw, preferred_element_type=jnp.float32
    )
    grad_wkey = jnp.einsum(
        "tk,tq->kq", first_hidden, grad_key_raw, preferred_element_type=jnp.float32
    )
    grad_wvalue = jnp.einsum(
        "tk,tq->kq", first_hidden, grad_value_low, preferred_element_type=jnp.float32
    )
    grad_one = jnp.einsum(
        "tq,kq->tk", grad_query_raw, query_full, preferred_element_type=jnp.float32
    )
    grad_one = grad_one + jnp.einsum(
        "tq,kq->tk", grad_key_raw, key_full, preferred_element_type=jnp.float32
    )
    grad_one = grad_one + jnp.einsum(
        "tq,kq->tk", grad_value_low, value_full, preferred_element_type=jnp.float32
    )
    gain_one_part = jnp.sum(grad_one * normed_one, axis=0)
    grad_tokens = grad_resid + norm_back(grad_one * norm1_gain, normed_one, inverse_one)
    shard_grads = (
        lax.psum_scatter(
            grad_wquery.astype(jnp.bfloat16), "ctx", scatter_dimension=0, tiled=True
        ).astype(jnp.float32),
        lax.psum_scatter(
            grad_wkey.astype(jnp.bfloat16), "ctx", scatter_dimension=0, tiled=True
        ).astype(jnp.float32),
        lax.psum_scatter(
            grad_wvalue.astype(jnp.bfloat16), "ctx", scatter_dimension=0, tiled=True
        ).astype(jnp.float32),
        lax.psum_scatter(
            grad_wout.astype(jnp.bfloat16), "ctx", scatter_dimension=0, tiled=True
        ).astype(jnp.float32),
        lax.psum_scatter(
            grad_wgate.astype(jnp.bfloat16), "ctx", scatter_dimension=0, tiled=True
        ).astype(jnp.float32),
        lax.psum_scatter(
            grad_wup.astype(jnp.bfloat16), "ctx", scatter_dimension=0, tiled=True
        ).astype(jnp.float32),
        lax.psum_scatter(
            grad_down.astype(jnp.bfloat16), "ctx", scatter_dimension=0, tiled=True
        ).astype(jnp.float32),
    )
    shard_grads = (
        lax.psum(shard_grads[0].astype(jnp.bfloat16), "grp").astype(jnp.float32),
        lax.psum(shard_grads[1].astype(jnp.bfloat16), "grp").astype(jnp.float32),
        lax.psum(shard_grads[2].astype(jnp.bfloat16), "grp").astype(jnp.float32),
        lax.psum(shard_grads[3].astype(jnp.bfloat16), "grp").astype(jnp.float32),
        lax.psum(shard_grads[4].astype(jnp.bfloat16), "grp").astype(jnp.float32),
        lax.psum(shard_grads[5].astype(jnp.bfloat16), "grp").astype(jnp.float32),
        lax.psum(shard_grads[6].astype(jnp.bfloat16), "grp").astype(jnp.float32),
    )
    gain_grads = lax.psum(
        (gain_one_part, gain_query_part, gain_key_part, gain_two_part), ("grp", "ctx")
    )
    return (
        outcome.astype(jnp.bfloat16),
        grad_tokens,
        gain_grads[0],
        shard_grads[0],
        shard_grads[1],
        shard_grads[2],
        gain_grads[1],
        gain_grads[2],
        shard_grads[3],
        gain_grads[3],
        shard_grads[4],
        shard_grads[5],
        shard_grads[6],
    )


f32 = jnp.float32
bf16 = jnp.bfloat16
AXES = ("grp", "ctx")
N_GRP = 4
N_CTX = 8
SCALE = 1.0 / math.sqrt(HEAD_SIZE)
EXP2_SCALE = math.log2(math.e) / math.sqrt(HEAD_SIZE)
VMEM_LIMIT = 60 * 1024 * 1024
RUN = 8 * BLK
PROMPT_BLOCKS = PROMPT // BLK
CONT_BLOCKS = CONT_LEN // BLK
CHUNK = 5
HELD = RUN + CONT_LEN


def nt(a, b):
    return lax.dot_general(a, b, (((1,), (1,)), ((), ())), preferred_element_type=f32)


def nn(a, b):
    return jnp.dot(a, b, preferred_element_type=f32)


def tn(a, b):
    return lax.dot_general(a, b, (((0,), (0,)), ((), ())), preferred_element_type=f32)


def rows_at(start, size):
    return pl.ds(pl.multiple_of(start, size), size)


def turned(u):
    return pltpu.roll(u, HEAD_SIZE // 2, 1)


def head(i):
    return slice(i * HEAD_SIZE, (i + 1) * HEAD_SIZE)


def params():
    return pltpu.CompilerParams(vmem_limit_bytes=VMEM_LIMIT)


def whole_call(kernel, name, args, outs, scratch=()):
    smem = pl.BlockSpec(memory_space=pltpu.SMEM)
    vmem = pl.BlockSpec(memory_space=pltpu.VMEM)
    return pl.pallas_call(
        kernel,
        in_specs=[smem if a.dtype == jnp.int32 else vmem for a in args],
        out_specs=[vmem] * len(outs),
        out_shape=[jax.ShapeDtypeStruct(s, t) for s, t in outs],
        scratch_shapes=list(scratch),
        compiler_params=params(),
        name=name,
    )(*args)


def deal_kernel(table, rows_ref, *outs):
    for e in range(8):
        for i in range(CHUNK):
            outs[e][i * BLK : (i + 1) * BLK, :] = rows_ref[rows_at(table[e, i] * BLK, BLK), :]


def deal(table, rows):
    shape = (CHUNK * BLK, rows.shape[1])
    return whole_call(deal_kernel, "deal_rows", (table, rows), [(shape, rows.dtype)] * 8)


def deal_all_kernel(table, rows_ref, out_ref):
    for e in range(8):
        for i in range(CHUNK):
            out_ref[e, i * BLK : (i + 1) * BLK, :] = rows_ref[rows_at(table[e, i] * BLK, BLK), :]


def deal_all(table, rows):
    shape = (8, CHUNK * BLK, rows.shape[1])
    return whole_call(deal_all_kernel, "deal_all", (table, rows), [(shape, rows.dtype)])[0]


def place_all_kernel(table, pieces, out_ref, held):
    for e in range(8):
        for i in range(CHUNK):
            held[rows_at(table[e, i] * BLK, BLK), :] = pieces[e, i * BLK : (i + 1) * BLK, :]
    out_ref[...] = held[: out_ref.shape[0], :].astype(out_ref.dtype)


def place_all(table, pieces, n_rows, kind):
    shape = (n_rows, pieces.shape[2])
    return whole_call(
        place_all_kernel,
        "place_all",
        (table, pieces),
        [(shape, kind)],
        [pltpu.VMEM((n_rows + BLK, shape[1]), pieces.dtype)],
    )[0]


def place_kernel(table, *refs):
    pieces, out_ref, held = refs[:8], refs[8], refs[-1]
    for e in range(8):
        for i in range(CHUNK):
            held[rows_at(table[e, i] * BLK, BLK), :] = pieces[e][i * BLK : (i + 1) * BLK, :]
    out_ref[...] = held[: out_ref.shape[0], :].astype(out_ref.dtype)


def place(table, pieces, n_rows, kind):
    shape = (n_rows, pieces[0].shape[1])
    return whole_call(
        place_kernel,
        "place_rows",
        (table, *pieces),
        [(shape, kind)],
        [pltpu.VMEM((n_rows + BLK, shape[1]), pieces[0].dtype)],
    )[0]


def place_norm_kernel(table, *refs):
    gain_ref, out_ref, low_ref, held = refs[8:]
    place_kernel(table, *refs[:8], out_ref, held)
    normed, _ = normed_parts(out_ref[...].astype(f32))
    low_ref[...] = (normed * gain_ref[...]).astype(bf16)


def place_norm(table, pieces, gain, n_rows):
    shape = (n_rows, pieces[0].shape[1])
    return whole_call(
        place_norm_kernel,
        "place_rows_norm",
        (table, *pieces, gain),
        [(shape, bf16), (shape, bf16)],
        [pltpu.VMEM((n_rows + BLK, shape[1]), bf16)],
    )


def gathered_rows(info, pieces, w_ref):
    for e in range(8):
        w_ref[rows_at((info[0] ^ e) * 128, 128), :] = pieces[e][...]


def lane_mean(u):
    ones = jnp.full((HEAD_SIZE, HEAD_SIZE), 1.0 / HEAD_SIZE, bf16)
    high = u.astype(bf16)
    return nn(high, ones) + nn((u - high.astype(f32)).astype(bf16), ones)


def head_normed(u):
    inverse = lax.rsqrt(lane_mean(u * u) + eps)
    return u * inverse, inverse


def query_kernel(info, h_ref, *refs):
    gain_ref, cos_ref, sin_ref, q_ref, raw_ref, w_ref = refs[8:]
    gathered_rows(info, refs[:8], w_ref)
    acc = nn(h_ref[...], w_ref[...])
    raw_ref[...] = acc
    for i in range(2):
        normed, _ = head_normed(acc[:, head(i)])
        u = normed * gain_ref[...]
        q_ref[:, head(i)] = (u * cos_ref[...] + turned(u) * sin_ref[...]).astype(bf16)


def key_value_kernel(info, h_ref, *refs):
    gain_ref, cos_ref, sin_ref, kv_ref, raw_ref, w_ref, send_ref = refs[8:]
    gathered_rows(info, refs[:8], w_ref)
    acc = nn(h_ref[...], w_ref[...])
    raw_ref[...] = acc[:, head(0)]
    normed, _ = head_normed(acc[:, head(0)])
    u = normed * gain_ref[...]
    kv_ref[:, head(0)] = (u * cos_ref[...] + turned(u) * sin_ref[...]).astype(bf16)
    kv_ref[:, head(1)] = acc[:, head(1)].astype(bf16)
    for b in range(2):
        send_ref[b * RUN : (b + 1) * RUN, :] = kv_ref[b * HELD : b * HELD + RUN, :]


def project(kernel, name, info, hidden, pieces, first, gain, cos, sin, raw_width, extra):
    rows, width = hidden.shape

    def still(g, s):
        return (0, 0)

    def moving(g, s):
        return (0, g)

    return pl.pallas_call(
        kernel,
        grid_spec=pltpu.PrefetchScalarGridSpec(
            num_scalar_prefetch=1,
            grid=(4,),
            in_specs=[pl.BlockSpec((rows, width), still)]
            + [pl.BlockSpec((128, 256), lambda g, s: (0, g + first))] * 8
            + [
                pl.BlockSpec((1, HEAD_SIZE), still),
                pl.BlockSpec((rows, HEAD_SIZE), still),
                pl.BlockSpec((rows, HEAD_SIZE), still),
            ],
            out_specs=[
                pl.BlockSpec((rows, 256), moving),
                pl.BlockSpec((rows, raw_width), moving),
                pl.BlockSpec((width, 256), moving),
            ]
            + [pl.BlockSpec((2 * RUN, 256), moving)] * extra,
        ),
        out_shape=[
            jax.ShapeDtypeStruct((rows, 1024), bf16),
            jax.ShapeDtypeStruct((rows, 4 * raw_width), f32),
            jax.ShapeDtypeStruct((width, 1024), bf16),
        ]
        + [jax.ShapeDtypeStruct((2 * RUN, 1024), bf16)] * extra,
        compiler_params=params(),
        name=name,
    )(info, hidden, *pieces, gain, cos, sin)


def seen_in_prompt(info, half):
    key = lax.broadcasted_iota(jnp.int32, (PROMPT, RUN), 0)
    tile = key // RUN
    run = info[3] ^ (tile // 2 + 4 * (tile % 2))
    row = lax.broadcasted_iota(jnp.int32, (PROMPT, RUN), 1) + (info[3] ^ (4 * half)) * RUN
    return run * RUN + key % RUN <= row


def seen_in_own():
    key = lax.broadcasted_iota(jnp.int32, (CONT_LEN, CONT_LEN), 0)
    row = lax.broadcasted_iota(jnp.int32, (CONT_LEN, CONT_LEN), 1)
    return key <= row


LSE_SPAN = 640


def units():
    for b in range(2):
        yield b, b * HELD + RUN, CONT_LEN, b * LSE_SPAN, False
    for b in range(2):
        yield b, b * HELD, RUN, b * LSE_SPAN + 512, True


def attn_fwd_kernel(info, q_ref, kv_ref, p0, p1, p2, p3, o_ref, lse_ref, p_ref):
    for t, p in enumerate((p0, p1, p2, p3)):
        p_ref[t * 2 * RUN : (t + 1) * 2 * RUN, :] = p[...]
    prompt = (p_ref[:, head(0)], jnp.transpose(p_ref[:, head(1)]))
    for b, row0, n, lane, in_prompt in units():
        own = slice(row0, row0 + n)
        tiles = [(*prompt, seen_in_prompt(info, b) if in_prompt else None)]
        if not in_prompt:
            tiles.append((kv_ref[own, head(0)], jnp.transpose(kv_ref[own, head(1)]), seen_in_own()))
        for i in range(2):
            q = q_ref[own, head(i)]
            total = jnp.zeros((1, n), f32)
            mixed = jnp.zeros((HEAD_SIZE, n), f32)
            for keys, values_t, seen in tiles:
                p = jnp.exp2(nt(keys, q) * EXP2_SCALE)
                if seen is not None:
                    p = jnp.where(seen, p, 0.0)
                total = total + jnp.sum(p, axis=0, keepdims=True)
                mixed = mixed + nn(values_t, p.astype(bf16))
            o_ref[own, head(i)] = jnp.transpose(mixed / total).astype(bf16)
            lse_ref[0, i : i + 1, lane : lane + n] = jnp.log2(total)


def attn_specs(rows, *names):
    specs = {
        "wide": pl.BlockSpec((rows, 256), lambda g, s: (0, g)),
        "head": pl.BlockSpec((rows, HEAD_SIZE), lambda g, s: (0, g)),
        "prompt": pl.BlockSpec((2 * RUN, 256), lambda g, s: (0, g)),
        "lse": pl.BlockSpec((1, 8, 2 * LSE_SPAN), lambda g, s: (g, 0, 0)),
        "table": pl.BlockSpec((rows, HEAD_SIZE), lambda g, s: (0, 0)),
        "gain": pl.BlockSpec((1, HEAD_SIZE), lambda g, s: (0, 0)),
        "gains": pl.BlockSpec((8, HEAD_SIZE), lambda g, s: (0, 0)),
    }
    return [specs[n] for n in names]


def attn_fwd(info, q, kv, prompt):
    rows = q.shape[0]
    return pl.pallas_call(
        attn_fwd_kernel,
        grid_spec=pltpu.PrefetchScalarGridSpec(
            num_scalar_prefetch=1,
            grid=(4,),
            in_specs=attn_specs(rows, "wide", "wide", *["prompt"] * 4),
            out_specs=attn_specs(rows, "wide", "lse"),
            scratch_shapes=[pltpu.VMEM((PROMPT, 256), bf16)],
        ),
        out_shape=[
            jax.ShapeDtypeStruct((rows, 1024), bf16),
            jax.ShapeDtypeStruct((4, 8, 2 * LSE_SPAN), f32),
        ],
        compiler_params=params(),
        cost_estimate=pl.CostEstimate(flops=20*10**9, bytes_accessed=10**7, transcendentals=0),
        name="attn_fwd",
    )(info, q, kv, *prompt)


def key_back(grad, raw, cos, sin, gain):
    normed, inverse = normed_parts(raw)
    grad = grad * SCALE
    back = grad * cos - turned(grad) * sin
    part = jnp.sum(back * normed, axis=0, keepdims=True)
    return norm_back(back * gain, normed, inverse).astype(bf16), part


def attn_bwd_kernel(info, q_ref, kv_ref, p0, p1, p2, p3, *refs):
    do_ref, o_ref, lse_ref, rawq_ref, rawk_ref, qg_ref, kg_ref, cos_ref, sin_ref = refs[:9]
    dq_ref, dkv_ref, d0, d1, d2, d3, gains_ref, dk_ref, dv_ref, p_ref = refs[9:]
    for t, p in enumerate((p0, p1, p2, p3)):
        p_ref[t * 2 * RUN : (t + 1) * 2 * RUN, :] = p[...]
    prompt = (p_ref[:, head(0)], jnp.transpose(p_ref[:, head(0)]), p_ref[:, head(1)])

    @pl.when(pl.program_id(0) == 0)
    def first():
        gains_ref[...] = jnp.zeros_like(gains_ref)

    for number, (b, row0, n, lane, in_prompt) in enumerate(units()):
        own = slice(row0, row0 + n)
        cos, sin = cos_ref[own, :], sin_ref[own, :]
        tiles = [(*prompt, seen_in_prompt(info, b) if in_prompt else None, True)]
        if not in_prompt:
            keys = kv_ref[own, head(0)]
            tiles.append((keys, jnp.transpose(keys), kv_ref[own, head(1)], seen_in_own(), False))
        own_dk = own_dv = 0.0
        for i in range(2):
            q, do = q_ref[own, head(i)], do_ref[own, head(i)]
            lse = lse_ref[0, i : i + 1, lane : lane + n]
            product = do.astype(f32) * o_ref[own, head(i)].astype(f32)
            delta = jnp.sum(jnp.transpose(product), axis=0, keepdims=True)
            dq = jnp.zeros((HEAD_SIZE, n), f32)
            for keys, keys_t, values, seen, shared in tiles:
                p = jnp.exp2(nt(keys, q) * EXP2_SCALE - lse)
                if seen is not None:
                    p = jnp.where(seen, p, 0.0)
                ds = (p * (nt(values, do) - delta)).astype(bf16)
                dk, dv = nn(ds, q), nn(p.astype(bf16), do)
                dq = dq + nn(keys_t, ds)
                if not shared:
                    own_dk, own_dv = own_dk + dk, own_dv + dv
                elif number == 0 and i == 0:
                    dk_ref[...] = dk
                    dv_ref[...] = dv
                else:
                    dk_ref[...] += dk
                    dv_ref[...] += dv
            back, part = key_back(jnp.transpose(dq), rawq_ref[own, head(i)], cos, sin, qg_ref[...])
            dq_ref[own, head(i)] = back
            gains_ref[0:1, :] += part
        if not in_prompt:
            back, part = key_back(own_dk, rawk_ref[own, :], cos, sin, kg_ref[...])
            dkv_ref[own, head(0)] = back
            dkv_ref[own, head(1)] = own_dv.astype(bf16)
            gains_ref[1:2, :] += part
        else:
            dkv_ref[own, :] = jnp.zeros((n, 256), bf16)
    for t, ref in enumerate((d0, d1, d2, d3)):
        ref[:, head(0)] = dk_ref[t * 256 : (t + 1) * 256, :].astype(bf16)
        ref[:, head(1)] = dv_ref[t * 256 : (t + 1) * 256, :].astype(bf16)


def attn_bwd(info, q, kv, prompt, do, o, lse, rawq, rawk, qg, kg, cos, sin):
    rows = q.shape[0]
    return pl.pallas_call(
        attn_bwd_kernel,
        grid_spec=pltpu.PrefetchScalarGridSpec(
            num_scalar_prefetch=1,
            grid=(4,),
            in_specs=attn_specs(rows, "wide", "wide", *["prompt"] * 4, "wide", "wide", "lse")
            + attn_specs(rows, "wide", "head", "gain", "gain", "table", "table"),
            out_specs=attn_specs(rows, "wide", "wide", *["prompt"] * 4, "gains"),
            scratch_shapes=[pltpu.VMEM((PROMPT, HEAD_SIZE), f32)] * 2
            + [pltpu.VMEM((PROMPT, 256), bf16)],
        ),
        out_shape=[jax.ShapeDtypeStruct((rows, 1024), bf16)] * 2
        + [jax.ShapeDtypeStruct((2 * RUN, 1024), bf16)] * 4
        + [jax.ShapeDtypeStruct((8, HEAD_SIZE), f32)],
        compiler_params=params(),
        cost_estimate=pl.CostEstimate(flops=45*10**9, bytes_accessed=10**7, transcendentals=0),
        name="attn_bwd",
    )(info, q, kv, *prompt, do, o, lse, rawq, rawk, qg, kg, cos, sin)


def prompt_back_kernel(d0, d1, d2, d3, dkv_ref, raw_ref, kg_ref, cos_ref, sin_ref, out_ref, gains_ref):
    out_ref[...] = dkv_ref[...]
    gains_ref[...] = jnp.zeros_like(gains_ref)
    for b in range(2):
        rows = slice(b * RUN, (b + 1) * RUN)
        own = slice(b * HELD, b * HELD + RUN)
        for h in range(4):
            cols = slice(h * 256, (h + 1) * 256)
            total = sum(d[rows, cols].astype(f32) for d in (d0, d1, d2, d3))
            back, part = key_back(
                total[:, head(0)], raw_ref[own, head(h)], cos_ref[own, :], sin_ref[own, :], kg_ref[...]
            )
            out_ref[own, h * 256 : h * 256 + 128] = back
            out_ref[own, h * 256 + 128 : (h + 1) * 256] = total[:, head(1)].astype(bf16)
            gains_ref[0:1, :] += part


def out_kernel(info, o_ref, *refs):
    pieces, (own_ref, sib_ref, w_ref) = refs[:2], refs[2:]
    for t in range(4):
        w_ref[rows_at((info[4] ^ t) * 256, 256), :] = pieces[t % 2][t // 2]
    half = own_ref.shape[0]
    own_ref[...] = nn(o_ref[:half, :], w_ref[...])
    sib_ref[...] = nn(o_ref[half:, :], w_ref[...]).astype(bf16)


def mlp_kernel(info, h_own, h_sib, g_own, g_sib, *refs):
    w2, w3 = refs[:10], refs[10:14]
    hid_ref, dgu_ref, out_ref, outs_ref, dh_ref, dhs_ref = refs[14:20]
    w_ref, wd_ref, out_acc, dh_acc = refs[20:]
    step = pl.program_id(0)
    ff = hid_ref.shape[1]
    half = out_ref.shape[0]
    for e in range(8):
        row = (info[0] ^ e) * 128
        w_ref[rows_at(row + info[1] * 64, 64), :] = w2[e][...]
        w_ref[rows_at(row + (1 - info[1]) * 64, 64), :] = w2[8 + e // 4][e % 4]
    for t in range(4):

        @pl.when(step == t)
        def take(t=t):
            wd_ref[...] = w3[t][...]

    @pl.when(step == 0)
    def zero():
        for ref in (out_ref, dh_ref, out_acc, dh_acc):
            ref[...] = jnp.zeros_like(ref)

    sides = ((h_own, g_own, out_ref, dh_ref), (h_sib, g_sib, out_acc, dh_acc))
    for b, (h_ref, g_ref, out, dh) in enumerate(sides):
        rows = slice(b * half, (b + 1) * half)
        both = nn(h_ref[...], w_ref[...])
        gate, up = both[:, :ff], both[:, ff:]
        sig = jax.nn.sigmoid(gate)
        silu = gate * sig
        hid = (silu * up).astype(bf16)
        hid_ref[rows, :] = hid
        dhid = nt(g_ref[...], wd_ref[...])
        dgu_ref[rows, :ff] = (dhid * up * sig * (1.0 + gate * (1.0 - sig))).astype(bf16)
        dgu_ref[rows, ff:] = (dhid * silu).astype(bf16)
        dh[...] += nt(dgu_ref[rows, :], w_ref[...])
        out[...] += nn(hid, wd_ref[...])

    @pl.when(step == 3)
    def finish():
        outs_ref[...] = out_acc[...].astype(bf16)
        dhs_ref[...] = dh_acc[...].astype(bf16)


def mlp(info, hidden, grad, w2, w3, ff):
    half, width = hidden[0].shape
    rows = 2 * half
    once = pl.Buffered(1)

    def still(shape):
        return pl.BlockSpec(shape, lambda g, s: (0, 0), pipeline_mode=once)

    return pl.pallas_call(
        mlp_kernel,
        grid_spec=pltpu.PrefetchScalarGridSpec(
            num_scalar_prefetch=1,
            grid=(4,),
            in_specs=[still((half, width))] * 4
            + [pl.BlockSpec((64, 2 * ff), lambda g, s: (0, s[4] ^ g))] * 8
            + [pl.BlockSpec((4, 64, 2 * ff), lambda g, s: (0, 0, s[4] ^ g))] * 2
            + [still(w3[0].shape)] * 4,
            out_specs=[
                pl.BlockSpec((rows, ff), lambda g, s: (0, s[4] ^ g)),
                pl.BlockSpec((rows, 2 * ff), lambda g, s: (0, s[4] ^ g)),
            ]
            + [pl.BlockSpec((half, width), lambda g, s: (0, 0))] * 4,
            scratch_shapes=[
                pltpu.VMEM((width, 2 * ff), bf16),
                pltpu.VMEM((ff, width), bf16),
                pltpu.VMEM((half, width), f32),
                pltpu.VMEM((half, width), f32),
            ],
        ),
        out_shape=[
            jax.ShapeDtypeStruct((rows, 4 * ff), bf16),
            jax.ShapeDtypeStruct((rows, 8 * ff), bf16),
            jax.ShapeDtypeStruct((half, width), f32),
            jax.ShapeDtypeStruct((half, width), bf16),
            jax.ShapeDtypeStruct((half, width), f32),
            jax.ShapeDtypeStruct((half, width), bf16),
        ],
        compiler_params=params(),
        cost_estimate=pl.CostEstimate(flops=38*10**9, bytes_accessed=10**7, transcendentals=0),
        name="feed_forward",
    )(info, *hidden, *grad, *w2, *w3)


def gate_up_kernel(info, own_ref, sib_ref, gate_ref, up_ref):
    ff = own_ref.shape[1] // 8
    for first, (low, high) in ((0, (own_ref, sib_ref)), (1, (sib_ref, own_ref))):

        @pl.when(info[2] == first)
        def write(low=low, high=high):
            for c, ref in enumerate((low, high)):
                for b in range(4):
                    cols = slice((c * 4 + b) * ff, (c * 4 + b + 1) * ff)
                    gate_ref[:, cols] = ref[:, 2 * b * ff : (2 * b + 1) * ff].astype(f32)
                    up_ref[:, cols] = ref[:, (2 * b + 1) * ff : (2 * b + 2) * ff].astype(f32)


def attn_weights_kernel(info, own_ref, sib_ref, query_ref, key_ref, value_ref):
    for first, (low, high) in ((0, (own_ref, sib_ref)), (1, (sib_ref, own_ref))):

        @pl.when(info[2] == first)
        def write(low=low, high=high):
            for c, ref in enumerate((low, high)):
                query_ref[:, c * 1024 : (c + 1) * 1024] = ref[:, :1024].astype(f32)
                for h in range(4):
                    start = 1024 + h * 256
                    to = head(c * 4 + h)
                    key_ref[:, to] = ref[:, start : start + 128].astype(f32)
                    value_ref[:, to] = ref[:, start + 128 : start + 256].astype(f32)


def device_of(y, core, z_hi, z_lo, x):
    return (y * 2 + core) * N_CTX + z_hi * 4 + z_lo * 2 + x


def bits_of(i):
    return ((i >> 4) & 1, (i >> 3) & 1, (i >> 2) & 1, (i >> 1) & 1, i & 1)


def permutation(target, sends=lambda *bits: True):
    devices = range(N_GRP * N_CTX)
    return [(i, device_of(*target(*bits_of(i)))) for i in devices if sends(*bits_of(i))]


def member_device(e):
    def target(y, core, z_hi, z_lo, x):
        m = (z_hi * 4 + z_lo * 2 + x) ^ e
        return (y, m >> 2, core, (m >> 1) & 1, m & 1)

    return target


SPREAD = [permutation(member_device(e)) for e in range(8)]
COLLECT = [[(b, a) for a, b in pairs] for pairs in SPREAD]
HALVES = permutation(
    lambda y, core, z_hi, z_lo, x: (y, z_hi, core, z_lo, x),
    lambda y, core, z_hi, z_lo, x: z_hi != core,
)
CUBES = [
    [device_of(y, m >> 2, z_hi, (m >> 1) & 1, m & 1) for m in range(8)]
    for y in range(2)
    for z_hi in range(2)
]
OVER_Y = permutation(lambda y, core, z_hi, z_lo, x: (1 - y, core, z_hi, z_lo, x))
SIBLING = permutation(lambda y, core, z_hi, z_lo, x: (y, 1 - core, z_hi, z_lo, x))
OVER_Y_HOME = permutation(
    lambda y, core, z_hi, z_lo, x: (1 - y, core, z_hi, z_lo, x),
    lambda y, core, z_hi, z_lo, x: z_hi == core,
)
MIDDLE = permutation(lambda y, core, z_hi, z_lo, x: (y, core, 1 - z_hi, z_lo, x))
MIDDLE_OUT = permutation(
    lambda y, core, z_hi, z_lo, x: (y, core, 1 - z_hi, z_lo, x),
    lambda y, core, z_hi, z_lo, x: z_hi == core,
)
MIDDLE_IN = permutation(
    lambda y, core, z_hi, z_lo, x: (y, core, 1 - z_hi, z_lo, x),
    lambda y, core, z_hi, z_lo, x: z_hi != core,
)
CHIP = [
    permutation(
        lambda y, core, z_hi, z_lo, x, t=t: (y, core, z_hi, z_lo ^ (t >> 1), x ^ (t & 1))
    )
    for t in range(4)
]


def permute(a, pairs):
    return lax.ppermute(a, AXES, pairs)


def pick(a, i, axis=0):
    return lax.dynamic_index_in_dim(a, i, axis, keepdims=False)


def added(*terms):
    return sum(t.astype(f32) for t in terms).astype(bf16)


def after(a, b):
    return lax.optimization_barrier((a, b))[0]


def together(*arrays):
    return lax.optimization_barrier(arrays)


def in_order(first, mine, other):
    return [jnp.where(first, mine, other), jnp.where(first, other, mine)]


def shards_split(
    tokens,
    block_table,
    norm1_gain,
    w_query,
    key_weight,
    value_weight,
    query_gain,
    key_norm_gain,
    w_out,
    norm2_gain,
    w_gate,
    w_up,
    w_down,
    out_grad,
):
    row_total, width = tokens.shape
    n_slots = row_total // BLK
    ff = w_gate.shape[1] // 8
    position = lax.axis_index("ctx").astype(jnp.int32)
    group_index = lax.axis_index("grp").astype(jnp.int32)
    y, core = group_index // 2, group_index % 2
    z_hi, chip = position // 4, position % 4
    z_lo, x = chip // 2, chip % 2
    member = core * 4 + chip
    info = jnp.stack([position, y, core, member, chip])
    at_home = z_hi == core
    qg, kg = query_gain.reshape(1, HEAD_SIZE), key_norm_gain.reshape(1, HEAD_SIZE)

    eight = jnp.arange(8, dtype=jnp.int32)
    five = jnp.arange(CHUNK, dtype=jnp.int32)[None, :]

    def slots_of(m):
        m = m.reshape(-1, 1)
        return jnp.where(five == 0, m, 7 + 7 * (m // 2) + 3 * (m % 2) + five)

    def held_at(natural, m):
        inside = natural - (PROMPT_BLOCKS + CONT_BLOCKS * m)
        valid = (five == 0) | ((inside >= 0) & (inside < CONT_BLOCKS))
        return jnp.where(valid, jnp.where(five == 0, natural - 8 * m, 8 + inside), n_slots), valid

    def look_up(rows, slots):
        match = slots[:, :, None] == jnp.arange(n_slots, dtype=jnp.int32)
        return jnp.sum(jnp.where(match, rows[:, None, :], 0), axis=2)

    tables = block_table.reshape(8, n_slots)
    send_slots = slots_of(position ^ eight)
    from_tables = jnp.concatenate(
        [lax.dynamic_slice_in_dim(tables, member ^ e, 1, 0) for e in range(8)], axis=0
    )
    arrive, _ = held_at(look_up(from_tables, jnp.broadcast_to(slots_of(member), (8, CHUNK))), member)
    leave = jnp.minimum(arrive, n_slots - 1)
    own_table = lax.dynamic_slice_in_dim(tables, position, 1, 0)
    _, valid = held_at(look_up(own_table, send_slots), (position ^ eight).reshape(-1, 1))
    home_slots = jnp.where(valid, send_slots, n_slots)

    def spread(a):
        return [permute(c, pairs) for c, pairs in zip(deal(send_slots, a), SPREAD)]

    def collect(a, kind):
        pieces = [permute(c, pairs) for c, pairs in zip(deal(leave, a), COLLECT)]
        return place(home_slots, pieces, row_total, kind)

    def regrouped(a):
        return jnp.where(at_home, a, permute(a, HALVES))

    def both(a):
        return jnp.concatenate([a, permute(a, SIBLING)], axis=0)

    def columns(w, parts):
        return pick(w.reshape(w.shape[0], 2, 4, -1), core, 1)

    own_one = jnp.concatenate(
        [
            columns(w_query, 2).reshape(-1, 1024),
            jnp.concatenate([columns(key_weight, 2), columns(value_weight, 2)], axis=2).reshape(
                -1, 1024
            ),
        ],
        axis=1,
    )
    own_two = jnp.concatenate([columns(w_gate, 2), columns(w_up, 2)], axis=2)
    own_two = pick(own_two.reshape(2, 64, 8 * ff), y)
    own_out, own_down = w_out, w_down

    def around(a):
        return [a] + [permute(a, CHIP[t]) for t in range(1, 4)]

    one = around(own_one)
    middle_one = permute(own_one, MIDDLE)
    arrived = spread(tokens)
    one = one + around(middle_one)

    cosine, sine = rotation(jnp.arange(PROMPT + CONT_LEN, dtype=jnp.int32))
    cos = jnp.concatenate([cosine[:, 0], cosine[:, 0]], axis=1)
    sin = jnp.concatenate([-sine[:, 0], sine[:, 0]], axis=1)

    def of_rows(table):
        parts = []
        for m in (member, member ^ 4):
            parts += [lax.dynamic_slice_in_dim(table, m * RUN, RUN, 0), table[PROMPT:]]
        return jnp.concatenate(parts, axis=0)

    cos, sin = of_rows(cos), of_rows(sin)

    inputs_low, first_low = place_norm(arrive, arrived, norm1_gain.reshape(1, width), row_total)
    hidden_one = both(first_low)
    own_two, w_out, w_down, out_grad = together(own_two, w_out, w_down, out_grad, first_low)[:4]
    middle_out = permute(after(w_out, one[:4]), MIDDLE_OUT)
    hidden_one, middle_out, own_two, w_down, out_grad, *one = together(
        hidden_one, middle_out, own_two, w_down, out_grad, *one
    )
    home_out = jnp.where(at_home, w_out, middle_out)

    two = around(own_two)
    middle_two = permute(own_two, MIDDLE)
    outs = jnp.stack([home_out, permute(home_out, CHIP[2])])
    kv, rawk, w_kv, prompt_kv = project(
        key_value_kernel, "key_value", info, hidden_one, one, 4, kg, cos, sin, HEAD_SIZE, 1
    )
    prompt_kv, outs, out_grad, hidden_q, middle_two, *two = together(
        prompt_kv, outs, out_grad, hidden_one, middle_two, *two
    )

    prompt = around(prompt_kv)
    outs = [outs, permute(outs, CHIP[1])]
    grad_here = regrouped(out_grad)
    q, rawq, w_q = project(query_kernel, "query", info, hidden_q, one, 0, qg, cos, sin, 256, 0)
    q, grad_here, middle_two, w_down, *rest = together(
        q, grad_here, middle_two, w_down, *outs, *prompt
    )
    outs, prompt = rest[:2], rest[2:]

    two += around(middle_two)
    other_two = [permute(jnp.stack(two[:4]), OVER_Y)]
    middle_down = permute(w_down, MIDDLE_OUT)
    mixed, lse = attn_fwd(info, q, kv, prompt)
    home_down = jnp.where(at_home, w_down, middle_down)
    mixed, home_down, grad_here, *rest = together(mixed, home_down, grad_here, *two, *other_two)
    two, other_two = rest[:8], rest[8:]

    other_two.append(permute(jnp.stack(two[4:]), OVER_Y))
    downs = around(home_down)
    chunk_starts = [8 + 7 * (m // 2) + 3 * (m % 2) for m in range(8)]
    grad_here = jnp.concatenate(
        [
            grad_here[: 8 * BLK].reshape(8, BLK, width),
            jnp.stack([grad_here[start * BLK : (start + 4) * BLK] for start in chunk_starts]),
        ],
        axis=1,
    )

    def swap_cube(a):
        return lax.all_to_all(a, AXES, 0, 0, tiled=True, axis_index_groups=CUBES)

    grad_here = swap_cube(grad_here)
    in_turn = jnp.concatenate(
        [lax.dynamic_slice_in_dim(arrive, member ^ e, 1, 0) for e in range(8)], axis=0
    )
    leave_in_turn = jnp.minimum(in_turn, n_slots - 1)
    home_in_turn = jnp.concatenate(
        [lax.dynamic_slice_in_dim(home_slots, position ^ e, 1, 0) for e in range(8)], axis=0
    )

    rows_kind = ((row_total, width), f32), ((row_total, width), bf16)
    out_own, out_sib, w_o = whole_call(
        out_kernel,
        "out_projection",
        (info, mixed, *outs),
        [*rows_kind, ((1024, width), bf16)],
    )
    inputs = inputs_low.astype(f32)
    resid_one = inputs + out_own + permute(out_sib, SIBLING).astype(f32)
    normed_two, inverse_two = normed_parts(resid_one)
    hidden_two = (normed_two * norm2_gain).astype(bf16)
    hidden_two, other_far, *downs = together(hidden_two, other_two[1], *downs)
    other_two = [other_two[0], other_far]
    hidden_two = [hidden_two, permute(hidden_two, SIBLING)]
    grad_low = place_all(in_turn, grad_here, row_total, bf16)
    grad_both = [grad_low, permute(grad_low, SIBLING)]
    hid, grad_gu, ff_own, ff_sib, back_own, back_sib = mlp(
        info, hidden_two, grad_both, two + other_two, downs, ff
    )
    hidden_two = jnp.concatenate(hidden_two, axis=0)
    grad_both = jnp.concatenate(grad_both, axis=0)
    grad_two = back_own + permute(back_sib, SIBLING).astype(f32)
    gain_two_part = jnp.sum(grad_two * normed_two, axis=0)
    grad_resid = grad_low.astype(f32) + norm_back(grad_two * norm2_gain, normed_two, inverse_two)
    grad_attn = both(grad_resid.astype(bf16))

    def chip_parts(grad):
        grad = grad.reshape(8, -1, grad.shape[-1])
        return [
            jnp.stack([pick(grad, position ^ t), pick(grad, position ^ (4 + t))]) for t in range(4)
        ]

    def sent_to_chips(parts):
        return [permute(parts[t], CHIP[t]) for t in range(1, 4)]

    def from_middle(part):
        return added(pick(part, z_hi), permute(pick(part, 1 - z_hi), MIDDLE))

    def halved(grad, axis, bit, pairs):
        return added(pick(grad, bit, axis), permute(pick(grad, 1 - bit, axis), pairs))

    grad_two_w = tn(hidden_two, grad_gu).astype(bf16).reshape(2, 2, 2, 2, 64, -1)
    keep_two, send_two = pick(grad_two_w, y, 3), pick(grad_two_w, 1 - y, 3)
    send_two = permute(send_two, OVER_Y)
    grad_down = tn(hid, grad_both).astype(bf16).reshape(2, 2, -1, width)
    grad_out = tn(mixed, grad_attn).astype(bf16).reshape(2, 2, -1, width)
    outcome = resid_one + ff_own + permute(ff_sib, SIBLING).astype(f32)
    leaving = deal_all(leave_in_turn, outcome.astype(bf16))
    grad_attn, grad_down, grad_out, leaving, _ = together(
        grad_attn, grad_down, grad_out, leaving, keep_two
    )
    keep_down, send_down = pick(grad_down, x, 1), permute(pick(grad_down, 1 - x, 1), CHIP[1])
    keep_out, send_out = pick(grad_out, z_lo), permute(pick(grad_out, 1 - z_lo), CHIP[2])
    leaving = swap_cube(leaving)
    grad_mixed = nt(grad_attn, w_o).astype(bf16)
    grad_q, grad_kv, *prompt_parts, gains = attn_bwd(
        info, q, kv, prompt, grad_mixed, mixed, lse, rawq, rawk, qg, kg, cos, sin
    )
    grad_q, grad_kv, send_down, send_out, leaving, *prompt_parts = together(
        grad_q, grad_kv, send_down, send_out, leaving, *prompt_parts
    )

    prompt_parts = [prompt_parts[0]] + [permute(prompt_parts[t], CHIP[t]) for t in range(1, 4)]
    grad_wq = tn(hidden_one, after(grad_q, prompt_parts[1])).astype(bf16).reshape(8, 2, 64, -1)
    keep_q, send_q = pick(grad_wq, y, 1), permute(pick(grad_wq, 1 - y, 1), OVER_Y)
    grad_q, send_down, send_out, send_two, leaving, *prompt_parts = together(
        grad_q, send_down, send_out, send_two, leaving, *prompt_parts
    )
    left = regrouped(leaving.reshape(-1, width))
    sum_two = added(keep_two, send_two)
    down, out = added(keep_down, send_down), added(keep_out, send_out)
    down = halved(down, 0, z_lo, CHIP[2])
    out = halved(out, 0, x, CHIP[1])
    sum_two = halved(sum_two, 2, x, CHIP[1])
    grad_kv, key_gains = whole_call(
        prompt_back_kernel,
        "prompt_back",
        (*prompt_parts, grad_kv, rawk, kg, cos, sin),
        [(grad_kv.shape, bf16), ((8, HEAD_SIZE), f32)],
    )
    grad_wkv = tn(hidden_one, grad_kv).astype(bf16).reshape(8, 2, 64, -1)
    grad_one = nt(grad_q, w_q) + nt(after(grad_kv, grad_wkv), w_kv)
    grad_one, sum_two = together(grad_one, sum_two)
    grad_one = grad_one[:row_total] + permute(
        grad_one[row_total:].astype(bf16), SIBLING
    ).astype(f32)
    normed_one, inverse_one = normed_parts(inputs)
    gain_one_part = jnp.sum(grad_one * normed_one, axis=0)
    grad_tokens = grad_resid + norm_back(grad_one * norm1_gain, normed_one, inverse_one)
    going = deal_all(leave_in_turn, grad_tokens.astype(bf16))
    gain_grads = jnp.concatenate(
        [gain_one_part, gain_two_part, gains[0], gains[1] + key_gains[0]]
    ).reshape(-1, HEAD_SIZE)
    going, gain_grads, down, out, keep_q, send_q, grad_wkv, left, sum_two = together(
        going, gain_grads, down, out, keep_q, send_q, grad_wkv, left, sum_two
    )
    going = swap_cube(going)
    q_parts = chip_parts(added(keep_q, send_q))
    q_sent = sent_to_chips(q_parts)
    keep_kv, send_kv = pick(grad_wkv, y, 1), permute(pick(grad_wkv, 1 - y, 1), OVER_Y)
    three = jnp.concatenate([down, out], axis=0)
    three = added(three, permute(three, MIDDLE_IN))
    gain_grads = gain_grads + permute(gain_grads, SIBLING)
    outcome = place_all(home_in_turn, left.reshape(8, -1, width), row_total, bf16)
    going, gain_grads, outcome, keep_kv, send_kv, sum_two, *q_sent = together(
        going, gain_grads, outcome, keep_kv, send_kv, sum_two, *q_sent
    )
    going = regrouped(going.reshape(-1, width))
    sum_two = halved(sum_two, 1, z_lo, CHIP[2])
    gain_grads = gain_grads + permute(gain_grads, CHIP[1])
    kv_parts = chip_parts(added(keep_kv, send_kv))
    kv_sent = sent_to_chips(kv_parts)
    part_q = added(q_parts[0], *q_sent)
    going, gain_grads, sum_two, three, *kv_sent = together(
        going, gain_grads, sum_two, three, *kv_sent
    )
    gain_grads = gain_grads + permute(gain_grads, CHIP[2])
    grad_tokens = place_all(home_in_turn, going.reshape(8, -1, width), row_total, f32)
    part_kv = added(kv_parts[0], *kv_sent)
    sum_one = jnp.concatenate([part_q, part_kv], axis=2)
    sum_one = added(sum_one[0], permute(sum_one[1], MIDDLE))
    three = added(three, permute(three, OVER_Y_HOME))
    sum_two = from_middle(sum_two)
    sum_one, sum_two, three, gain_grads = together(sum_one, sum_two, three, gain_grads)
    sum_two = jnp.concatenate(in_order(y == 0, sum_two, permute(sum_two, OVER_Y)), axis=0)
    gain_grads = gain_grads + permute(gain_grads, OVER_Y)
    sum_one = jnp.concatenate(in_order(y == 0, sum_one, permute(sum_one, OVER_Y)), axis=0)
    total = jnp.where(at_home, three, permute(three, SIBLING)).astype(f32)
    sum_one, sum_two, gain_grads = together(sum_one, sum_two, gain_grads)
    gain_grads = gain_grads + permute(gain_grads, MIDDLE)
    shard = sum_two.shape[0]
    gate_grad, up_grad = whole_call(
        gate_up_kernel,
        "gate_up_gradients",
        (info, sum_two, permute(sum_two, SIBLING)),
        [((shard, 8 * ff), f32)] * 2,
    )
    query_grad, key_grad, value_grad = whole_call(
        attn_weights_kernel,
        "attn_weight_gradients",
        (info, sum_one, permute(sum_one, SIBLING)),
        [((shard, 2048), f32), ((shard, 1024), f32), ((shard, 1024), f32)],
    )
    gain_grads = gain_grads.reshape(-1)
    return (
        outcome,
        grad_tokens,
        gain_grads[:width],
        query_grad,
        key_grad,
        value_grad,
        gain_grads[2 * width : 2 * width + HEAD_SIZE],
        gain_grads[2 * width + HEAD_SIZE :],
        total[3 * RUN :],
        gain_grads[width : 2 * width],
        gate_grad,
        up_grad,
        total[: 3 * RUN],
    )


def solution(mesh):
    split = mesh.shape["grp"] == N_GRP and mesh.shape["ctx"] == N_CTX
    return jax.shard_map(
        shards_split if split else shards,
        mesh=mesh,
        in_specs=(
            P(("grp", "ctx"), None),
            P(),
            P(),
            P("ctx", None),
            P("ctx", None),
            P("ctx", None),
            P(),
            P(),
            P("ctx", None),
            P(),
            P("ctx", None),
            P("ctx", None),
            P("ctx", None),
            P(("grp", "ctx"), None),
        ),
        out_specs=(
            P(("grp", "ctx"), None),
            P(("grp", "ctx"), None),
            P(),
            P("ctx", None),
            P("ctx", None),
            P("ctx", None),
            P(),
            P(),
            P("ctx", None),
            P(),
            P("ctx", None),
            P("ctx", None),
            P("ctx", None),
        ),
        check_vma=False,
    )
```
